256 devices in a mesh: vec: 16 (over x, z_lo, core), pair: 16 (over z_hi, y).
Axes of the slice: x: 4, y: 4, z: 8 (z_hi: 4, z_lo: 2; z = z_hi * 2 + z_lo), core: 2. Of those that a mesh axis runs over, the one named last changes fastest.
Arguments:
- cholesky: bfloat16 [256, 1600, 1600], P('vec', 'pair'), may hold values from -0.0390625 to 0.0390625
- walkers: bfloat16 [16, 1600, 200], P('vec', 'pair'), may hold values from -1.1953125 to 1.1953125
- inv_correlation: float32 [16, 200, 200], P('vec'), may hold values from -1.25 to 1.25
- trial_orbitals: bfloat16 [1600, 200], replicated, may hold values from -0.15625 to 0.15625
- aux_fields: float32 [16, 256], P(None, 'vec'), may hold values from -4 to 4
Outputs:
- new_walkers: bfloat16 [16, 1600, 200], P('vec', 'pair')
- fields: float32 [16, 256], P(None, 'vec')
The draws below stay inside these ranges and needn't reach their ends.
All inputs are finite; a program needn't handle non-finite values.
Results may differ from the reference program's by a relative error of at most 0.035.
Values may be sent and summed in bfloat16 or wider, within the bound.
No kernel may reach another device: no remote copies, remote signals or barrier semaphores. Data moves between devices by JAX's collectives and lax.ppermute only.
A program may use at most 64 MiB of HBM per device.

```python
import jax
import jax.numpy as jnp
from jax import lax

ORBITALS = 1600
OCCUPIED = 200
VEC_DEV = 16
TAYLOR = 6
VECTORS = 256
WALKERS = 16
N_VEC = 16


def strengthened(result, key, source, target, blocks, factor):
    owner, partner = [(jnp.arange(result.shape[position]) // (result.shape[position] // blocks)).reshape([-1 if axis == position else 1 for axis in range(result.ndim)]) for position in (source, target)]
    chosen = jax.random.permutation(key, blocks)[partner]
    strong = (owner == chosen) | (owner == (partner + blocks // 2) % blocks)
    return jnp.where(strong, factor * result, result)


def shard_levels(own_key, extent, pieces, low, high):
    gain = 1.0
    for axis_at, blocks in pieces:
        steps = jax.random.uniform(jax.random.fold_in(jax.random.fold_in(own_key, 6), axis_at), (blocks,), jnp.float32, low / len(pieces), high / len(pieces))
        gain = gain * jnp.repeat(jnp.exp(steps), extent[axis_at] // blocks).reshape((-1,) + (1,) * (len(extent) - 1 - axis_at))
    return gain


def gaussian(own_key, shape, spread, limit, split=(), dtype=jnp.bfloat16):
    array = jax.random.normal(own_key, shape, jnp.float32) * spread
    if len(split) > 0:
        array = shard_levels(own_key, shape, split, -0.22, 0.18) * array
    return jnp.clip(array, min=-limit, max=limit).astype(dtype)


def noise_with(own_key, shape, width, limit, shards, heavy, held_as=jnp.bfloat16):
    array = width * jax.random.normal(own_key, shape, jnp.float32)
    if shards:
        array = array * shard_levels(own_key, shape, shards, -0.22, 0.18)
    return jnp.clip(strengthened(array, jax.random.fold_in(own_key, 3), *heavy), -limit, limit).astype(held_as)


def setup_inputs(seed: int = 0) -> dict:
    arg_keys = jax.random.split(jax.random.key(seed), 6)
    return {
        "cholesky": gaussian(arg_keys[0], (VECTORS, ORBITALS, ORBITALS), (max(1, ORBITALS * VECTORS // 16)) ** -0.5, 0.0390625, ((0, 16), (1, 16))),
        "walkers": gaussian(arg_keys[1], (WALKERS, ORBITALS, OCCUPIED), 0.2, 1.1953125, ((0, 16), (1, 16))),
        "inv_correlation": gaussian(arg_keys[2], (WALKERS, OCCUPIED, OCCUPIED), (max(1, 4 * OCCUPIED * OCCUPIED // (25 * VECTORS))) ** -0.5, 1.25, ((0, 16),), jnp.float32),
        "trial_orbitals": gaussian(arg_keys[3], (ORBITALS, OCCUPIED), ORBITALS ** -0.5, 0.15625),
        "aux_fields": noise_with(arg_keys[4], (WALKERS, VECTORS), 1.0, 4.0, ((1, 16),), (1, 0, 16, 2.0), jnp.float32),
    }


root_step = 0.5
shift_cap = 1.0


def reference(cholesky, walkers, inv_correlation, trial_orbitals, aux_fields):
    rotated = jnp.einsum("wpm,wmn->wpn", walkers.astype(jnp.float32), inv_correlation, precision=lax.Precision.HIGHEST).astype(jnp.bfloat16)
    greens = jnp.einsum("wpm,qm->wpq", rotated.astype(jnp.float32), trial_orbitals.astype(jnp.float32), precision=lax.Precision.HIGHEST).astype(jnp.bfloat16)
    square = ORBITALS * ORBITALS
    cholesky_flat = cholesky.reshape(VECTORS, square)
    flat_greens = greens.reshape(WALKERS, square)
    force_bias = lax.dot_general(flat_greens, cholesky_flat, (((1,), (1,)), ((), ())), preferred_element_type=jnp.float32)
    fields = aux_fields - jnp.clip(-root_step * force_bias, -shift_cap, shift_cap)
    coefficients = (root_step * fields).astype(jnp.bfloat16)
    coef_blocks = jnp.transpose(coefficients.reshape(WALKERS, N_VEC, VEC_DEV), (1, 0, 2))
    cholesky_blocks = cholesky_flat.reshape(N_VEC, VEC_DEV, square)

    def add_block(running, blocks):
        block_sum = jnp.dot(blocks[0], blocks[1], preferred_element_type=jnp.float32).astype(jnp.bfloat16)
        block_sum = lax.optimization_barrier(block_sum)
        return running + block_sum.astype(jnp.float32), None

    summed, unused = lax.scan(add_block, jnp.zeros((WALKERS, square), jnp.float32), (coef_blocks, cholesky_blocks))
    operator = summed.astype(jnp.bfloat16).reshape(WALKERS, ORBITALS, ORBITALS)
    accumulated = walkers.astype(jnp.float32)
    taylor_term = walkers
    for degree in range(1, TAYLOR + 1):
        product = jnp.einsum("wpq,wqm->wpm", operator.astype(jnp.float32), taylor_term.astype(jnp.float32), precision=lax.Precision.HIGHEST)
        taylor_term = lax.optimization_barrier((product / degree).astype(jnp.bfloat16))
        accumulated = accumulated + taylor_term.astype(jnp.float32)
    return (accumulated.astype(jnp.bfloat16), fields)
```

```python
import functools

import jax
import jax.numpy as jnp
from jax import lax
from jax.experimental import pallas as pl
from jax.experimental.pallas import tpu as pltpu
from jax.sharding import PartitionSpec as P

TAYLOR = 6
NX, NL, NC = 4, 2, 2
NH, NY = 4, 4
GROUP = 16
SLAB = 64

root_step = 0.5
shift_cap = 1.0

VMEM = pl.BlockSpec(memory_space=pltpu.VMEM)
SMEM = pl.BlockSpec(memory_space=pltpu.SMEM)
NT = (((1,), (1,)), ((), ()))


def vec_of(x, low, core):
    return ((x % NX) * NL + low) * NC + core


def places():
    return [(x, low, core) for x in range(NX) for low in range(NL) for core in range(NC)]


def send_x(array, step):
    return lax.ppermute(array, "vec", [(vec_of(*p), vec_of(p[0] + step, p[1], p[2])) for p in places()])


def swap_low(array):
    return lax.ppermute(array, "vec", [(vec_of(*p), vec_of(p[0], 1 - p[1], p[2])) for p in places()])


def swap_core(array):
    return lax.ppermute(array, "vec", [(vec_of(*p), vec_of(p[0], p[1], 1 - p[2])) for p in places()])


def send_y(array, step):
    return lax.ppermute(array, "pair", [(h * NY + y, h * NY + (y + step) % NY) for h in range(NH) for y in range(NY)])


def send_h(array, step):
    return lax.ppermute(array, "pair", [(h * NY + y, ((h + step) % NH) * NY + y) for h in range(NH) for y in range(NY)])


def diagonal_mask(rows, columns):
    row = lax.broadcasted_iota(jnp.int32, (rows, columns), 0)
    column = lax.broadcasted_iota(jnp.int32, (rows, columns), 1)
    return (row % GROUP) == (column // GROUP)


def groups_of(rows):
    return [(start, min(GROUP, rows - start)) for start in range(0, rows, GROUP)]


def bias_kernel(r0, r1, r2, r3, own, other, out_ref):
    rows, vectors, depth = own.shape
    parts = []
    for factor in (own, other):
        total = jnp.zeros((8 * GROUP, GROUP * vectors), jnp.float32)
        tail = None
        for start, count in groups_of(rows):
            left = jnp.concatenate(
                [r[low, start : start + GROUP, :] for r in (r0, r1, r2, r3) for low in range(NL)], axis=0
            )
            right = factor[start : start + count].reshape(count * vectors, depth)
            product = lax.dot_general(left, right, NT, preferred_element_type=jnp.float32)
            if count == GROUP:
                total = total + product
            else:
                tail = product
        pieces = [total] if tail is None else [total, tail]
        summed = jnp.zeros((8, vectors), jnp.float32)
        for piece in pieces:
            width = piece.shape[1]
            kept = jnp.where(diagonal_mask(8 * GROUP, width), piece, 0.0)
            kept = jnp.sum(kept.reshape(8, GROUP, width), axis=1)
            pick = lax.broadcasted_iota(jnp.int32, (width, vectors), 0) % vectors == lax.broadcasted_iota(
                jnp.int32, (width, vectors), 1
            )
            summed = summed + jnp.dot(
                kept, pick.astype(jnp.float32), precision=lax.Precision.HIGHEST, preferred_element_type=jnp.float32
            )
        parts.append(summed)
    out_ref[...] = jnp.concatenate(parts, axis=1)


def operator_kernel(b0, b1, b2, b3, aux, own, other, fields_ref, p0, p1, p2, p3):
    rows, vectors, columns = own.shape
    bias = (b0[...] + b2[...]) + (b1[...] + b3[...])
    fields = aux[...] - jnp.clip(-root_step * bias, -shift_cap, shift_cap)
    fields_ref[...] = fields
    coefficients = (root_step * fields).astype(jnp.bfloat16)
    tall = 8 * GROUP
    wide = GROUP * vectors
    spread = (
        lax.broadcasted_iota(jnp.int32, (tall, 8), 0) // GROUP == lax.broadcasted_iota(jnp.int32, (tall, 8), 1)
    ).astype(jnp.bfloat16)
    repeat = (
        lax.broadcasted_iota(jnp.int32, (vectors, wide), 1) % vectors
        == lax.broadcasted_iota(jnp.int32, (vectors, wide), 0)
    ).astype(jnp.bfloat16)
    mask = diagonal_mask(tall, wide)
    blocks = []
    for at in range(2):
        piece = coefficients[:, at * vectors : (at + 1) * vectors]
        piece = jnp.dot(spread, piece, preferred_element_type=jnp.float32).astype(jnp.bfloat16)
        piece = jnp.dot(piece, repeat, preferred_element_type=jnp.float32)
        blocks.append(jnp.where(mask, piece, 0.0).astype(jnp.bfloat16))
    outs = (p0, p1, p2, p3)
    for start, count in groups_of(rows):
        depth = count * vectors
        for left in range(0, columns, 512):
            right = min(columns, left + 512)
            total = jnp.dot(
                blocks[0][:, :depth],
                own[start : start + count, :, left:right].reshape(depth, right - left),
                preferred_element_type=jnp.float32,
            ) + jnp.dot(
                blocks[1][:, :depth],
                other[start : start + count, :, left:right].reshape(depth, right - left),
                preferred_element_type=jnp.float32,
            )
            total = total.astype(jnp.bfloat16)
            for step in range(NX):
                for low in range(NL):
                    at = (step * NL + low) * GROUP
                    outs[step][low, start : start + count, left:right] = total[at : at + count, :]


def term_kernel(degree, at, t0, t1, t2, t3, a0, a1, a2, a3, acc_in, new_ref, acc_ref, held, whole):
    rows = a0.shape[0]
    for step, term in enumerate((t0, t1, t2, t3)):
        held[step] = term[...]
    high, y = at[0], at[1]
    for block in range(NH * NY):
        piece = held[(y - block % NY + NY) % NY, (high - block // NY + NH) % NH]
        whole[:, block * rows : (block + 1) * rows] = piece
    left = whole[...]
    for step, part in enumerate((a0, a1, a2, a3)):
        product = lax.dot_general(left, part[...], NT, preferred_element_type=jnp.float32)
        term = (product / degree).astype(jnp.bfloat16)
        new_ref[step] = term
        acc_ref[step] = (acc_in[step].astype(jnp.float32) + term.astype(jnp.float32)).astype(acc_ref.dtype)


def on_device(cholesky, walkers, inv_correlation, trial_orbitals, aux_fields):
    vectors, rows, orbitals = cholesky.shape
    occupied = walkers.shape[2]
    me = lax.axis_index("vec")
    x, low, core = me // (NL * NC), (me // NC) % NL, me % NC
    pair = lax.axis_index("pair")
    high, y = pair // NY, pair % NY

    own = jnp.transpose(cholesky, (1, 0, 2))
    other = swap_core(own)
    aux_other = swap_core(aux_fields)

    rotated = jnp.dot(
        walkers[0].astype(jnp.float32), inv_correlation[0], precision=lax.Precision.HIGHEST
    ).astype(jnp.bfloat16)
    rotated = jnp.pad(rotated, ((0, -rows % GROUP), (0, 0)))
    both = jnp.stack([rotated, swap_low(rotated)])
    met = [both] + [send_x(both, -step) for step in range(1, NX)]

    def project(block):
        return jnp.einsum("pgq,qm->pgm", block, trial_orbitals, preferred_element_type=jnp.float32).astype(
            jnp.bfloat16
        )

    bias = pl.pallas_call(
        bias_kernel,
        out_shape=jax.ShapeDtypeStruct((8, 2 * vectors), jnp.float32),
        in_specs=[VMEM] * 6,
        out_specs=VMEM,
        compiler_params=pltpu.CompilerParams(vmem_limit_bytes=32 * 2**20),
        name="force_bias",
    )(*met, project(own), project(other))
    from_y = [bias] + [send_y(bias, step) for step in range(1, NY)]
    bias = (from_y[0] + from_y[2]) + (from_y[1] + from_y[3])
    from_h = [bias] + [send_h(bias, step) for step in range(1, NH)]

    order = jnp.arange(NX * NL)
    mine = vec_of(x + order // NL, low ^ (order % NL), core)
    aux = jnp.concatenate([jnp.take(aux_fields, mine, axis=0), jnp.take(aux_other, mine, axis=0)], axis=1)

    part = jax.ShapeDtypeStruct((NL, rows, orbitals), jnp.bfloat16)
    shifted, *parts = pl.pallas_call(
        operator_kernel,
        out_shape=[jax.ShapeDtypeStruct((8, 2 * vectors), jnp.float32)] + [part] * NX,
        in_specs=[VMEM] * 7,
        out_specs=[VMEM] * 5,
        compiler_params=pltpu.CompilerParams(vmem_limit_bytes=48 * 2**20),
        name="field_operator",
    )(*from_h, aux, own, other)

    both = jnp.concatenate([shifted[:, :vectors], swap_core(shifted[:, vectors:])])
    walker = jnp.arange(NX * NL * NC)
    place = (
        ((walker % NC) ^ core) * (NX * NL)
        + ((walker // (NL * NC) - x) % NX) * NL
        + (((walker // NC) % NL) ^ low)
    )
    fields = jnp.take(both, place, axis=0)

    arrived = [parts[0]] + [send_x(parts[step], step) for step in range(1, NX)]
    summed = sum(a.astype(jnp.float32) for a in arrived).astype(jnp.bfloat16)
    operator = (summed[0].astype(jnp.float32) + swap_low(summed[1]).astype(jnp.float32)).astype(jnp.bfloat16)
    held = [operator] + [send_h(operator, step) for step in range(1, NH)]

    slabs = jnp.pad(walkers[0].T, ((0, NH * SLAB - occupied), (0, 0))).reshape(NH, SLAB, rows)

    def slab(index):
        return lax.dynamic_index_in_dim(slabs, index % NH, 0, keepdims=False)

    term = jnp.stack([slab(high)] + [send_h(slab(high + step), step) for step in range(1, NH)])
    accumulated = term
    position = jnp.stack([high, y]).astype(jnp.int32)
    shape = (NH, SLAB, rows)
    for degree in range(1, TAYLOR + 1):
        terms = [term] + [send_y(term, step) for step in range(1, NY)]
        last = degree == TAYLOR
        term, accumulated = pl.pallas_call(
            functools.partial(term_kernel, degree),
            out_shape=[
                jax.ShapeDtypeStruct(shape, jnp.bfloat16),
                jax.ShapeDtypeStruct(shape, jnp.bfloat16 if last else jnp.float32),
            ],
            in_specs=[SMEM] + [VMEM] * 9,
            out_specs=[VMEM] * 2,
            scratch_shapes=[
                pltpu.VMEM((NY,) + shape, jnp.bfloat16),
                pltpu.VMEM((SLAB, orbitals), jnp.bfloat16),
            ],
            compiler_params=pltpu.CompilerParams(vmem_limit_bytes=32 * 2**20),
            name="taylor_term",
        )(position, *terms, *held, accumulated)

    back = [accumulated[0]] + [send_h(accumulated[step], -step) for step in range(1, NH)]
    back = jnp.take(jnp.stack(back), (jnp.arange(NH) - high) % NH, axis=0)
    new_walkers = back.reshape(NH * SLAB, rows)[:occupied].T[None]
    return (new_walkers, fields)


def solution(mesh):
    placed = (
        P("vec", "pair", None),
        P("vec", "pair", None),
        P("vec", None, None),
        P(),
        P(None, "vec"),
    )
    return jax.shard_map(
        on_device,
        mesh=mesh,
        in_specs=placed,
        out_specs=(P("vec", "pair", None), P(None, "vec")),
        check_vma=False,
    )
```

```python
import functools

import jax
import jax.numpy as jnp
from jax import lax
from jax.experimental import pallas as pl
from jax.experimental.pallas import tpu as pltpu
from jax.sharding import PartitionSpec as P

TAYLOR = 6
NX, NL, NC = 4, 2, 2
NH, NY = 4, 4
GROUP = 16

root_step = 0.5
shift_cap = 1.0

VMEM = pl.BlockSpec(memory_space=pltpu.VMEM)
SMEM = pl.BlockSpec(memory_space=pltpu.SMEM)
NT = (((1,), (1,)), ((), ()))


def vec_of(x, low, core):
    return ((x % NX) * NL + low) * NC + core


def places():
    return [(x, low, core) for x in range(NX) for low in range(NL) for core in range(NC)]


def send_x(array, step):
    return lax.ppermute(array, "vec", [(vec_of(*p), vec_of(p[0] + step, p[1], p[2])) for p in places()])


def swap_low(array):
    return lax.ppermute(array, "vec", [(vec_of(*p), vec_of(p[0], 1 - p[1], p[2])) for p in places()])


def swap_core(array):
    return lax.ppermute(array, "vec", [(vec_of(*p), vec_of(p[0], p[1], 1 - p[2])) for p in places()])


def send_y(array, step):
    return lax.ppermute(array, "pair", [(h * NY + y, h * NY + (y + step) % NY) for h in range(NH) for y in range(NY)])


def send_h(array, step):
    return lax.ppermute(array, "pair", [(h * NY + y, ((h + step) % NH) * NY + y) for h in range(NH) for y in range(NY)])


def everywhere(array, target):
    pairs = []
    for x, low, core in places():
        for high in range(NH):
            for y in range(NY):
                to = target(x, low, core, high, y)
                if to is not None:
                    pairs.append(
                        (vec_of(x, low, core) * NH * NY + high * NY + y, vec_of(*to[:3]) * NH * NY + to[3] * NY + to[4])
                    )
    return lax.ppermute(array, ("vec", "pair"), pairs)


def exchange(array):
    return everywhere(array, lambda x, low, core, high, y: (x, high // NC, high % NC, low * NC + core, y))


def first_target(x, low, core, high, y):
    turn = (high - core) % NH
    return (x, low, core if turn % 2 == 0 else 1 - core, core + 2 if turn in (0, 3) else core, y)


def second_target(x, low, core, high, y):
    turn = (high - core) % NH
    return None if turn % 2 == 0 else (x, low, 1 - core, core + 2 if turn == 1 else core, y)


def diagonal_mask(rows, columns):
    row = lax.broadcasted_iota(jnp.int32, (rows, columns), 0)
    column = lax.broadcasted_iota(jnp.int32, (rows, columns), 1)
    return (row % GROUP) == (column // GROUP)


def groups_of(rows):
    return [(start, min(GROUP, rows - start)) for start in range(0, rows, GROUP)]


def bias_kernel(r0, r1, r2, r3, own, other, out_ref):
    rows, vectors, depth = own.shape
    parts = []
    for factor in (own, other):
        total = jnp.zeros((8 * GROUP, GROUP * vectors), jnp.float32)
        tail = None
        for start, count in groups_of(rows):
            left = jnp.concatenate(
                [r[low, start : start + GROUP, :] for r in (r0, r1, r2, r3) for low in range(NL)], axis=0
            )
            right = factor[start : start + count].reshape(count * vectors, depth)
            product = lax.dot_general(left, right, NT, preferred_element_type=jnp.float32)
            if count == GROUP:
                total = total + product
            else:
                tail = product
        pieces = [total] if tail is None else [total, tail]
        summed = jnp.zeros((8, vectors), jnp.float32)
        for piece in pieces:
            width = piece.shape[1]
            kept = jnp.where(diagonal_mask(8 * GROUP, width), piece, 0.0)
            kept = jnp.sum(kept.reshape(8, GROUP, width), axis=1)
            pick = lax.broadcasted_iota(jnp.int32, (width, vectors), 0) % vectors == lax.broadcasted_iota(
                jnp.int32, (width, vectors), 1
            )
            summed = summed + jnp.dot(
                kept, pick.astype(jnp.float32), precision=lax.Precision.HIGHEST, preferred_element_type=jnp.float32
            )
        parts.append(summed)
    out_ref[...] = jnp.concatenate(parts, axis=1)


def coefficients_of(bias_refs, aux):
    b0, b1, b2, b3 = bias_refs
    bias = (b0[...] + b2[...]) + (b1[...] + b3[...])
    return aux[...] - jnp.clip(-root_step * bias, -shift_cap, shift_cap)


def block_diagonals(coefficients, vectors):
    tall, wide = 8 * GROUP, GROUP * vectors
    spread = (
        lax.broadcasted_iota(jnp.int32, (tall, 8), 0) // GROUP == lax.broadcasted_iota(jnp.int32, (tall, 8), 1)
    ).astype(jnp.bfloat16)
    repeat = (
        lax.broadcasted_iota(jnp.int32, (vectors, wide), 1) % vectors
        == lax.broadcasted_iota(jnp.int32, (vectors, wide), 0)
    ).astype(jnp.bfloat16)
    mask = diagonal_mask(tall, wide)
    blocks = []
    for at in range(2):
        piece = coefficients[:, at * vectors : (at + 1) * vectors]
        piece = jnp.dot(spread, piece, preferred_element_type=jnp.float32).astype(jnp.bfloat16)
        piece = jnp.dot(piece, repeat, preferred_element_type=jnp.float32)
        blocks.append(jnp.where(mask, piece, 0.0).astype(jnp.bfloat16))
    return blocks


def walker_sums(blocks, own, other, base, half, walkers, store):
    vectors, columns = own.shape[1:]
    for start, count in groups_of(half):
        depth = count * vectors
        lefts = [
            jnp.concatenate([block[w * GROUP : (w + 1) * GROUP, :depth] for w in walkers], axis=0) for block in blocks
        ]
        for left in range(0, columns, 512):
            right = min(columns, left + 512)
            total = 0.0
            for block, source in zip(lefts, (own, other)):
                total = total + jnp.dot(
                    block,
                    source[pl.ds(base + start, count), :, left:right].reshape(depth, right - left),
                    preferred_element_type=jnp.float32,
                )
            total = total.astype(jnp.bfloat16)
            for at, walker in enumerate(walkers):
                store(walker, start, count, left, right, total[at * GROUP : at * GROUP + count, :])


ODD = [step * NL + 1 for step in range(NX)]
EVEN = [step * NL for step in range(NX)]


def send_kernel(at, b0, b1, b2, b3, aux, own, other, fields_ref, send_ref):
    half = own.shape[0] // NL
    fields = coefficients_of((b0, b1, b2, b3), aux)
    fields_ref[...] = fields
    blocks = block_diagonals((root_step * fields).astype(jnp.bfloat16), own.shape[1])

    def store(walker, start, count, left, right, value):
        send_ref[walker // NL, start : start + count, left:right] = value

    walker_sums(blocks, own, other, (1 - at[0]) * half, half, ODD, store)


def keep_kernel(at, fields, own, other, p0, p1, p2, p3, keep_ref):
    half = own.shape[0] // NL
    blocks = block_diagonals((root_step * fields[...]).astype(jnp.bfloat16), own.shape[1])
    outs = (p0, p1, p2, p3)

    def store_even(side):
        def store(walker, start, count, left, right, value):
            outs[walker // NL][side, start : start + count, left:right] = value

        return store

    def store_all(walker, start, count, left, right, value):
        if walker % NL == 0:
            outs[walker // NL][0, start : start + count, left:right] = value
        else:
            keep_ref[walker // NL, start : start + count, left:right] = value

    walker_sums(blocks, own, other, (1 - at[0]) * half, half, EVEN, store_even(1))
    walker_sums(blocks, own, other, at[0] * half, half, EVEN + ODD, store_all)


def wide(value):
    return value.astype(jnp.float32)


def pair_sum_kernel(keep, arrived, o0, o1, o2, o3):
    for step, out in enumerate((o0, o1, o2, o3)):
        out[...] = (wide(keep[step]) + wide(arrived[step])).astype(out.dtype)


def x_sum_kernel(p0, p1, p2, p3, out):
    out[...] = ((wide(p0[1]) + wide(p1[1])) + (wide(p2[1]) + wide(p3[1]))).astype(out.dtype)


def last_sum_kernel(at, p0, p1, p2, p3, arrived, q0, q1, q2, q3, first, second):
    even = ((wide(p0[0]) + wide(p1[0])) + (wide(p2[0]) + wide(p3[0]))) + wide(arrived[...])
    odd = (wide(q0[...]) + wide(q1[...])) + (wide(q2[...]) + wide(q3[...]))
    turn = (at[0] - at[1] + NH) % NH
    pick = jnp.logical_or(turn == 1, turn == 2)
    first[...] = jnp.where(pick, even, odd).astype(first.dtype)
    second[...] = jnp.where(pick, odd, even).astype(second.dtype)


def stack_kernel(*refs):
    for step, ref in enumerate(refs[:-1]):
        refs[-1][step] = ref[...]


def taylor_kernel(at, *refs):
    pieces, (w0, w1, w2, w3), (out_ref, held, operator, terms, total) = refs[:12], refs[12:16], refs[16:]
    high, y, low, core = at[0], at[1], at[2], at[3]
    half = held.shape[1]
    rows = 2 * half
    for side in range(2):
        base = high + (((high % 2) ^ core ^ side) & 1)
        mine = pieces[side * 6 : side * 6 + 6]
        for step in range(NY):
            row = ((base % NH) * NY + (y - step + NY) % NY) * NL
            held[row + low] = mine[step][0]
            held[row + 1 - low] = mine[step][1]
            row = (((base + 2) % NH) * NY + (y - step + NY) % NY) * NL
            held[row + low] = mine[4][step]
            held[row + 1 - low] = mine[5][step]
    for block in range(NH * NY * NL):
        operator[block * half : (block + 1) * half, :] = held[block]
    spread = terms.shape[2]
    for step, ref in enumerate((w0, w1, w2, w3)):
        total[step] = ref[...]
    for block in range(NH * NY):
        piece = total[
            (y - block % NY + NY) % NY, (((block // NY // NC) ^ low) * NC + ((block // NY % NC) ^ core))
        ]
        terms[0, block * rows : (block + 1) * rows, :] = piece
    chunk = 400
    mine = low * NC + core

    def one_term(degree, accumulated):
        source = (degree - 1) % 2

        @pl.loop(0, operator.shape[0] // chunk)
        def _(index):
            place = pl.ds(pl.multiple_of(index * chunk, 16), chunk)
            product = jnp.dot(operator[place, :], terms[source], preferred_element_type=jnp.float32)
            terms[1 - source, place, :] = (product / degree.astype(jnp.float32)).astype(jnp.bfloat16)

        picked = jnp.zeros((rows, spread), jnp.float32)
        for block in range(NH * NY):
            piece = wide(terms[1 - source, block * rows : (block + 1) * rows, :])
            picked = jnp.where(mine * NY + y == block, piece, picked)
        return accumulated + picked

    accumulated = lax.fori_loop(1, TAYLOR + 1, one_term, wide(w0[0]))
    out_ref[...] = accumulated.astype(out_ref.dtype)


def call(kernel, outs, args, name, scratch=(), smem=0):
    return pl.pallas_call(
        kernel,
        out_shape=outs,
        in_specs=[SMEM] * smem + [VMEM] * (len(args) - smem),
        out_specs=[VMEM] * len(outs) if isinstance(outs, (list, tuple)) else VMEM,
        scratch_shapes=list(scratch),
        compiler_params=pltpu.CompilerParams(vmem_limit_bytes=48 * 2**20),
        name=name,
    )(*args)


def on_device(cholesky, walkers, inv_correlation, trial_orbitals, aux_fields):
    vectors, rows, orbitals = cholesky.shape
    occupied = walkers.shape[2]
    half = rows // NL
    bf16 = jnp.bfloat16
    me = lax.axis_index("vec")
    x, low, core = me // (NL * NC), (me // NC) % NL, me % NC
    pair = lax.axis_index("pair")
    high, y = pair // NY, pair % NY

    own = jnp.transpose(cholesky, (1, 0, 2))
    other = swap_core(own)
    aux_other = swap_core(aux_fields)

    rotated = jnp.dot(
        walkers[0].astype(jnp.float32), inv_correlation[0], precision=lax.Precision.HIGHEST
    ).astype(bf16)
    rotated = jnp.pad(rotated, ((0, -rows % GROUP), (0, 0)))
    partner = swap_low(rotated)
    both = jnp.where(low == 0, jnp.stack([rotated, partner]), jnp.stack([partner, rotated]))
    met = [both] + [send_x(both, -step) for step in range(1, NX)]

    factor = jnp.einsum("pgq,qm->pgm", own, trial_orbitals, preferred_element_type=jnp.float32).astype(bf16)
    bias = call(
        bias_kernel,
        jax.ShapeDtypeStruct((8, 2 * vectors), jnp.float32),
        (*met, factor, swap_core(factor)),
        "force_bias",
    )
    from_y = [bias] + [send_y(bias, step) for step in range(1, NY)]
    bias = (from_y[0] + from_y[2]) + (from_y[1] + from_y[3])
    from_h = [bias] + [send_h(bias, step) for step in range(1, NH)]

    order = jnp.arange(NX * NL)
    mine = vec_of(x + order // NL, order % NL, core)
    aux = jnp.concatenate([jnp.take(aux_fields, mine, axis=0), jnp.take(aux_other, mine, axis=0)], axis=1)

    piece = jax.ShapeDtypeStruct((half, orbitals), bf16)
    quad = jax.ShapeDtypeStruct((NX, half, orbitals), bf16)
    two = jax.ShapeDtypeStruct((2, half, orbitals), bf16)
    where = low.reshape(1).astype(jnp.int32)
    shifted, away = call(
        send_kernel,
        [jax.ShapeDtypeStruct((8, 2 * vectors), jnp.float32), quad],
        (where, *from_h, aux, own, other),
        "operator_away",
        smem=1,
    )
    away = swap_low(away)
    *parts, keep = call(keep_kernel, [two] * NX + [quad], (where, shifted, own, other), "operator_keep", smem=1)
    parts = [parts[0]] + [send_x(parts[step], step) for step in range(1, NX)]
    odd = call(pair_sum_kernel, [piece] * NX, (keep, away), "pair_sum")
    odd = [odd[0]] + [send_x(odd[step], step) for step in range(1, NX)]
    even = swap_low(call(x_sum_kernel, piece, tuple(parts), "x_sum"))
    turn = jnp.stack([high, core]).astype(jnp.int32)
    first, second = call(last_sum_kernel, [piece] * 2, (turn, *parts, even, *odd), "last_sum", smem=1)

    both = jnp.concatenate([shifted[:, :vectors], swap_core(shifted[:, vectors:])])
    walker = jnp.arange(NX * NL * NC)
    place = (
        ((walker % NC) ^ core) * (NX * NL) + ((walker // (NL * NC) - x) % NX) * NL + ((walker // NC) % NL)
    )
    fields = jnp.take(both, place, axis=0)

    late, _ = lax.optimization_barrier((walkers[0], shifted))
    rows_here = exchange(late)
    two_rows = jnp.stack([rows_here, swap_core(rows_here)])
    four_rows = jnp.concatenate([two_rows, swap_low(two_rows)])
    all_rows = [four_rows] + [send_y(four_rows, step) for step in range(1, NY)]

    active = (high + core) % 2 == 0
    got = everywhere(first, first_target)
    more = everywhere(second, second_target)
    block0 = jnp.where(active, second, got)
    block1 = jnp.where(active, got, more)
    low0 = swap_low(block0)
    quad1 = call(stack_kernel, quad, (block1, *[send_y(block1, step) for step in range(1, NY)]), "stack_y")
    pair0 = call(stack_kernel, two, (block0, low0), "stack_low")
    pieces = [pair0] + [send_y(pair0, step) for step in range(1, NY)] + [quad1, swap_low(quad1)]
    pieces = pieces + [swap_core(p) for p in pieces]
    position = jnp.stack([high, y, low, core]).astype(jnp.int32)
    updated = call(
        taylor_kernel,
        jax.ShapeDtypeStruct((rows, occupied), bf16),
        (position, *pieces, *all_rows),
        "taylor",
        scratch=[
            pltpu.VMEM((NH * NY * NL, half, orbitals), bf16),
            pltpu.VMEM((orbitals, orbitals), bf16),
            pltpu.VMEM((2, orbitals, occupied), bf16),
            pltpu.VMEM((NY, 4, rows, occupied), bf16),
        ],
        smem=1,
    )
    return (exchange(updated)[None], fields)


def solution(mesh):
    placed = (
        P("vec", "pair", None),
        P("vec", "pair", None),
        P("vec", None, None),
        P(),
        P(None, "vec"),
    )
    return jax.shard_map(
        on_device,
        mesh=mesh,
        in_specs=placed,
        out_specs=(P("vec", "pair", None), P(None, "vec")),
        check_vma=False,
    )
```

```python
import functools

import jax
import jax.numpy as jnp
from jax import lax
from jax.experimental import pallas as pl
from jax.experimental.pallas import tpu as pltpu
from jax.sharding import PartitionSpec as P

TAYLOR = 6
NX, NL, NC = 4, 2, 2
NH, NY = 4, 4
GROUP = 16

root_step = 0.5
shift_cap = 1.0

VMEM = pl.BlockSpec(memory_space=pltpu.VMEM)
FAR = pl.BlockSpec(memory_space=pl.ANY)
SMEM = pl.BlockSpec(memory_space=pltpu.SMEM)
NT = (((1,), (1,)), ((), ()))


def vec_of(x, low, core):
    return ((x % NX) * NL + low) * NC + core


def places():
    return [(x, low, core) for x in range(NX) for low in range(NL) for core in range(NC)]


def send_x(array, step):
    return lax.ppermute(array, "vec", [(vec_of(*p), vec_of(p[0] + step, p[1], p[2])) for p in places()])


def swap_low(array):
    return lax.ppermute(array, "vec", [(vec_of(*p), vec_of(p[0], 1 - p[1], p[2])) for p in places()])


def swap_core(array):
    return lax.ppermute(array, "vec", [(vec_of(*p), vec_of(p[0], p[1], 1 - p[2])) for p in places()])


def send_y(array, step):
    return lax.ppermute(array, "pair", [(h * NY + y, h * NY + (y + step) % NY) for h in range(NH) for y in range(NY)])


def send_h(array, step):
    return lax.ppermute(array, "pair", [(h * NY + y, ((h + step) % NH) * NY + y) for h in range(NH) for y in range(NY)])


def everywhere(array, target):
    pairs = []
    for x, low, core in places():
        for high in range(NH):
            for y in range(NY):
                to = target(x, low, core, high, y)
                if to is not None:
                    pairs.append(
                        (vec_of(x, low, core) * NH * NY + high * NY + y, vec_of(*to[:3]) * NH * NY + to[3] * NY + to[4])
                    )
    return lax.ppermute(array, ("vec", "pair"), pairs)


def exchange(array):
    return everywhere(array, lambda x, low, core, high, y: (x, high // NC, high % NC, low * NC + core, y))


def first_target(x, low, core, high, y):
    turn = (high - core) % NH
    return (x, low, core if turn % 2 == 0 else 1 - core, core + 2 if turn in (0, 3) else core, y)


def second_target(x, low, core, high, y):
    turn = (high - core) % NH
    return None if turn % 2 == 0 else (x, low, 1 - core, core + 2 if turn == 1 else core, y)


def diagonal_mask(rows, columns):
    row = lax.broadcasted_iota(jnp.int32, (rows, columns), 0)
    column = lax.broadcasted_iota(jnp.int32, (rows, columns), 1)
    return (row % GROUP) == (column // GROUP)


def groups_of(rows):
    return [(start, min(GROUP, rows - start)) for start in range(0, rows, GROUP)]


def factor_kernel(after, trial, block, out_ref):
    count, vectors, depth = block.shape
    product = jnp.dot(
        block[...].reshape(count * vectors, depth), trial[...], preferred_element_type=jnp.float32
    ).astype(jnp.bfloat16)
    out_ref[...] = product.reshape(count, vectors, trial.shape[1])


def bias_kernel(r0, r1, r2, r3, own, other, walker, neighbour, out_ref, stacked):
    stacked[: walker.shape[0], :] = walker[...]
    stacked[walker.shape[0] :, :] = neighbour[...]
    rows, vectors, depth = own.shape
    parts = []
    for factor in (own, other):
        total = jnp.zeros((8 * GROUP, GROUP * vectors), jnp.float32)
        tail = None
        for start, count in groups_of(rows):
            left = jnp.concatenate(
                [r[low, start : start + GROUP, :] for r in (r0, r1, r2, r3) for low in range(NL)], axis=0
            )
            right = factor[start : start + count].reshape(count * vectors, depth)
            product = lax.dot_general(left, right, NT, preferred_element_type=jnp.float32)
            if count == GROUP:
                total = total + product
            else:
                tail = product
        pieces = [total] if tail is None else [total, tail]
        summed = jnp.zeros((8, vectors), jnp.float32)
        for piece in pieces:
            width = piece.shape[1]
            kept = jnp.where(diagonal_mask(8 * GROUP, width), piece, 0.0)
            kept = jnp.sum(kept.reshape(8, GROUP, width), axis=1)
            pick = lax.broadcasted_iota(jnp.int32, (width, vectors), 0) % vectors == lax.broadcasted_iota(
                jnp.int32, (width, vectors), 1
            )
            summed = summed + jnp.dot(
                kept, pick.astype(jnp.float32), precision=lax.Precision.HIGHEST, preferred_element_type=jnp.float32
            )
        parts.append(summed)
    out_ref[...] = jnp.concatenate(parts, axis=1)


def coefficients_of(bias_refs, aux):
    b0, b1, b2, b3 = bias_refs
    bias = (b0[...] + b2[...]) + (b1[...] + b3[...])
    return aux[...] - jnp.clip(-root_step * bias, -shift_cap, shift_cap)


def block_diagonals(coefficients, vectors):
    tall, wide = 8 * GROUP, GROUP * vectors
    spread = (
        lax.broadcasted_iota(jnp.int32, (tall, 8), 0) // GROUP == lax.broadcasted_iota(jnp.int32, (tall, 8), 1)
    ).astype(jnp.bfloat16)
    repeat = (
        lax.broadcasted_iota(jnp.int32, (vectors, wide), 1) % vectors
        == lax.broadcasted_iota(jnp.int32, (vectors, wide), 0)
    ).astype(jnp.bfloat16)
    mask = diagonal_mask(tall, wide)
    blocks = []
    for at in range(2):
        piece = coefficients[:, at * vectors : (at + 1) * vectors]
        piece = jnp.dot(spread, piece, preferred_element_type=jnp.float32).astype(jnp.bfloat16)
        piece = jnp.dot(piece, repeat, preferred_element_type=jnp.float32)
        blocks.append(jnp.where(mask, piece, 0.0).astype(jnp.bfloat16))
    return blocks


def walker_sums(blocks, held, copies, other, base, store):
    half, vectors, columns = held.shape
    for (start, count), copy in zip(groups_of(half), copies):
        copy.wait()
        depth = count * vectors
        for left in range(0, columns, 512):
            right = min(columns, left + 512)
            total = jnp.dot(
                blocks[0][:, :depth],
                held[start : start + count, :, left:right].reshape(depth, right - left),
                preferred_element_type=jnp.float32,
            ) + jnp.dot(
                blocks[1][:, :depth],
                other[pl.ds(base + start, count), :, left:right].reshape(depth, right - left),
                preferred_element_type=jnp.float32,
            )
            total = total.astype(jnp.bfloat16)
            for walker in ALL:
                store(walker, start, count, left, right, total[walker * GROUP : walker * GROUP + count, :])


ALL = list(range(NX * NL))


def fetch(source, base, held, sems):
    copies = []
    for at, (start, count) in enumerate(groups_of(held.shape[0])):
        copy = pltpu.make_async_copy(
            source.at[pl.ds(base + start, count)], held.at[pl.ds(start, count)], sems.at[at]
        )
        copy.start()
        copies.append(copy)
    return copies


def away_kernel(at, b0, b1, b2, b3, aux, own, other, after, fields_ref, even_ref, odd_ref, held, sems):
    half = held.shape[0]
    base = (1 - at[0]) * half
    copies = fetch(own, base, held, sems)
    fields = coefficients_of((b0, b1, b2, b3), aux)
    fields_ref[...] = fields
    blocks = block_diagonals((root_step * fields).astype(jnp.bfloat16), own.shape[1])

    def store(walker, start, count, left, right, value):
        out = odd_ref if walker % NL else even_ref
        row = walker // NL * half + start
        out[row : row + count, left:right] = value

    walker_sums(blocks, held, copies, other, base, store)


def keep_kernel(at, fields, even, walkers, partner, own, other, p0, p1, p2, p3, odd_ref, stacked, held, sems):
    half = held.shape[0]
    base = at[0] * half
    copies = fetch(own, base, held, sems)
    blocks = block_diagonals((root_step * fields[...]).astype(jnp.bfloat16), own.shape[1])
    outs = (p0, p1, p2, p3)
    for step, out in enumerate(outs):
        out[half:, :] = even[step * half : (step + 1) * half, :]
    stacked[: walkers.shape[0], :] = walkers[...]
    stacked[walkers.shape[0] :, :] = partner[...]

    def store(walker, start, count, left, right, value):
        if walker % NL:
            row = walker // NL * half + start
            odd_ref[row : row + count, left:right] = value
        else:
            outs[walker // NL][start : start + count, left:right] = value

    walker_sums(blocks, held, copies, other, base, store)


def wide(value):
    return value.astype(jnp.float32)


def pair_sum_kernel(keep, arrived, o0, o1, o2, o3):
    half = o0.shape[0]
    for step, out in enumerate((o0, o1, o2, o3)):
        rows = slice(step * half, (step + 1) * half)
        out[...] = (wide(keep[rows, :]) + wide(arrived[rows, :])).astype(out.dtype)


def x_sum_kernel(p0, p1, p2, p3, out):
    half = out.shape[0]
    out[...] = (
        (wide(p0[half:, :]) + wide(p1[half:, :])) + (wide(p2[half:, :]) + wide(p3[half:, :]))
    ).astype(out.dtype)


def last_sum_kernel(at, p0, p1, p2, p3, arrived, q0, q1, q2, q3, w1, w2, w3, first, second):
    half = first.shape[0]
    even = (
        (wide(p0[:half, :]) + wide(p1[:half, :])) + (wide(p2[:half, :]) + wide(p3[:half, :]))
    ) + wide(arrived[...])
    odd = (wide(q0[...]) + wide(q1[...])) + (wide(q2[...]) + wide(q3[...]))
    turn = (at[0] - at[1] + NH) % NH
    pick = jnp.logical_or(turn == 1, turn == 2)
    first[...] = jnp.where(pick, even, odd).astype(first.dtype)
    second[...] = jnp.where(pick, odd, even).astype(second.dtype)


def choose_kernel(at, second, got, more, block0, block1):
    active = (at[0] + at[1]) % 2 == 0

    @pl.when(active)
    def _():
        block0[...] = second[...]
        block1[...] = got[...]

    @pl.when(jnp.logical_not(active))
    def _():
        block0[...] = got[...]
        block1[...] = more[...]


def stack_kernel(*refs, after=0):
    sources, out = refs[: len(refs) - 1 - after], refs[-1]
    half = sources[0].shape[0]
    for step, ref in enumerate(sources):
        out[step * half : (step + 1) * half, :] = ref[...]


def taylor_kernel(at, *refs):
    pieces, (w0, w1, w2, w3), (out_ref, held, operator, terms, total) = refs[:12], refs[12:16], refs[16:]
    high, y, low, core = at[0], at[1], at[2], at[3]
    half = held.shape[1]
    rows = 2 * half
    for side in range(2):
        base = high + (((high % 2) ^ core ^ side) & 1)
        mine = pieces[side * 6 : side * 6 + 6]
        for step in range(NY):
            row = ((base % NH) * NY + (y - step + NY) % NY) * NL
            held[row + low] = mine[step][:half, :]
            held[row + 1 - low] = mine[step][half:, :]
            row = (((base + 2) % NH) * NY + (y - step + NY) % NY) * NL
            held[row + low] = mine[4][step * half : (step + 1) * half, :]
            held[row + 1 - low] = mine[5][step * half : (step + 1) * half, :]
    for block in range(NH * NY * NL):
        operator[block * half : (block + 1) * half, :] = held[block]
    spread = terms.shape[2]
    for step, ref in enumerate((w0, w1, w2, w3)):
        for at_row in range(NL * NC):
            total[step, at_row] = ref[at_row * rows : (at_row + 1) * rows, :]
    for block in range(NH * NY):
        piece = total[
            (y - block % NY + NY) % NY, (((block // NY // NC) ^ low) * NC + ((block // NY % NC) ^ core))
        ]
        terms[0, block * rows : (block + 1) * rows, :] = piece
    mine = low * NC + core

    def one_term(degree, accumulated):
        source = (degree - 1) % 2

        product = jnp.dot(operator[...], terms[source], preferred_element_type=jnp.float32)
        terms[1 - source] = (product / degree.astype(jnp.float32)).astype(jnp.bfloat16)

        picked = jnp.zeros((rows, spread), jnp.float32)
        for block in range(NH * NY):
            piece = wide(terms[1 - source, block * rows : (block + 1) * rows, :])
            picked = jnp.where(mine * NY + y == block, piece, picked)
        return accumulated + picked

    accumulated = lax.fori_loop(1, TAYLOR + 1, one_term, wide(w0[:rows, :]))
    out_ref[...] = accumulated.astype(out_ref.dtype)


def call(kernel, outs, args, name, scratch=(), smem=0, idle=0, far=(), limit=16):
    specs = [SMEM] * smem + [VMEM] * (len(args) - smem - idle) + [FAR] * idle
    for at in far:
        specs[at] = FAR
    return pl.pallas_call(
        kernel,
        out_shape=outs,
        in_specs=specs,
        out_specs=[VMEM] * len(outs) if isinstance(outs, (list, tuple)) else VMEM,
        scratch_shapes=list(scratch),
        compiler_params=pltpu.CompilerParams(vmem_limit_bytes=limit * 2**20),
        name=name,
    )(*args)


def on_device(cholesky, walkers, inv_correlation, trial_orbitals, aux_fields):
    vectors, rows, orbitals = cholesky.shape
    occupied = walkers.shape[2]
    half = rows // NL
    bf16, f32 = jnp.bfloat16, jnp.float32
    shaped = jax.ShapeDtypeStruct
    me = lax.axis_index("vec")
    x, low, core = me // (NL * NC), (me // NC) % NL, me % NC
    pair = lax.axis_index("pair")
    high, y = pair // NY, pair % NY

    own = jnp.transpose(cholesky, (1, 0, 2))
    other = swap_core(own)
    aux_other = swap_core(aux_fields)
    rows_here = exchange(walkers[0])

    rotated = jnp.dot(
        walkers[0].astype(f32), inv_correlation[0], precision=lax.Precision.HIGHEST
    ).astype(bf16)
    rotated = jnp.pad(rotated, ((0, -rows % GROUP), (0, 0)))
    partner = swap_low(rotated)
    count = 20
    factor = pl.pallas_call(
        factor_kernel,
        out_shape=shaped((rows, vectors, occupied), bf16),
        grid=(rows // count,),
        in_specs=[
            FAR,
            pl.BlockSpec((orbitals, occupied), lambda i: (0, 0)),
            pl.BlockSpec((count, vectors, orbitals), lambda i: (i, 0, 0)),
        ],
        out_specs=pl.BlockSpec((count, vectors, occupied), lambda i: (i, 0, 0)),
        compiler_params=pltpu.CompilerParams(vmem_limit_bytes=16 * 2**20),
        cost_estimate=pl.CostEstimate(
            flops=2 * rows * vectors * orbitals * occupied, bytes_accessed=8 * 10**6, transcendentals=0
        ),
        name="vector_factor",
    )(rotated, trial_orbitals, own)
    both = jnp.where(low == 0, jnp.stack([rotated, partner]), jnp.stack([partner, rotated]))
    met = [both] + [send_x(both, -step) for step in range(1, NX)]

    bias, two_rows = call(
        bias_kernel,
        [shaped((8, 2 * vectors), f32), shaped((2 * rows, occupied), bf16)],
        (*met, factor, swap_core(factor), rows_here, swap_core(rows_here)),
        "force_bias",
    )
    from_y = [bias] + [send_y(bias, step) for step in range(1, NY)]
    rows_low = swap_low(two_rows)
    bias = (from_y[0] + from_y[2]) + (from_y[1] + from_y[3])
    from_h = [bias] + [send_h(bias, step) for step in range(1, NH)]

    order = jnp.arange(NX * NL)
    mine = vec_of(x + order // NL, order % NL, core)
    aux = jnp.concatenate([jnp.take(aux_fields, mine, axis=0), jnp.take(aux_other, mine, axis=0)], axis=1)

    piece, two, quad = [shaped((n * half, orbitals), bf16) for n in (1, 2, 4)]
    where = low.reshape(1).astype(jnp.int32)
    scratch = [pltpu.VMEM((half, vectors, orbitals), bf16), pltpu.SemaphoreType.DMA((len(groups_of(half)),))]
    shifted, even, away = call(
        away_kernel,
        [shaped((8, 2 * vectors), f32), quad, quad],
        (where, *from_h, aux, own, other, rows_low),
        "operator_away",
        scratch=scratch,
        smem=1,
        idle=1,
        far=(6,),
    )
    away = swap_low(away)
    *parts, keep, four_rows = call(
        keep_kernel,
        [two] * NX + [quad, shaped((4 * rows, occupied), bf16)],
        (where, shifted, even, two_rows, rows_low, own, other),
        "operator_keep",
        scratch=scratch,
        smem=1,
        far=(5,),
    )
    parts = [parts[0]] + [send_x(parts[step], step) for step in range(1, NX)]
    all_rows = [four_rows] + [send_y(four_rows, step) for step in range(1, NY)]
    odd = call(pair_sum_kernel, [piece] * NX, (keep, away), "pair_sum")
    odd = [odd[0]] + [send_x(odd[step], step) for step in range(1, NX)]
    even = swap_low(call(x_sum_kernel, piece, tuple(parts), "x_sum"))
    turn = jnp.stack([high, core]).astype(jnp.int32)
    first, second = call(
        last_sum_kernel, [piece] * 2, (turn, *parts, even, *odd, *all_rows[1:]), "last_sum", smem=1, idle=3
    )

    both = jnp.concatenate([shifted[:, :vectors], swap_core(shifted[:, vectors:])])
    walker = jnp.arange(NX * NL * NC)
    place = (
        ((walker % NC) ^ core) * (NX * NL) + ((walker // (NL * NC) - x) % NX) * NL + ((walker // NC) % NL)
    )
    fields = jnp.take(both, place, axis=0)

    got = everywhere(first, first_target)
    more = everywhere(second, second_target)
    block0, block1 = call(choose_kernel, [piece] * 2, (turn, second, got, more), "choose", smem=1)
    pair0 = call(stack_kernel, two, (block0, swap_low(block0)), "stack_low")
    block1s = [block1] + [send_y(block1, step) for step in range(1, NY)]
    quad1 = call(functools.partial(stack_kernel, after=1), quad, (*block1s, pair0), "stack_y", idle=1)
    pieces = [pair0] + [send_y(pair0, step) for step in range(1, NY)] + [quad1, swap_low(quad1)]
    pieces = pieces + [swap_core(p) for p in pieces]
    position = jnp.stack([high, y, low, core]).astype(jnp.int32)
    updated = call(
        taylor_kernel,
        shaped((rows, occupied), bf16),
        (position, *pieces, *all_rows),
        "taylor",
        scratch=[
            pltpu.VMEM((NH * NY * NL, half, orbitals), bf16),
            pltpu.VMEM((orbitals, orbitals), bf16),
            pltpu.VMEM((2, orbitals, occupied), bf16),
            pltpu.VMEM((NY, 4, rows, occupied), bf16),
        ],
        smem=1,
        limit=28,
    )
    return (exchange(updated)[None], fields)


def solution(mesh):
    placed = (
        P("vec", "pair", None),
        P("vec", "pair", None),
        P("vec", None, None),
        P(),
        P(None, "vec"),
    )
    return jax.shard_map(
        on_device,
        mesh=mesh,
        in_specs=placed,
        out_specs=(P("vec", "pair", None), P(None, "vec")),
        check_vma=False,
    )
```

```python
import functools

import jax
import jax.numpy as jnp
from jax import lax
from jax.experimental import pallas as pl
from jax.experimental.pallas import tpu as pltpu
from jax.sharding import PartitionSpec as P

TAYLOR = 6
NX, NL, NC = 4, 2, 2
NH, NY = 4, 4
PITCH = 56
GROUP = 16

root_step = 0.5
shift_cap = 1.0

VMEM = pl.BlockSpec(memory_space=pltpu.VMEM)
FAR = pl.BlockSpec(memory_space=pl.ANY)
SMEM = pl.BlockSpec(memory_space=pltpu.SMEM)
NT = (((1,), (1,)), ((), ()))


def vec_of(x, low, core):
    return ((x % NX) * NL + low) * NC + core


def places():
    return [(x, low, core) for x in range(NX) for low in range(NL) for core in range(NC)]


def send_x(array, step):
    return lax.ppermute(array, "vec", [(vec_of(*p), vec_of(p[0] + step, p[1], p[2])) for p in places()])


def swap_low(array):
    return lax.ppermute(array, "vec", [(vec_of(*p), vec_of(p[0], 1 - p[1], p[2])) for p in places()])


def swap_core(array):
    return lax.ppermute(array, "vec", [(vec_of(*p), vec_of(p[0], p[1], 1 - p[2])) for p in places()])


def send_y(array, step):
    return lax.ppermute(array, "pair", [(h * NY + y, h * NY + (y + step) % NY) for h in range(NH) for y in range(NY)])


def send_h(array, step):
    return lax.ppermute(array, "pair", [(h * NY + y, ((h + step) % NH) * NY + y) for h in range(NH) for y in range(NY)])


def everywhere(array, target):
    pairs = []
    for x, low, core in places():
        for high in range(NH):
            for y in range(NY):
                to = target(x, low, core, high, y)
                if to is not None:
                    pairs.append(
                        (vec_of(x, low, core) * NH * NY + high * NY + y, vec_of(*to[:3]) * NH * NY + to[3] * NY + to[4])
                    )
    return lax.ppermute(array, ("vec", "pair"), pairs)


def exchange(array):
    return everywhere(array, lambda x, low, core, high, y: (x, high // NC, high % NC, low * NC + core, y))


def first_target(x, low, core, high, y):
    turn = (high - core) % NH
    return (x, low, core if turn % 2 == 0 else 1 - core, core + 2 if turn in (0, 3) else core, y)


def second_target(x, low, core, high, y):
    turn = (high - core) % NH
    return None if turn % 2 == 0 else (x, low, 1 - core, core + 2 if turn == 1 else core, y)


def diagonal_mask(rows, columns):
    row = lax.broadcasted_iota(jnp.int32, (rows, columns), 0)
    column = lax.broadcasted_iota(jnp.int32, (rows, columns), 1)
    return (row % GROUP) == (column // GROUP)


def groups_of(rows):
    return [(start, min(GROUP, rows - start)) for start in range(0, rows, GROUP)]


def factor_kernel(after, trial, aux, block, out_ref, aux_out, block_out):
    aux_out[...] = aux[...]
    block_out[...] = block[...]
    count, vectors, depth = block.shape
    product = lax.dot_general(
        block[...].reshape(count * vectors, depth), trial[...], NT, preferred_element_type=jnp.float32
    ).astype(jnp.bfloat16)
    out_ref[...] = product.reshape(count, vectors, trial.shape[0])


def bias_kernel(r0, r1, r2, r3, own, other, out_ref):
    rows, vectors, depth = own.shape
    parts = []
    for factor in (own, other):
        total = jnp.zeros((8 * GROUP, GROUP * vectors), jnp.float32)
        tail = None
        for start, count in groups_of(rows):
            left = jnp.concatenate(
                [r[low, start : start + GROUP, :] for r in (r0, r1, r2, r3) for low in range(NL)], axis=0
            )
            right = factor[start : start + count].reshape(count * vectors, depth)
            product = lax.dot_general(left, right, NT, preferred_element_type=jnp.float32)
            if count == GROUP:
                total = total + product
            else:
                tail = product
        pieces = [total] if tail is None else [total, tail]
        summed = jnp.zeros((8, vectors), jnp.float32)
        for piece in pieces:
            width = piece.shape[1]
            kept = jnp.where(diagonal_mask(8 * GROUP, width), piece, 0.0)
            kept = jnp.sum(kept.reshape(8, GROUP, width), axis=1)
            pick = lax.broadcasted_iota(jnp.int32, (width, vectors), 0) % vectors == lax.broadcasted_iota(
                jnp.int32, (width, vectors), 1
            )
            summed = summed + jnp.dot(
                kept, pick.astype(jnp.float32), precision=lax.Precision.HIGHEST, preferred_element_type=jnp.float32
            )
        parts.append(summed)
    out_ref[...] = jnp.concatenate(parts, axis=1)


def coefficients_of(bias_refs, aux):
    b0, b1, b2, b3 = bias_refs
    bias = (b0[...] + b2[...]) + (b1[...] + b3[...])
    return aux[...] - jnp.clip(-root_step * bias, -shift_cap, shift_cap)


def block_diagonals(coefficients, vectors):
    tall, wide = 8 * GROUP, GROUP * vectors
    spread = (
        lax.broadcasted_iota(jnp.int32, (tall, 8), 0) // GROUP == lax.broadcasted_iota(jnp.int32, (tall, 8), 1)
    ).astype(jnp.bfloat16)
    repeat = (
        lax.broadcasted_iota(jnp.int32, (vectors, wide), 1) % vectors
        == lax.broadcasted_iota(jnp.int32, (vectors, wide), 0)
    ).astype(jnp.bfloat16)
    mask = diagonal_mask(tall, wide)
    blocks = []
    for at in range(2):
        piece = coefficients[:, at * vectors : (at + 1) * vectors]
        piece = jnp.dot(spread, piece, preferred_element_type=jnp.float32).astype(jnp.bfloat16)
        piece = jnp.dot(piece, repeat, preferred_element_type=jnp.float32)
        blocks.append(jnp.where(mask, piece, 0.0).astype(jnp.bfloat16))
    return blocks


def walker_sums(blocks, own, other, base, half, store):
    vectors, columns = own.shape[1:]
    for start, count in groups_of(half):
        depth = count * vectors
        for left in range(0, columns, 512):
            right = min(columns, left + 512)
            total = jnp.dot(
                blocks[0][:, :depth],
                own[pl.ds(base + start, count), :, left:right].reshape(depth, right - left),
                preferred_element_type=jnp.float32,
            ) + jnp.dot(
                blocks[1][:, :depth],
                other[pl.ds(base + start, count), :, left:right].reshape(depth, right - left),
                preferred_element_type=jnp.float32,
            )
            total = total.astype(jnp.bfloat16)
            for walker in ALL:
                store(walker, start, count, left, right, total[walker * GROUP : walker * GROUP + count, :])


ALL = list(range(NX * NL))


def away_kernel(at, b0, b1, b2, b3, aux, own, other, fields_ref, e0, e1, e2, e3, odd_ref):
    half = e0.shape[0]
    base = (1 - at[0]) * half
    fields = coefficients_of((b0, b1, b2, b3), aux)
    fields_ref[...] = fields
    blocks = block_diagonals((root_step * fields).astype(jnp.bfloat16), own.shape[1])
    outs = (e0, e1, e2, e3)

    def store(walker, start, count, left, right, value):
        if walker % NL:
            row = walker // NL * PITCH + start
            odd_ref[row : row + count, left:right] = value
        else:
            outs[walker // NL][start : start + count, left:right] = value

    walker_sums(blocks, own, other, base, half, store)


def keep_kernel(at, fields, walkers, own, other, e0, e1, e2, e3, o0, o1, o2, o3, walkers_out):
    half = e0.shape[0]
    base = at[0] * half
    walkers_out[...] = walkers[...]
    blocks = block_diagonals((root_step * fields[...]).astype(jnp.bfloat16), own.shape[1])
    outs = (e0, o0, e1, o1, e2, o2, e3, o3)

    def store(walker, start, count, left, right, value):
        outs[walker][start : start + count, left:right] = value

    walker_sums(blocks, own, other, base, half, store)


def wide(value):
    return value.astype(jnp.float32)


def pair_sum_kernel(k0, k1, k2, k3, arrived, w0, w1, w2, w3, o0, o1, o2, o3, stacked):
    half, rows = o0.shape[0], w0.shape[0]
    for step, walkers in enumerate((w0, w1, w2, w3)):
        stacked[step * rows : (step + 1) * rows, :] = walkers[...]
    for step, (keep, out) in enumerate(((k0, o0), (k1, o1), (k2, o2), (k3, o3))):
        out[...] = (wide(keep[...]) + wide(arrived[step * PITCH : step * PITCH + half, :])).astype(out.dtype)


def x_sum_kernel(p0, p1, p2, p3, out):
    out[...] = ((wide(p0[...]) + wide(p1[...])) + (wide(p2[...]) + wide(p3[...]))).astype(out.dtype)


def last_sum_kernel(at, p0, p1, p2, p3, arrived, q0, q1, q2, q3, after, first, second):
    even = ((wide(p0[...]) + wide(p1[...])) + (wide(p2[...]) + wide(p3[...]))) + wide(arrived[...])
    odd = (wide(q0[...]) + wide(q1[...])) + (wide(q2[...]) + wide(q3[...]))
    turn = (at[0] - at[1] + NH) % NH
    pick = jnp.logical_or(turn == 1, turn == 2)
    first[...] = jnp.where(pick, even, odd).astype(first.dtype)
    second[...] = jnp.where(pick, odd, even).astype(second.dtype)


def choose_kernel(at, second, got, more, walkers, neighbours, block0, block1, stacked):
    stacked[: walkers.shape[0], :] = walkers[...]
    stacked[walkers.shape[0] :, :] = neighbours[...]
    active = (at[0] + at[1]) % 2 == 0

    @pl.when(active)
    def _():
        block0[...] = second[...]
        block1[...] = got[...]

    @pl.when(jnp.logical_not(active))
    def _():
        block0[...] = got[...]
        block1[...] = more[...]


def stack_kernel(*refs, after=0):
    sources, out = refs[: len(refs) - 1 - after], refs[-1]
    half = sources[0].shape[0]
    for step, ref in enumerate(sources):
        out[step * half : (step + 1) * half, :] = ref[...]


def taylor_kernel(at, *refs):
    pieces, (walkers, partners), (out_ref, held, operator, terms, total) = refs[:12], refs[12:14], refs[14:]
    high, y, low, core = at[0], at[1], at[2], at[3]
    half = held.shape[1]
    rows = 2 * half
    for side in range(2):
        base = high + (((high % 2) ^ core ^ side) & 1)
        mine = pieces[side * 6 : side * 6 + 6]
        for step in range(NY):
            row = ((base % NH) * NY + (y - step + NY) % NY) * NL
            held[row + low] = mine[step][:half, :]
            held[row + 1 - low] = mine[step][half:, :]
            row = (((base + 2) % NH) * NY + (y - step + NY) % NY) * NL
            held[row + low] = mine[4][step * half : (step + 1) * half, :]
            held[row + 1 - low] = mine[5][step * half : (step + 1) * half, :]
    for block in range(NH * NY * NL):
        operator[block * half : (block + 1) * half, :] = held[block]
    spread = terms.shape[2]
    for far, ref in enumerate((walkers, partners)):
        for step in range(NC * NY):
            total[far, step // NY, step % NY] = ref[step * rows : (step + 1) * rows, :]
    for block in range(NH * NY):
        row, column = block // NY, block % NY
        piece = total[(row // NC) ^ low, (row % NC) ^ core, (y - column + NY) % NY]
        terms[0, block * rows : (block + 1) * rows, :] = piece
    mine = low * NC + core

    def one_term(degree, accumulated):
        source = (degree - 1) % 2

        product = jnp.dot(operator[...], terms[source], preferred_element_type=jnp.float32)
        terms[1 - source] = (product / degree.astype(jnp.float32)).astype(jnp.bfloat16)

        picked = jnp.zeros((rows, spread), jnp.float32)
        for block in range(NH * NY):
            piece = wide(terms[1 - source, block * rows : (block + 1) * rows, :])
            picked = jnp.where(mine * NY + y == block, piece, picked)
        return accumulated + picked

    accumulated = lax.fori_loop(1, TAYLOR + 1, one_term, wide(walkers[:rows, :]))
    out_ref[...] = accumulated.astype(out_ref.dtype)


def call(kernel, outs, args, name, scratch=(), smem=0, idle=0, limit=16):
    specs = [SMEM] * smem + [VMEM] * (len(args) - smem - idle) + [FAR] * idle
    return pl.pallas_call(
        kernel,
        out_shape=outs,
        in_specs=specs,
        out_specs=[VMEM] * len(outs) if isinstance(outs, (list, tuple)) else VMEM,
        scratch_shapes=list(scratch),
        compiler_params=pltpu.CompilerParams(vmem_limit_bytes=limit * 2**20),
        name=name,
    )(*args)


def on_device(cholesky, walkers, inv_correlation, trial_orbitals, aux_fields):
    vectors, rows, orbitals = cholesky.shape
    occupied = walkers.shape[2]
    half = rows // NL
    bf16, f32 = jnp.bfloat16, jnp.float32
    shaped = jax.ShapeDtypeStruct
    me = lax.axis_index("vec")
    x, low, core = me // (NL * NC), (me // NC) % NL, me % NC
    pair = lax.axis_index("pair")
    high, y = pair // NY, pair % NY

    own = jnp.transpose(cholesky, (1, 0, 2))
    other = swap_core(own)

    rotated = jnp.dot(
        walkers[0].astype(f32), inv_correlation[0], precision=lax.Precision.HIGHEST
    ).astype(bf16)
    rotated = jnp.pad(rotated, ((0, -rows % GROUP), (0, 0)))
    partner = swap_low(rotated)
    count = 20
    factor, aux_here, near = pl.pallas_call(
        factor_kernel,
        out_shape=[shaped((rows, vectors, occupied), bf16), shaped(aux_fields.shape, f32), shaped(own.shape, bf16)],
        grid=(rows // count,),
        in_specs=[
            FAR,
            pl.BlockSpec((occupied, orbitals), lambda i: (0, 0)),
            pl.BlockSpec(aux_fields.shape, lambda i: (0, 0)),
            pl.BlockSpec((count, vectors, orbitals), lambda i: (i, 0, 0)),
        ],
        out_specs=[
            pl.BlockSpec((count, vectors, occupied), lambda i: (i, 0, 0)),
            pl.BlockSpec(aux_fields.shape, lambda i: (0, 0)),
            pl.BlockSpec((count, vectors, orbitals), lambda i: (i, 0, 0)),
        ],
        compiler_params=pltpu.CompilerParams(vmem_limit_bytes=46 * 2**20),
        cost_estimate=pl.CostEstimate(
            flops=2 * rows * vectors * orbitals * occupied, bytes_accessed=8 * 10**6, transcendentals=0
        ),
        name="vector_factor",
    )(rotated, trial_orbitals.T, aux_fields, own)
    both = jnp.where(low == 0, jnp.stack([rotated, partner]), jnp.stack([partner, rotated]))
    met = [both] + [send_x(both, -step) for step in range(1, NX)]

    aux_other = swap_core(aux_here)
    bias = call(
        bias_kernel,
        shaped((8, 2 * vectors), f32),
        (*met, factor, swap_core(factor)),
        "force_bias",
    )
    from_y = [bias] + [send_y(bias, step) for step in range(1, NY)]
    bias = (from_y[0] + from_y[2]) + (from_y[1] + from_y[3])
    from_h = [bias] + [send_h(bias, step) for step in range(1, NH)]

    order = jnp.arange(NX * NL)
    mine = vec_of(x + order // NL, order % NL, core)
    aux = jnp.concatenate([jnp.take(aux_fields, mine, axis=0), jnp.take(aux_other, mine, axis=0)], axis=1)

    piece, two, quad = [shaped((n * half, orbitals), bf16) for n in (1, 2, 4)]
    where = low.reshape(1).astype(jnp.int32)
    shifted, *even_away, odd_away = call(
        away_kernel,
        [shaped((8, 2 * vectors), f32)] + [piece] * NX + [shaped((NX * PITCH, orbitals), bf16)],
        (where, *from_h, aux, near, other),
        "operator_away",
        smem=1,
    )
    odd_away = swap_low(odd_away)
    even_away = [even_away[0]] + [send_x(even_away[step], step) for step in range(1, NX)]
    *parts, walkers_here = call(
        keep_kernel,
        [piece] * (2 * NX) + [shaped((rows, occupied), bf16)],
        (where, shifted, walkers[0], near, other),
        "operator_keep",
        smem=1,
    )
    even, odd = parts[:NX], parts[NX:]
    even = [even[0]] + [send_x(even[step], step) for step in range(1, NX)]
    arrived = swap_low(call(x_sum_kernel, piece, tuple(even_away), "x_sum"))
    along_y = [walkers_here] + [send_y(walkers_here, step) for step in range(1, NY)]
    *odd, four_rows = call(
        pair_sum_kernel, [piece] * NX + [shaped((NY * rows, occupied), bf16)], (*odd, odd_away, *along_y), "pair_sum"
    )
    odd = [odd[0]] + [send_x(odd[step], step) for step in range(1, NX)]
    rows_here = exchange(four_rows)
    turn = jnp.stack([high, core]).astype(jnp.int32)
    first, second = call(
        last_sum_kernel, [piece] * 2, (turn, *even, arrived, *odd, rows_here), "last_sum", smem=1, idle=1
    )

    both = jnp.concatenate([shifted[:, :vectors], swap_core(shifted[:, vectors:])])
    walker = jnp.arange(NX * NL * NC)
    place = (
        ((walker % NC) ^ core) * (NX * NL) + ((walker // (NL * NC) - x) % NX) * NL + ((walker // NC) % NL)
    )
    fields = jnp.take(both, place, axis=0)

    got = everywhere(first, first_target)
    more = everywhere(second, second_target)
    block0, block1, all_rows = call(
        choose_kernel,
        [piece] * 2 + [shaped((NC * NY * rows, occupied), bf16)],
        (turn, second, got, more, rows_here, swap_core(rows_here)),
        "choose",
        smem=1,
    )
    low_rows = swap_low(all_rows)
    pair0 = call(stack_kernel, two, (block0, swap_low(block0)), "stack_low")
    block1s = [block1] + [send_y(block1, step) for step in range(1, NY)]
    quad1 = call(functools.partial(stack_kernel, after=2), quad, (*block1s, pair0, low_rows), "stack_y", idle=2)
    pieces = [pair0] + [send_y(pair0, step) for step in range(1, NY)] + [quad1, swap_low(quad1)]
    pieces = pieces + [swap_core(p) for p in pieces]
    position = jnp.stack([high, y, low, core]).astype(jnp.int32)
    updated = call(
        taylor_kernel,
        shaped((rows, occupied), bf16),
        (position, *pieces, all_rows, low_rows),
        "taylor",
        scratch=[
            pltpu.VMEM((NH * NY * NL, half, orbitals), bf16),
            pltpu.VMEM((orbitals, orbitals), bf16),
            pltpu.VMEM((2, orbitals, occupied), bf16),
            pltpu.VMEM((NL, NC, NY, rows, occupied), bf16),
        ],
        smem=1,
        limit=28,
    )
    return (exchange(updated)[None], fields)


def solution(mesh):
    placed = (
        P("vec", "pair", None),
        P("vec", "pair", None),
        P("vec", None, None),
        P(),
        P(None, "vec"),
    )
    return jax.shard_map(
        on_device,
        mesh=mesh,
        in_specs=placed,
        out_specs=(P("vec", "pair", None), P(None, "vec")),
        check_vma=False,
    )
```

```python
import functools

import jax
import jax.numpy as jnp
from jax import lax
from jax.experimental import pallas as pl
from jax.experimental.pallas import tpu as pltpu
from jax.sharding import PartitionSpec as P

TAYLOR = 6
NX, NL, NC = 4, 2, 2
NH, NY = 4, 4
PITCH = 56
GROUP = 16

root_step = 0.5
shift_cap = 1.0

VMEM = pl.BlockSpec(memory_space=pltpu.VMEM)
FAR = pl.BlockSpec(memory_space=pl.ANY)
SMEM = pl.BlockSpec(memory_space=pltpu.SMEM)
NT = (((1,), (1,)), ((), ()))


def vec_of(x, low, core):
    return ((x % NX) * NL + low) * NC + core


def places():
    return [(x, low, core) for x in range(NX) for low in range(NL) for core in range(NC)]


def send_x(array, step):
    return lax.ppermute(array, "vec", [(vec_of(*p), vec_of(p[0] + step, p[1], p[2])) for p in places()])


def swap_low(array):
    return lax.ppermute(array, "vec", [(vec_of(*p), vec_of(p[0], 1 - p[1], p[2])) for p in places()])


def swap_core(array):
    return lax.ppermute(array, "vec", [(vec_of(*p), vec_of(p[0], p[1], 1 - p[2])) for p in places()])


def send_y(array, step):
    return lax.ppermute(array, "pair", [(h * NY + y, h * NY + (y + step) % NY) for h in range(NH) for y in range(NY)])


def send_h(array, step):
    return lax.ppermute(array, "pair", [(h * NY + y, ((h + step) % NH) * NY + y) for h in range(NH) for y in range(NY)])


def everywhere(array, target):
    pairs = []
    for x, low, core in places():
        for high in range(NH):
            for y in range(NY):
                to = target(x, low, core, high, y)
                if to is not None:
                    pairs.append(
                        (vec_of(x, low, core) * NH * NY + high * NY + y, vec_of(*to[:3]) * NH * NY + to[3] * NY + to[4])
                    )
    return lax.ppermute(array, ("vec", "pair"), pairs)


def exchange(array):
    return everywhere(array, lambda x, low, core, high, y: (x, high // NC, high % NC, low * NC + core, y))


def first_target(x, low, core, high, y):
    turn = (high - core) % NH
    return (x, low, core if turn % 2 == 0 else 1 - core, core + 2 if turn in (0, 3) else core, y)


def second_target(x, low, core, high, y):
    turn = (high - core) % NH
    return None if turn % 2 == 0 else (x, low, 1 - core, core + 2 if turn == 1 else core, y)


def diagonal_mask(rows, columns):
    row = lax.broadcasted_iota(jnp.int32, (rows, columns), 0)
    column = lax.broadcasted_iota(jnp.int32, (rows, columns), 1)
    return (row % GROUP) == (column // GROUP)


def groups_of(rows):
    return [(start, min(GROUP, rows - start)) for start in range(0, rows, GROUP)]


def factor_kernel(after, trial, block, out_ref):
    count, vectors, depth = block.shape
    product = lax.dot_general(
        block[...].reshape(count * vectors, depth), trial[...], NT, preferred_element_type=jnp.float32
    ).astype(jnp.bfloat16)
    out_ref[...] = product.reshape(count, vectors, trial.shape[0])


def bias_kernel(r0, r1, r2, r3, own, other, aux, walkers, passed, out_ref, aux_out, walkers_out, passed_out):
    aux_out[...] = aux[...]
    walkers_out[...] = walkers[...]
    rows, vectors, depth = own.shape
    parts = []
    for factor in (own, other):
        total = jnp.zeros((8 * GROUP, GROUP * vectors), jnp.float32)
        tail = None
        for start, count in groups_of(rows):
            left = jnp.concatenate(
                [r[low, start : start + GROUP, :] for r in (r0, r1, r2, r3) for low in range(NL)], axis=0
            )
            right = factor[start : start + count].reshape(count * vectors, depth)
            product = lax.dot_general(left, right, NT, preferred_element_type=jnp.float32)
            if count == GROUP:
                total = total + product
            else:
                tail = product
        pieces = [total] if tail is None else [total, tail]
        summed = jnp.zeros((8, vectors), jnp.float32)
        for piece in pieces:
            width = piece.shape[1]
            kept = jnp.where(diagonal_mask(8 * GROUP, width), piece, 0.0)
            kept = jnp.sum(kept.reshape(8, GROUP, width), axis=1)
            pick = lax.broadcasted_iota(jnp.int32, (width, vectors), 0) % vectors == lax.broadcasted_iota(
                jnp.int32, (width, vectors), 1
            )
            summed = summed + jnp.dot(
                kept, pick.astype(jnp.float32), precision=lax.Precision.HIGHEST, preferred_element_type=jnp.float32
            )
        parts.append(summed)
    out_ref[...] = jnp.concatenate(parts, axis=1)


def coefficients_of(bias_refs, aux):
    b0, b1, b2, b3 = bias_refs
    bias = (b0[...] + b2[...]) + (b1[...] + b3[...])
    return aux[...] - jnp.clip(-root_step * bias, -shift_cap, shift_cap)


def block_diagonals(coefficients, vectors):
    tall, wide = 8 * GROUP, GROUP * vectors
    spread = (
        lax.broadcasted_iota(jnp.int32, (tall, 8), 0) // GROUP == lax.broadcasted_iota(jnp.int32, (tall, 8), 1)
    ).astype(jnp.bfloat16)
    repeat = (
        lax.broadcasted_iota(jnp.int32, (vectors, wide), 1) % vectors
        == lax.broadcasted_iota(jnp.int32, (vectors, wide), 0)
    ).astype(jnp.bfloat16)
    mask = diagonal_mask(tall, wide)
    blocks = []
    for at in range(2):
        piece = coefficients[:, at * vectors : (at + 1) * vectors]
        piece = jnp.dot(spread, piece, preferred_element_type=jnp.float32).astype(jnp.bfloat16)
        piece = jnp.dot(piece, repeat, preferred_element_type=jnp.float32)
        blocks.append(jnp.where(mask, piece, 0.0).astype(jnp.bfloat16))
    return blocks


def walker_sums(blocks, own, other, base, half, store):
    vectors, columns = own.shape[1:]
    for start, count in groups_of(half):
        depth = count * vectors
        for left in range(0, columns, 512):
            right = min(columns, left + 512)
            total = jnp.dot(
                blocks[0][:, :depth],
                own[pl.ds(base + start, count), :, left:right].reshape(depth, right - left),
                preferred_element_type=jnp.float32,
            ) + jnp.dot(
                blocks[1][:, :depth],
                other[pl.ds(base + start, count), :, left:right].reshape(depth, right - left),
                preferred_element_type=jnp.float32,
            )
            total = total.astype(jnp.bfloat16)
            for walker in ALL:
                store(walker, start, count, left, right, total[walker * GROUP : walker * GROUP + count, :])


ALL = list(range(NX * NL))


def away_kernel(at, b0, b1, b2, b3, aux, walkers, neighbours, own, other, fields_ref, e0, e1, e2, e3, odd_ref, two_rows):
    two_rows[: walkers.shape[0], :] = walkers[...]
    two_rows[walkers.shape[0] :, :] = neighbours[...]
    half = e0.shape[0]
    base = (1 - at[0]) * half
    fields = coefficients_of((b0, b1, b2, b3), aux)
    fields_ref[...] = fields
    blocks = block_diagonals((root_step * fields).astype(jnp.bfloat16), own.shape[1])
    outs = (e0, e1, e2, e3)

    def store(walker, start, count, left, right, value):
        if walker % NL:
            row = walker // NL * PITCH + start
            odd_ref[row : row + count, left:right] = value
        else:
            outs[walker // NL][start : start + count, left:right] = value

    walker_sums(blocks, own, other, base, half, store)


def keep_kernel(at, fields, own, other, e0, e1, e2, e3, o0, o1, o2, o3):
    half = e0.shape[0]
    base = at[0] * half
    blocks = block_diagonals((root_step * fields[...]).astype(jnp.bfloat16), own.shape[1])
    outs = (e0, o0, e1, o1, e2, o2, e3, o3)

    def store(walker, start, count, left, right, value):
        outs[walker][start : start + count, left:right] = value

    walker_sums(blocks, own, other, base, half, store)


def wide(value):
    return value.astype(jnp.float32)


def pair_sum_kernel(k0, k1, k2, k3, arrived, o0, o1, o2, o3):
    half = o0.shape[0]
    for step, (keep, out) in enumerate(((k0, o0), (k1, o1), (k2, o2), (k3, o3))):
        out[...] = (wide(keep[...]) + wide(arrived[step * PITCH : step * PITCH + half, :])).astype(out.dtype)


def x_sum_kernel(p0, p1, p2, p3, out):
    out[...] = ((wide(p0[...]) + wide(p1[...])) + (wide(p2[...]) + wide(p3[...]))).astype(out.dtype)


def last_sum_kernel(at, p0, p1, p2, p3, arrived, q0, q1, q2, q3, walkers, partners, first, second, stacked):
    stacked[: walkers.shape[0], :] = walkers[...]
    stacked[walkers.shape[0] :, :] = partners[...]
    even = ((wide(p0[...]) + wide(p1[...])) + (wide(p2[...]) + wide(p3[...]))) + wide(arrived[...])
    odd = (wide(q0[...]) + wide(q1[...])) + (wide(q2[...]) + wide(q3[...]))
    turn = (at[0] - at[1] + NH) % NH
    pick = jnp.logical_or(turn == 1, turn == 2)
    first[...] = jnp.where(pick, even, odd).astype(first.dtype)
    second[...] = jnp.where(pick, odd, even).astype(second.dtype)


def choose_kernel(at, second, got, more, w1, w2, w3, block0, block1):
    active = (at[0] + at[1]) % 2 == 0

    @pl.when(active)
    def _():
        block0[...] = second[...]
        block1[...] = got[...]

    @pl.when(jnp.logical_not(active))
    def _():
        block0[...] = got[...]
        block1[...] = more[...]


def stack_kernel(*refs, after=0):
    sources, out = refs[: len(refs) - 1 - after], refs[-1]
    half = sources[0].shape[0]
    for step, ref in enumerate(sources):
        out[step * half : (step + 1) * half, :] = ref[...]


def taylor_kernel(at, *refs):
    pieces, walkers, (out_ref, held, operator, terms, total) = refs[:12], refs[12:16], refs[16:]
    high, y, low, core = at[0], at[1], at[2], at[3]
    half = held.shape[1]
    rows = 2 * half
    for side in range(2):
        base = high + (((high % 2) ^ core ^ side) & 1)
        mine = pieces[side * 6 : side * 6 + 6]
        for step in range(NY):
            row = ((base % NH) * NY + (y - step + NY) % NY) * NL
            held[row + low] = mine[step][:half, :]
            held[row + 1 - low] = mine[step][half:, :]
            row = (((base + 2) % NH) * NY + (y - step + NY) % NY) * NL
            held[row + low] = mine[4][step * half : (step + 1) * half, :]
            held[row + 1 - low] = mine[5][step * half : (step + 1) * half, :]
    for block in range(NH * NY * NL):
        operator[block * half : (block + 1) * half, :] = held[block]
    spread = terms.shape[2]
    for step, ref in enumerate(walkers):
        for at_row in range(NL * NC):
            total[step, at_row // NC, at_row % NC] = ref[at_row * rows : (at_row + 1) * rows, :]
    for block in range(NH * NY):
        row, column = block // NY, block % NY
        piece = total[(y - column + NY) % NY, (row // NC) ^ low, (row % NC) ^ core]
        terms[0, block * rows : (block + 1) * rows, :] = piece
    mine = low * NC + core

    def one_term(degree, accumulated):
        source = (degree - 1) % 2

        product = jnp.dot(operator[...], terms[source], preferred_element_type=jnp.float32)
        terms[1 - source] = (product / degree.astype(jnp.float32)).astype(jnp.bfloat16)

        picked = jnp.zeros((rows, spread), jnp.float32)
        for block in range(NH * NY):
            piece = wide(terms[1 - source, block * rows : (block + 1) * rows, :])
            picked = jnp.where(mine * NY + y == block, piece, picked)
        return accumulated + picked

    accumulated = lax.fori_loop(1, TAYLOR + 1, one_term, wide(walkers[0][:rows, :]))
    out_ref[...] = accumulated.astype(out_ref.dtype)


def call(kernel, outs, args, name, scratch=(), smem=0, idle=0, limit=16):
    specs = [SMEM] * smem + [VMEM] * (len(args) - smem - idle) + [FAR] * idle
    return pl.pallas_call(
        kernel,
        out_shape=outs,
        in_specs=specs,
        out_specs=[VMEM] * len(outs) if isinstance(outs, (list, tuple)) else VMEM,
        scratch_shapes=list(scratch),
        compiler_params=pltpu.CompilerParams(vmem_limit_bytes=limit * 2**20),
        name=name,
    )(*args)


def on_device(cholesky, walkers, inv_correlation, trial_orbitals, aux_fields):
    vectors, rows, orbitals = cholesky.shape
    occupied = walkers.shape[2]
    half = rows // NL
    bf16, f32 = jnp.bfloat16, jnp.float32
    shaped = jax.ShapeDtypeStruct
    me = lax.axis_index("vec")
    x, low, core = me // (NL * NC), (me // NC) % NL, me % NC
    pair = lax.axis_index("pair")
    high, y = pair // NY, pair % NY

    own = jnp.transpose(cholesky, (1, 0, 2))
    other = swap_core(own)

    rotated = jnp.dot(
        walkers[0].astype(f32), inv_correlation[0], precision=lax.Precision.HIGHEST
    ).astype(bf16)
    rotated = jnp.pad(rotated, ((0, -rows % GROUP), (0, 0)))
    partner = swap_low(rotated)
    count = 20
    factor = pl.pallas_call(
        factor_kernel,
        out_shape=shaped((rows, vectors, occupied), bf16),
        grid=(rows // count,),
        in_specs=[
            FAR,
            pl.BlockSpec((occupied, orbitals), lambda i: (0, 0)),
            pl.BlockSpec((count, vectors, orbitals), lambda i: (i, 0, 0)),
        ],
        out_specs=pl.BlockSpec((count, vectors, occupied), lambda i: (i, 0, 0)),
        compiler_params=pltpu.CompilerParams(vmem_limit_bytes=52 * 2**20),
        cost_estimate=pl.CostEstimate(
            flops=2 * rows * vectors * orbitals * occupied, bytes_accessed=8 * 10**6, transcendentals=0
        ),
        name="vector_factor",
    )(rotated, trial_orbitals.T, own)
    both = jnp.where(low == 0, jnp.stack([rotated, partner]), jnp.stack([partner, rotated]))
    met = [both] + [send_x(both, -step) for step in range(1, NX)]

    rows_here = exchange(walkers[0])
    bias, aux_here, rows_here, other = pl.pallas_call(
        bias_kernel,
        out_shape=[
            shaped((8, 2 * vectors), f32),
            shaped(aux_fields.shape, f32),
            shaped((rows, occupied), bf16),
            shaped(other.shape, bf16),
        ],
        in_specs=[VMEM] * 8 + [FAR],
        out_specs=[VMEM] * 3 + [FAR],
        input_output_aliases={8: 3},
        compiler_params=pltpu.CompilerParams(vmem_limit_bytes=16 * 2**20),
        name="force_bias",
    )(*met, factor, swap_core(factor), aux_fields, rows_here, other)
    from_y = [bias] + [send_y(bias, step) for step in range(1, NY)]
    bias = (from_y[0] + from_y[2]) + (from_y[1] + from_y[3])
    from_h = [bias] + [send_h(bias, step) for step in range(1, NH)]

    aux_other = swap_core(aux_here)
    near = swap_core(other)
    order = jnp.arange(NX * NL)
    mine = vec_of(x + order // NL, order % NL, core)
    aux = jnp.concatenate([jnp.take(aux_fields, mine, axis=0), jnp.take(aux_other, mine, axis=0)], axis=1)

    piece, two, quad = [shaped((n * half, orbitals), bf16) for n in (1, 2, 4)]
    where = low.reshape(1).astype(jnp.int32)
    shifted, *even_away, odd_away, two_rows = call(
        away_kernel,
        [shaped((8, 2 * vectors), f32)]
        + [piece] * NX
        + [shaped((NX * PITCH, orbitals), bf16), shaped((NC * rows, occupied), bf16)],
        (where, *from_h, aux, rows_here, swap_core(rows_here), near, other),
        "operator_away",
        smem=1,
    )
    odd_away = swap_low(odd_away)
    low_rows = swap_low(two_rows)
    even_away = [even_away[0]] + [send_x(even_away[step], step) for step in range(1, NX)]
    parts = call(
        keep_kernel,
        [piece] * (2 * NX),
        (where, shifted, near, other),
        "operator_keep",
        smem=1,
    )
    even, odd = parts[:NX], parts[NX:]
    even = [even[0]] + [send_x(even[step], step) for step in range(1, NX)]
    arrived = swap_low(call(x_sum_kernel, piece, tuple(even_away), "x_sum"))
    odd = call(pair_sum_kernel, [piece] * NX, (*odd, odd_away), "pair_sum")
    odd = [odd[0]] + [send_x(odd[step], step) for step in range(1, NX)]
    turn = jnp.stack([high, core]).astype(jnp.int32)
    first, second, four_rows = call(
        last_sum_kernel,
        [piece] * 2 + [shaped((NL * NC * rows, occupied), bf16)],
        (turn, *even, arrived, *odd, two_rows, low_rows),
        "last_sum",
        smem=1,
    )
    all_rows = [four_rows] + [send_y(four_rows, step) for step in range(1, NY)]

    both = jnp.concatenate([shifted[:, :vectors], swap_core(shifted[:, vectors:])])
    walker = jnp.arange(NX * NL * NC)
    place = (
        ((walker % NC) ^ core) * (NX * NL) + ((walker // (NL * NC) - x) % NX) * NL + ((walker // NC) % NL)
    )
    fields = jnp.take(both, place, axis=0)

    got = everywhere(first, first_target)
    more = everywhere(second, second_target)
    block0, block1 = call(
        choose_kernel, [piece] * 2, (turn, second, got, more, *all_rows[1:]), "choose", smem=1, idle=3
    )
    pair0 = call(stack_kernel, two, (block0, swap_low(block0)), "stack_low")
    block1s = [block1] + [send_y(block1, step) for step in range(1, NY)]
    quad1 = call(functools.partial(stack_kernel, after=1), quad, (*block1s, pair0), "stack_y", idle=1)
    pieces = [pair0] + [send_y(pair0, step) for step in range(1, NY)] + [quad1, swap_low(quad1)]
    pieces = pieces + [swap_core(p) for p in pieces]
    position = jnp.stack([high, y, low, core]).astype(jnp.int32)
    updated = call(
        taylor_kernel,
        shaped((rows, occupied), bf16),
        (position, *pieces, *all_rows),
        "taylor",
        scratch=[
            pltpu.VMEM((NH * NY * NL, half, orbitals), bf16),
            pltpu.VMEM((orbitals, orbitals), bf16),
            pltpu.VMEM((2, orbitals, occupied), bf16),
            pltpu.VMEM((NY, NL, NC, rows, occupied), bf16),
        ],
        smem=1,
        limit=28,
    )
    return (exchange(updated)[None], fields)


def solution(mesh):
    placed = (
        P("vec", "pair", None),
        P("vec", "pair", None),
        P("vec", None, None),
        P(),
        P(None, "vec"),
    )
    return jax.shard_map(
        on_device,
        mesh=mesh,
        in_specs=placed,
        out_specs=(P("vec", "pair", None), P(None, "vec")),
        check_vma=False,
    )
```

```python
import jax
import jax.numpy as jnp
from jax import lax
from jax.experimental import pallas as pl
from jax.experimental.pallas import tpu as pltpu
from jax.sharding import PartitionSpec as P

TAYLOR = 6
NX, NL, NC = 4, 2, 2
NH, NY = 4, 4
PITCH = 56
GROUP = 16

root_step = 0.5
shift_cap = 1.0

VMEM = pl.BlockSpec(memory_space=pltpu.VMEM)
FAR = pl.BlockSpec(memory_space=pl.ANY)
SMEM = pl.BlockSpec(memory_space=pltpu.SMEM)
NT = (((1,), (1,)), ((), ()))


def vec_of(x, low, core):
    return ((x % NX) * NL + low) * NC + core


def places():
    return [(x, low, core) for x in range(NX) for low in range(NL) for core in range(NC)]


def send_x(array, step):
    return lax.ppermute(array, "vec", [(vec_of(*p), vec_of(p[0] + step, p[1], p[2])) for p in places()])


def swap_low(array):
    return lax.ppermute(array, "vec", [(vec_of(*p), vec_of(p[0], 1 - p[1], p[2])) for p in places()])


def swap_core(array):
    return lax.ppermute(array, "vec", [(vec_of(*p), vec_of(p[0], p[1], 1 - p[2])) for p in places()])


def send_y(array, step):
    return lax.ppermute(array, "pair", [(h * NY + y, h * NY + (y + step) % NY) for h in range(NH) for y in range(NY)])


def send_h(array, step):
    return lax.ppermute(array, "pair", [(h * NY + y, ((h + step) % NH) * NY + y) for h in range(NH) for y in range(NY)])


def everywhere(array, target):
    pairs = []
    for x, low, core in places():
        for high in range(NH):
            for y in range(NY):
                to = target(x, low, core, high, y)
                if to is not None:
                    pairs.append(
                        (vec_of(x, low, core) * NH * NY + high * NY + y, vec_of(*to[:3]) * NH * NY + to[3] * NY + to[4])
                    )
    return lax.ppermute(array, ("vec", "pair"), pairs)


def exchange(array):
    return everywhere(array, lambda x, low, core, high, y: (x, high // NC, high % NC, low * NC + core, y))


def first_target(x, low, core, high, y):
    turn = (high - core) % NH
    return (x, low, core if turn % 2 == 0 else 1 - core, core + 2 if turn in (0, 3) else core, y)


def second_target(x, low, core, high, y):
    turn = (high - core) % NH
    return None if turn % 2 == 0 else (x, low, 1 - core, core + 2 if turn == 1 else core, y)


def diagonal_mask(rows, columns):
    row = lax.broadcasted_iota(jnp.int32, (rows, columns), 0)
    column = lax.broadcasted_iota(jnp.int32, (rows, columns), 1)
    return (row % GROUP) == (column // GROUP)


def groups_of(rows):
    return [(start, min(GROUP, rows - start)) for start in range(0, rows, GROUP)]


def rotate_kernel(walkers, inverse, out_ref):
    rows = walkers.shape[0]
    out_ref[...] = jnp.zeros_like(out_ref)
    out_ref[:rows, :] = jnp.dot(
        walkers[...].astype(jnp.float32),
        inverse[...],
        precision=lax.Precision.HIGHEST,
        preferred_element_type=jnp.float32,
    ).astype(jnp.bfloat16)


def order_kernel(at, rotated, partner, trial, out_ref, trial_out):
    trial_out[...] = trial[...]
    out_ref[at[0]] = rotated[...]
    out_ref[1 - at[0]] = partner[...]


def sum_kernel(b0, b1, b2, b3, out_ref):
    out_ref[...] = (b0[...] + b2[...]) + (b1[...] + b3[...])


def write_fields(at, shifted, swapped, out_ref):
    vectors = out_ref.shape[1]
    for step in range(NX):
        for low in range(NL):
            chip = ((at[1] + step) % NX) * NL + low
            row = step * NL + low
            out_ref[pl.ds(chip * NC + at[2], 1), :] = shifted[row : row + 1, :vectors]
            out_ref[pl.ds(chip * NC + 1 - at[2], 1), :] = swapped[row : row + 1, :]


def factor_kernel(trial, block, a1, a2, a3, a4, out_ref):
    count, vectors, depth = block.shape
    product = lax.dot_general(
        block[...].reshape(count * vectors, depth), trial[...], NT, preferred_element_type=jnp.float32
    ).astype(jnp.bfloat16)
    out_ref[...] = product.reshape(count, vectors, trial.shape[0])


def bias_kernel(r0, r1, r2, r3, own, other, aux, walkers, passed, out_ref, aux_out, walkers_out, passed_out):
    aux_out[...] = aux[...]
    walkers_out[...] = walkers[...]
    rows, vectors, depth = own.shape
    parts = []
    for factor in (own, other):
        total = jnp.zeros((8 * GROUP, GROUP * vectors), jnp.float32)
        tail = None
        for start, count in groups_of(rows):
            left = jnp.concatenate(
                [r[low, start : start + GROUP, :] for r in (r0, r1, r2, r3) for low in range(NL)], axis=0
            )
            right = factor[start : start + count].reshape(count * vectors, depth)
            product = lax.dot_general(left, right, NT, preferred_element_type=jnp.float32)
            if count == GROUP:
                total = total + product
            else:
                tail = product
        pieces = [total] if tail is None else [total, tail]
        summed = jnp.zeros((8, vectors), jnp.float32)
        for piece in pieces:
            width = piece.shape[1]
            kept = jnp.where(diagonal_mask(8 * GROUP, width), piece, 0.0)
            kept = jnp.sum(kept.reshape(8, GROUP, width), axis=1)
            pick = lax.broadcasted_iota(jnp.int32, (width, vectors), 0) % vectors == lax.broadcasted_iota(
                jnp.int32, (width, vectors), 1
            )
            summed = summed + jnp.dot(
                kept, pick.astype(jnp.float32), precision=lax.Precision.HIGHEST, preferred_element_type=jnp.float32
            )
        parts.append(summed)
    out_ref[...] = jnp.concatenate(parts, axis=1)


def fields_of(bias_refs, at, aux, aux_other, gathered):
    b0, b1, b2, b3 = bias_refs
    bias = (b0[...] + b2[...]) + (b1[...] + b3[...])
    vectors = aux.shape[1]
    for step in range(NX):
        for low in range(NL):
            walker = (((at[1] + step) % NX) * NL + low) * NC + at[2]
            row = step * NL + low
            gathered[row : row + 1, :vectors] = aux[pl.ds(walker, 1), :]
            gathered[row : row + 1, vectors:] = aux_other[pl.ds(walker, 1), :]
    return gathered[...] - jnp.clip(-root_step * bias, -shift_cap, shift_cap)


def block_diagonals(coefficients, vectors):
    tall, wide = 8 * GROUP, GROUP * vectors
    spread = (
        lax.broadcasted_iota(jnp.int32, (tall, 8), 0) // GROUP == lax.broadcasted_iota(jnp.int32, (tall, 8), 1)
    ).astype(jnp.bfloat16)
    repeat = (
        lax.broadcasted_iota(jnp.int32, (vectors, wide), 1) % vectors
        == lax.broadcasted_iota(jnp.int32, (vectors, wide), 0)
    ).astype(jnp.bfloat16)
    mask = diagonal_mask(tall, wide)
    blocks = []
    for at in range(2):
        piece = coefficients[:, at * vectors : (at + 1) * vectors]
        piece = jnp.dot(spread, piece, preferred_element_type=jnp.float32).astype(jnp.bfloat16)
        piece = jnp.dot(piece, repeat, preferred_element_type=jnp.float32)
        blocks.append(jnp.where(mask, piece, 0.0).astype(jnp.bfloat16))
    return blocks


def walker_sums(blocks, own, other, base, half, store):
    vectors, columns = own.shape[1:]
    for start, count in groups_of(half):
        depth = count * vectors
        for left in range(0, columns, 512):
            right = min(columns, left + 512)
            total = jnp.dot(
                blocks[0][:, :depth],
                own[pl.ds(base + start, count), :, left:right].reshape(depth, right - left),
                preferred_element_type=jnp.float32,
            ) + jnp.dot(
                blocks[1][:, :depth],
                other[pl.ds(base + start, count), :, left:right].reshape(depth, right - left),
                preferred_element_type=jnp.float32,
            )
            total = total.astype(jnp.bfloat16)
            for walker in ALL:
                store(walker, start, count, left, right, total[walker * GROUP : walker * GROUP + count, :])


ALL = list(range(NX * NL))


def away_kernel(
    at, b0, b1, b2, b3, aux, aux_other, walkers, neighbours, own, other,
    fields_ref, swap_ref, e0, e1, e2, e3, odd_ref, two_rows, gathered,
):
    two_rows[: walkers.shape[0], :] = walkers[...]
    two_rows[walkers.shape[0] :, :] = neighbours[...]
    half = e0.shape[0]
    base = (1 - at[0]) * half
    fields = fields_of((b0, b1, b2, b3), at, aux, aux_other, gathered)
    fields_ref[...] = fields
    swap_ref[...] = fields[:, own.shape[1] :]
    blocks = block_diagonals((root_step * fields).astype(jnp.bfloat16), own.shape[1])
    outs = (e0, e1, e2, e3)

    def store(walker, start, count, left, right, value):
        if walker % NL:
            row = walker // NL * PITCH + start
            odd_ref[row : row + count, left:right] = value
        else:
            outs[walker // NL][start : start + count, left:right] = value

    walker_sums(blocks, own, other, base, half, store)


def keep_kernel(at, fields, own, other, e0, e1, e2, e3, o0, o1, o2, o3):
    half = e0.shape[0]
    base = at[0] * half
    blocks = block_diagonals((root_step * fields[...]).astype(jnp.bfloat16), own.shape[1])
    outs = (e0, o0, e1, o1, e2, o2, e3, o3)

    def store(walker, start, count, left, right, value):
        outs[walker][start : start + count, left:right] = value

    walker_sums(blocks, own, other, base, half, store)


def wide(value):
    return value.astype(jnp.float32)


def pair_sum_kernel(at, k0, k1, k2, k3, arrived, shifted, swapped, o0, o1, o2, o3, fields_ref):
    write_fields(at, shifted, swapped, fields_ref)
    half = o0.shape[0]
    for step, (keep, out) in enumerate(((k0, o0), (k1, o1), (k2, o2), (k3, o3))):
        out[...] = (wide(keep[...]) + wide(arrived[step * PITCH : step * PITCH + half, :])).astype(out.dtype)


def x_sum_kernel(p0, p1, p2, p3, out):
    out[...] = ((wide(p0[...]) + wide(p1[...])) + (wide(p2[...]) + wide(p3[...]))).astype(out.dtype)


def last_sum_kernel(at, p0, p1, p2, p3, arrived, q0, q1, q2, q3, walkers, partners, first, second, stacked):
    stacked[: walkers.shape[0], :] = walkers[...]
    stacked[walkers.shape[0] :, :] = partners[...]
    even = ((wide(p0[...]) + wide(p1[...])) + (wide(p2[...]) + wide(p3[...]))) + wide(arrived[...])
    odd = (wide(q0[...]) + wide(q1[...])) + (wide(q2[...]) + wide(q3[...]))
    turn = (at[3] - at[2] + NH) % NH
    pick = jnp.logical_or(turn == 1, turn == 2)
    first[...] = jnp.where(pick, even, odd).astype(first.dtype)
    second[...] = jnp.where(pick, odd, even).astype(second.dtype)


def choose_kernel(at, second, got, more, w1, w2, w3, block0, block1):
    active = (at[2] + at[3]) % 2 == 0

    @pl.when(active)
    def _():
        block0[...] = second[...]
        block1[...] = got[...]

    @pl.when(jnp.logical_not(active))
    def _():
        block0[...] = got[...]
        block1[...] = more[...]


def stack_kernel(low, high, out):
    half = low.shape[0]
    out[:half, :] = low[...]
    out[half:, :] = high[...]


def stack_y_kernel(b0, b1, b2, b3, pair, quad, both):
    half = b0.shape[0]
    both[: 2 * half, :] = pair[...]
    for step, ref in enumerate((b0, b1, b2, b3)):
        quad[step * half : (step + 1) * half, :] = ref[...]
        both[(step + 2) * half : (step + 3) * half, :] = ref[...]


def pass_kernel(*refs):
    pass


def taylor_kernel(at, *refs):
    pieces, walkers, (out_ref, held, operator, terms, total) = refs[:11], refs[11:15], refs[15:]
    low, core, high, y = at[0], at[2], at[3], at[4]
    half = held.shape[1]
    rows = 2 * half
    for side in range(2):
        base = high + (((high % 2) ^ core ^ side) & 1)
        if side == 0:
            mine = [(ref, 0) for ref in pieces[:6]]
        else:
            mine = [(pieces[6], 0), *((ref, 0) for ref in pieces[7:10]), (pieces[6], 2), (pieces[10], 0)]

        def take(source, index):
            ref, skip = mine[source]
            return ref[(skip + index) * half : (skip + index + 1) * half, :]

        for step in range(NY):
            row = ((base % NH) * NY + (y - step + NY) % NY) * NL
            held[row + low] = take(step, 0)
            held[row + 1 - low] = take(step, 1)
            row = (((base + 2) % NH) * NY + (y - step + NY) % NY) * NL
            held[row + low] = take(4, step)
            held[row + 1 - low] = take(5, step)
    for block in range(NH * NY * NL):
        operator[block * half : (block + 1) * half, :] = held[block]
    spread = terms.shape[2]
    for step, ref in enumerate(walkers):
        for at_row in range(NL * NC):
            total[step, at_row // NC, at_row % NC] = ref[at_row * rows : (at_row + 1) * rows, :]
    for block in range(NH * NY):
        row, column = block // NY, block % NY
        piece = total[(y - column + NY) % NY, (row // NC) ^ low, (row % NC) ^ core]
        terms[0, block * rows : (block + 1) * rows, :] = piece
    mine = low * NC + core

    def one_term(degree, accumulated):
        source = (degree - 1) % 2

        product = jnp.dot(operator[...], terms[source], preferred_element_type=jnp.float32)
        terms[1 - source] = (product / degree.astype(jnp.float32)).astype(jnp.bfloat16)

        picked = jnp.zeros((rows, spread), jnp.float32)
        for block in range(NH * NY):
            piece = wide(terms[1 - source, block * rows : (block + 1) * rows, :])
            picked = jnp.where(mine * NY + y == block, piece, picked)
        return accumulated + picked

    accumulated = lax.fori_loop(1, TAYLOR + 1, one_term, wide(walkers[0][:rows, :]))
    out_ref[...] = accumulated.astype(out_ref.dtype)


def call(kernel, outs, args, name, scratch=(), smem=0, idle=0, limit=16):
    specs = [SMEM] * smem + [VMEM] * (len(args) - smem - idle) + [FAR] * idle
    return pl.pallas_call(
        kernel,
        out_shape=outs,
        in_specs=specs,
        out_specs=[VMEM] * len(outs) if isinstance(outs, (list, tuple)) else VMEM,
        scratch_shapes=list(scratch),
        compiler_params=pltpu.CompilerParams(vmem_limit_bytes=limit * 2**20),
        name=name,
    )(*args)


def on_device(cholesky, walkers, inv_correlation, trial_orbitals, aux_fields):
    vectors, rows, orbitals = cholesky.shape
    occupied = walkers.shape[2]
    half = rows // NL
    bf16, f32 = jnp.bfloat16, jnp.float32
    shaped = jax.ShapeDtypeStruct
    me = lax.axis_index("vec")
    x, low, core = me // (NL * NC), (me // NC) % NL, me % NC
    pair = lax.axis_index("pair")
    high, y = pair // NY, pair % NY

    here = jnp.stack([low, x, core, high, y]).astype(jnp.int32)
    own = jnp.transpose(cholesky, (1, 0, 2))
    other = swap_core(own)
    rotated = call(
        rotate_kernel,
        shaped((rows + -rows % GROUP, occupied), bf16),
        (walkers[0], inv_correlation[0]),
        "rotate",
    )
    partner = swap_low(rotated)
    both, trial = call(
        order_kernel,
        [shaped((NL,) + rotated.shape, bf16), shaped((occupied, orbitals), bf16)],
        (here, rotated, partner, trial_orbitals.T),
        "order",
        smem=1,
    )
    rows_here = exchange(walkers[0])
    met = [both] + [send_x(both, -step) for step in range(1, NX)]
    factor = call(
        factor_kernel,
        shaped((rows, vectors, occupied), bf16),
        (trial, other, *met[1:], rows_here),
        "vector_factor",
        idle=4,
    )
    bias, aux_here, rows_here, other = pl.pallas_call(
        bias_kernel,
        out_shape=[
            shaped((8, 2 * vectors), f32),
            shaped(aux_fields.shape, f32),
            shaped((rows, occupied), bf16),
            shaped(other.shape, bf16),
        ],
        in_specs=[VMEM] * 8 + [FAR],
        out_specs=[VMEM] * 3 + [FAR],
        input_output_aliases={8: 3},
        compiler_params=pltpu.CompilerParams(vmem_limit_bytes=16 * 2**20),
        name="force_bias",
    )(*met, swap_core(factor), factor, aux_fields, rows_here, other)
    near = swap_core(other)
    aux_other = swap_core(aux_here)
    from_y = [bias] + [send_y(bias, step) for step in range(1, NY)]
    bias = call(sum_kernel, shaped(bias.shape, f32), tuple(from_y), "sum_y")
    from_h = [bias] + [send_h(bias, step) for step in range(1, NH)]

    piece, two, quad = [shaped((n * half, orbitals), bf16) for n in (1, 2, 4)]
    shifted, shifted_other, *even_away, odd_away, two_rows = call(
        away_kernel,
        [shaped((8, 2 * vectors), f32), shaped((8, vectors), f32)]
        + [piece] * NX
        + [shaped((NX * PITCH, orbitals), bf16), shaped((NC * rows, occupied), bf16)],
        (here, *from_h, aux_fields, aux_other, rows_here, swap_core(rows_here), near, other),
        "operator_away",
        scratch=[pltpu.VMEM((8, 2 * vectors), f32)],
        smem=1,
    )
    shifted_other = swap_core(shifted_other)
    odd_away = swap_low(odd_away)
    low_rows = swap_low(two_rows)
    even_away = [even_away[0]] + [send_x(even_away[step], step) for step in range(1, NX)]
    parts = call(
        keep_kernel,
        [piece] * (2 * NX),
        (here, shifted, near, other),
        "operator_keep",
        smem=1,
    )
    even, odd = parts[:NX], parts[NX:]
    even = [even[0]] + [send_x(even[step], step) for step in range(1, NX)]
    arrived = swap_low(call(x_sum_kernel, piece, tuple(even_away), "x_sum"))
    *odd, fields = call(
        pair_sum_kernel,
        [piece] * NX + [shaped(aux_fields.shape, f32)],
        (here, *odd, odd_away, shifted, shifted_other),
        "pair_sum",
        smem=1,
    )
    odd = [odd[0]] + [send_x(odd[step], step) for step in range(1, NX)]
    first, second, four_rows = call(
        last_sum_kernel,
        [piece] * 2 + [shaped((NL * NC * rows, occupied), bf16)],
        (here, *even, arrived, *odd, two_rows, low_rows),
        "last_sum",
        smem=1,
    )
    all_rows = [four_rows] + [send_y(four_rows, step) for step in range(1, NY)]

    got = everywhere(first, first_target)
    more = everywhere(second, second_target)
    block0, block1 = call(
        choose_kernel, [piece] * 2, (here, second, got, more, *all_rows[1:]), "choose", smem=1, idle=3
    )
    pair0 = call(stack_kernel, two, (block0, swap_low(block0)), "stack_low")
    block1s = [block1] + [send_y(block1, step) for step in range(1, NY)]
    quad1, mine = call(stack_y_kernel, [quad, shaped((6 * half, orbitals), bf16)], (*block1s, pair0), "stack_y")
    mine = swap_core(mine)
    arrived = [send_y(pair0, step) for step in range(1, NY)] + [swap_low(quad1)]
    arrived = pl.pallas_call(
        pass_kernel,
        out_shape=[two] * 3 + [quad],
        in_specs=[FAR] * 5,
        out_specs=[FAR] * 4,
        input_output_aliases={at: at for at in range(4)},
        name="gathered",
    )(*arrived, mine)
    pieces = [pair0, *arrived[:3], quad1, arrived[3], mine] + [swap_core(a) for a in arrived]
    updated = call(
        taylor_kernel,
        shaped((rows, occupied), bf16),
        (here, *pieces, *all_rows),
        "taylor",
        scratch=[
            pltpu.VMEM((NH * NY * NL, half, orbitals), bf16),
            pltpu.VMEM((orbitals, orbitals), bf16),
            pltpu.VMEM((2, orbitals, occupied), bf16),
            pltpu.VMEM((NY, NL, NC, rows, occupied), bf16),
        ],
        smem=1,
        limit=28,
    )
    return (exchange(updated)[None], fields)


def solution(mesh):
    placed = (
        P("vec", "pair", None),
        P("vec", "pair", None),
        P("vec", None, None),
        P(),
        P(None, "vec"),
    )
    return jax.shard_map(
        on_device,
        mesh=mesh,
        in_specs=placed,
        out_specs=(P("vec", "pair", None), P(None, "vec")),
        check_vma=False,
    )
```

```python
import jax
import jax.numpy as jnp
from jax import lax
from jax.experimental import pallas as pl
from jax.experimental.pallas import tpu as pltpu
from jax.sharding import PartitionSpec as P

TAYLOR = 6
NX, NL, NC = 4, 2, 2
NH, NY = 4, 4
PITCH = 56
GROUP = 16

root_step = 0.5
shift_cap = 1.0

VMEM = pl.BlockSpec(memory_space=pltpu.VMEM)
FAR = pl.BlockSpec(memory_space=pl.ANY)
NT = (((1,), (1,)), ((), ()))


def vec_of(x, low, core):
    return ((x % NX) * NL + low) * NC + core


def places():
    return [(x, low, core) for x in range(NX) for low in range(NL) for core in range(NC)]


def send_x(array, step):
    return lax.ppermute(array, "vec", [(vec_of(*p), vec_of(p[0] + step, p[1], p[2])) for p in places()])


def swap_low(array):
    return lax.ppermute(array, "vec", [(vec_of(*p), vec_of(p[0], 1 - p[1], p[2])) for p in places()])


def swap_core(array):
    return lax.ppermute(array, "vec", [(vec_of(*p), vec_of(p[0], p[1], 1 - p[2])) for p in places()])


def send_y(array, step):
    return lax.ppermute(array, "pair", [(h * NY + y, h * NY + (y + step) % NY) for h in range(NH) for y in range(NY)])


def send_h(array, step):
    return lax.ppermute(array, "pair", [(h * NY + y, ((h + step) % NH) * NY + y) for h in range(NH) for y in range(NY)])


def everywhere(array, target):
    pairs = []
    for x, low, core in places():
        for high in range(NH):
            for y in range(NY):
                to = target(x, low, core, high, y)
                if to is not None:
                    pairs.append(
                        (vec_of(x, low, core) * NH * NY + high * NY + y, vec_of(*to[:3]) * NH * NY + to[3] * NY + to[4])
                    )
    return lax.ppermute(array, ("vec", "pair"), pairs)


def exchange(array):
    return everywhere(array, lambda x, low, core, high, y: (x, high // NC, high % NC, low * NC + core, y))


def first_target(x, low, core, high, y):
    turn = (high - core) % NH
    return (x, low, core if turn % 2 == 0 else 1 - core, core + 2 if turn in (0, 3) else core, y)


def second_target(x, low, core, high, y):
    turn = (high - core) % NH
    return None if turn % 2 == 0 else (x, low, 1 - core, core + 2 if turn == 1 else core, y)


def position():
    me, pair = lax.axis_index("vec"), lax.axis_index("pair")
    return (me // NC) % NL, me // (NL * NC), me % NC, pair // NY, pair % NY


def diagonal_mask(rows, columns):
    row = lax.broadcasted_iota(jnp.int32, (rows, columns), 0)
    column = lax.broadcasted_iota(jnp.int32, (rows, columns), 1)
    return (row % GROUP) == (column // GROUP)


def groups_of(rows):
    return [(start, min(GROUP, rows - start)) for start in range(0, rows, GROUP)]


def rotate_kernel(walkers, inverse, out_ref, walkers_out):
    rows = walkers.shape[1]
    mine = walkers[...].astype(jnp.float32).T
    walkers_out[...] = mine.astype(jnp.bfloat16)
    out_ref[...] = jnp.zeros_like(out_ref)
    out_ref[:rows, :] = jnp.dot(
        mine, inverse[...], precision=lax.Precision.HIGHEST, preferred_element_type=jnp.float32
    ).astype(jnp.bfloat16)


def order_kernel(rotated, partner, trial, out_ref, trial_out):
    at = position()
    trial_out[...] = trial[...]
    out_ref[at[0]] = rotated[...]
    out_ref[1 - at[0]] = partner[...]


def sum_kernel(b0, b1, b2, b3, out_ref):
    out_ref[...] = (b0[...] + b2[...]) + (b1[...] + b3[...])


def write_fields(at, shifted, swapped, out_ref):
    vectors = out_ref.shape[1]
    for step in range(NX):
        for low in range(NL):
            chip = ((at[1] + step) % NX) * NL + low
            row = step * NL + low
            out_ref[pl.ds(chip * NC + at[2], 1), :] = shifted[row : row + 1, :vectors]
            out_ref[pl.ds(chip * NC + 1 - at[2], 1), :] = swapped[row : row + 1, :]


def factor_kernel(trial, block, a1, a2, a3, a4, out_ref):
    count, vectors, depth = block.shape
    product = lax.dot_general(
        block[...].reshape(count * vectors, depth), trial[...], NT, preferred_element_type=jnp.float32
    ).astype(jnp.bfloat16)
    out_ref[...] = product.reshape(count, vectors, trial.shape[0])


def bias_kernel(r0, r1, r2, r3, own, other, aux, walkers, passed, out_ref, aux_out, walkers_out, passed_out):
    aux_out[...] = aux[...]
    walkers_out[...] = walkers[...]
    rows, vectors, depth = own.shape
    parts = []
    for factor in (own, other):
        total = jnp.zeros((8 * GROUP, GROUP * vectors), jnp.float32)
        tail = None
        for start, count in groups_of(rows):
            left = jnp.concatenate(
                [r[low, start : start + GROUP, :] for r in (r0, r1, r2, r3) for low in range(NL)], axis=0
            )
            right = factor[start : start + count].reshape(count * vectors, depth)
            product = lax.dot_general(left, right, NT, preferred_element_type=jnp.float32)
            if count == GROUP:
                total = total + product
            else:
                tail = product
        pieces = [total] if tail is None else [total, tail]
        summed = jnp.zeros((8, vectors), jnp.float32)
        for piece in pieces:
            width = piece.shape[1]
            kept = jnp.where(diagonal_mask(8 * GROUP, width), piece, 0.0)
            kept = jnp.sum(kept.reshape(8, GROUP, width), axis=1)
            pick = lax.broadcasted_iota(jnp.int32, (width, vectors), 0) % vectors == lax.broadcasted_iota(
                jnp.int32, (width, vectors), 1
            )
            summed = summed + jnp.dot(
                kept, pick.astype(jnp.float32), precision=lax.Precision.HIGHEST, preferred_element_type=jnp.float32
            )
        parts.append(summed)
    out_ref[...] = jnp.concatenate(parts, axis=1)


def fields_of(bias_refs, at, aux, aux_other, gathered):
    b0, b1, b2, b3 = bias_refs
    bias = (b0[...] + b2[...]) + (b1[...] + b3[...])
    vectors = aux.shape[1]
    for step in range(NX):
        for low in range(NL):
            walker = (((at[1] + step) % NX) * NL + low) * NC + at[2]
            row = step * NL + low
            gathered[row : row + 1, :vectors] = aux[pl.ds(walker, 1), :]
            gathered[row : row + 1, vectors:] = aux_other[pl.ds(walker, 1), :]
    return gathered[...] - jnp.clip(-root_step * bias, -shift_cap, shift_cap)


def block_diagonals(coefficients, vectors):
    tall, wide = 8 * GROUP, GROUP * vectors
    spread = (
        lax.broadcasted_iota(jnp.int32, (tall, 8), 0) // GROUP == lax.broadcasted_iota(jnp.int32, (tall, 8), 1)
    ).astype(jnp.bfloat16)
    repeat = (
        lax.broadcasted_iota(jnp.int32, (vectors, wide), 1) % vectors
        == lax.broadcasted_iota(jnp.int32, (vectors, wide), 0)
    ).astype(jnp.bfloat16)
    mask = diagonal_mask(tall, wide)
    blocks = []
    for at in range(2):
        piece = coefficients[:, at * vectors : (at + 1) * vectors]
        piece = jnp.dot(spread, piece, preferred_element_type=jnp.float32).astype(jnp.bfloat16)
        piece = jnp.dot(piece, repeat, preferred_element_type=jnp.float32)
        blocks.append(jnp.where(mask, piece, 0.0).astype(jnp.bfloat16))
    return blocks


def walker_sums(blocks, own, other, base, half, store):
    vectors, columns = own.shape[1:]
    for start, count in groups_of(half):
        depth = count * vectors
        for left in range(0, columns, 512):
            right = min(columns, left + 512)
            total = jnp.dot(
                blocks[0][:, :depth],
                own[pl.ds(base + start, count), :, left:right].reshape(depth, right - left),
                preferred_element_type=jnp.float32,
            ) + jnp.dot(
                blocks[1][:, :depth],
                other[pl.ds(base + start, count), :, left:right].reshape(depth, right - left),
                preferred_element_type=jnp.float32,
            )
            total = total.astype(jnp.bfloat16)
            for walker in ALL:
                store(walker, start, count, left, right, total[walker * GROUP : walker * GROUP + count, :])


ALL = list(range(NX * NL))


def away_kernel(
    b0, b1, b2, b3, aux, aux_other, walkers, neighbours, own, other,
    fields_ref, swap_ref, e0, e1, e2, e3, odd_ref, two_rows, gathered,
):
    at = position()
    two_rows[: walkers.shape[0], :] = walkers[...]
    two_rows[walkers.shape[0] :, :] = neighbours[...]
    half = e0.shape[0]
    base = (1 - at[0]) * half
    fields = fields_of((b0, b1, b2, b3), at, aux, aux_other, gathered)
    fields_ref[...] = fields
    swap_ref[...] = fields[:, own.shape[1] :]
    blocks = block_diagonals((root_step * fields).astype(jnp.bfloat16), own.shape[1])
    outs = (e0, e1, e2, e3)

    def store(walker, start, count, left, right, value):
        if walker % NL:
            row = walker // NL * PITCH + start
            odd_ref[row : row + count, left:right] = value
        else:
            outs[walker // NL][start : start + count, left:right] = value

    walker_sums(blocks, own, other, base, half, store)


def keep_kernel(fields, own, other, e0, e1, e2, e3, o0, o1, o2, o3):
    half = e0.shape[0]
    base = position()[0] * half
    blocks = block_diagonals((root_step * fields[...]).astype(jnp.bfloat16), own.shape[1])
    outs = (e0, o0, e1, o1, e2, o2, e3, o3)

    def store(walker, start, count, left, right, value):
        outs[walker][start : start + count, left:right] = value

    walker_sums(blocks, own, other, base, half, store)


def wide(value):
    return value.astype(jnp.float32)


def pair_sum_kernel(k0, k1, k2, k3, arrived, shifted, swapped, o0, o1, o2, o3, fields_ref):
    write_fields(position(), shifted, swapped, fields_ref)
    half = o0.shape[0]
    for step, (keep, out) in enumerate(((k0, o0), (k1, o1), (k2, o2), (k3, o3))):
        out[...] = (wide(keep[...]) + wide(arrived[step * PITCH : step * PITCH + half, :])).astype(out.dtype)


def x_sum_kernel(p0, p1, p2, p3, out):
    out[...] = ((wide(p0[...]) + wide(p1[...])) + (wide(p2[...]) + wide(p3[...]))).astype(out.dtype)


def last_sum_kernel(p0, p1, p2, p3, arrived, q0, q1, q2, q3, walkers, partners, first, second, stacked):
    stacked[: walkers.shape[0], :] = walkers[...]
    stacked[walkers.shape[0] :, :] = partners[...]
    even = ((wide(p0[...]) + wide(p1[...])) + (wide(p2[...]) + wide(p3[...]))) + wide(arrived[...])
    odd = (wide(q0[...]) + wide(q1[...])) + (wide(q2[...]) + wide(q3[...]))
    at = position()
    turn = (at[3] - at[2] + NH) % NH
    pick = jnp.logical_or(turn == 1, turn == 2)
    first[...] = jnp.where(pick, even, odd).astype(first.dtype)
    second[...] = jnp.where(pick, odd, even).astype(second.dtype)


def choose_kernel(second, got, more, w1, w2, w3, block0, block1):
    at = position()
    active = (at[2] + at[3]) % 2 == 0

    @pl.when(active)
    def _():
        block0[...] = second[...]
        block1[...] = got[...]

    @pl.when(jnp.logical_not(active))
    def _():
        block0[...] = got[...]
        block1[...] = more[...]


def stack_kernel(low, high, out):
    half = low.shape[0]
    out[:half, :] = low[...]
    out[half:, :] = high[...]


def stack_y_kernel(b0, b1, b2, b3, pair, quad, both):
    half = b0.shape[0]
    both[: 2 * half, :] = pair[...]
    for step, ref in enumerate((b0, b1, b2, b3)):
        quad[step * half : (step + 1) * half, :] = ref[...]
        both[(step + 2) * half : (step + 3) * half, :] = ref[...]


def pass_kernel(*refs):
    pass


def taylor_kernel(*refs):
    pieces, walkers, (out_ref, held, operator, terms, total) = refs[:11], refs[11:15], refs[15:]
    low, _, core, high, y = position()
    half = held.shape[1]
    rows = 2 * half
    for side in range(2):
        base = high + (((high % 2) ^ core ^ side) & 1)
        if side == 0:
            mine = [(ref, 0) for ref in pieces[:6]]
        else:
            mine = [(pieces[6], 0), *((ref, 0) for ref in pieces[7:10]), (pieces[6], 2), (pieces[10], 0)]

        def take(source, index):
            ref, skip = mine[source]
            return ref[(skip + index) * half : (skip + index + 1) * half, :]

        for step in range(NY):
            row = ((base % NH) * NY + (y - step + NY) % NY) * NL
            held[row + low] = take(step, 0)
            held[row + 1 - low] = take(step, 1)
            row = (((base + 2) % NH) * NY + (y - step + NY) % NY) * NL
            held[row + low] = take(4, step)
            held[row + 1 - low] = take(5, step)
    for block in range(NH * NY * NL):
        operator[block * half : (block + 1) * half, :] = held[block]
    spread = terms.shape[2]
    for step, ref in enumerate(walkers):
        for at_row in range(NL * NC):
            total[step, at_row // NC, at_row % NC] = ref[at_row * rows : (at_row + 1) * rows, :]
    for block in range(NH * NY):
        row, column = block // NY, block % NY
        piece = total[(y - column + NY) % NY, (row // NC) ^ low, (row % NC) ^ core]
        terms[0, block * rows : (block + 1) * rows, :] = piece
    mine = low * NC + core

    def one_term(degree, accumulated):
        source = (degree - 1) % 2

        product = jnp.dot(operator[...], terms[source], preferred_element_type=jnp.float32)
        terms[1 - source] = (product / degree.astype(jnp.float32)).astype(jnp.bfloat16)

        picked = jnp.zeros((rows, spread), jnp.float32)
        for block in range(NH * NY):
            piece = wide(terms[1 - source, block * rows : (block + 1) * rows, :])
            picked = jnp.where(mine * NY + y == block, piece, picked)
        return accumulated + picked

    accumulated = lax.fori_loop(1, TAYLOR + 1, one_term, wide(walkers[0][:rows, :]))
    out_ref[...] = accumulated.astype(out_ref.dtype)


def call(kernel, outs, args, name, scratch=(), idle=0, limit=16):
    specs = [VMEM] * (len(args) - idle) + [FAR] * idle
    return pl.pallas_call(
        kernel,
        out_shape=outs,
        in_specs=specs,
        out_specs=[VMEM] * len(outs) if isinstance(outs, (list, tuple)) else VMEM,
        scratch_shapes=list(scratch),
        compiler_params=pltpu.CompilerParams(vmem_limit_bytes=limit * 2**20),
        name=name,
    )(*args)


def on_device(cholesky, walkers, inv_correlation, trial_orbitals, aux_fields):
    vectors, rows, orbitals = cholesky.shape
    occupied = walkers.shape[2]
    half = rows // NL
    bf16, f32 = jnp.bfloat16, jnp.float32
    shaped = jax.ShapeDtypeStruct
    own = jnp.transpose(cholesky, (1, 0, 2))
    other = swap_core(own)
    rotated, walker = call(
        rotate_kernel,
        [shaped((rows + -rows % GROUP, occupied), bf16), shaped((rows, occupied), bf16)],
        (walkers[0].T, inv_correlation[0]),
        "rotate",
    )
    partner = swap_low(rotated)
    both, trial = call(
        order_kernel,
        [shaped((NL,) + rotated.shape, bf16), shaped((occupied, orbitals), bf16)],
        (rotated, partner, trial_orbitals.T),
        "order",
    )
    rows_here = exchange(walker)
    met = [both] + [send_x(both, -step) for step in range(1, NX)]
    factor = call(
        factor_kernel,
        shaped((rows, vectors, occupied), bf16),
        (trial, other, *met[1:], rows_here),
        "vector_factor",
        idle=4,
    )
    bias, aux_here, rows_here, other = pl.pallas_call(
        bias_kernel,
        out_shape=[
            shaped((8, 2 * vectors), f32),
            shaped(aux_fields.shape, f32),
            shaped((rows, occupied), bf16),
            shaped(other.shape, bf16),
        ],
        in_specs=[VMEM] * 8 + [FAR],
        out_specs=[VMEM] * 3 + [FAR],
        input_output_aliases={8: 3},
        compiler_params=pltpu.CompilerParams(vmem_limit_bytes=16 * 2**20),
        name="force_bias",
    )(*met, swap_core(factor), factor, aux_fields, rows_here, other)
    near = swap_core(other)
    aux_other = swap_core(aux_here)
    from_y = [bias] + [send_y(bias, step) for step in range(1, NY)]
    bias = call(sum_kernel, shaped(bias.shape, f32), tuple(from_y), "sum_y")
    from_h = [bias] + [send_h(bias, step) for step in range(1, NH)]

    piece, two, quad = [shaped((n * half, orbitals), bf16) for n in (1, 2, 4)]
    shifted, shifted_other, *even_away, odd_away, two_rows = call(
        away_kernel,
        [shaped((8, 2 * vectors), f32), shaped((8, vectors), f32)]
        + [piece] * NX
        + [shaped((NX * PITCH, orbitals), bf16), shaped((NC * rows, occupied), bf16)],
        (*from_h, aux_fields, aux_other, rows_here, swap_core(rows_here), near, other),
        "operator_away",
        scratch=[pltpu.VMEM((8, 2 * vectors), f32)],
    )
    shifted_other = swap_core(shifted_other)
    odd_away = swap_low(odd_away)
    low_rows = swap_low(two_rows)
    even_away = [even_away[0]] + [send_x(even_away[step], step) for step in range(1, NX)]
    parts = call(
        keep_kernel,
        [piece] * (2 * NX),
        (shifted, near, other),
        "operator_keep",
    )
    even, odd = parts[:NX], parts[NX:]
    even = [even[0]] + [send_x(even[step], step) for step in range(1, NX)]
    arrived = swap_low(call(x_sum_kernel, piece, tuple(even_away), "x_sum"))
    *odd, fields = call(
        pair_sum_kernel,
        [piece] * NX + [shaped(aux_fields.shape, f32)],
        (*odd, odd_away, shifted, shifted_other),
        "pair_sum",
    )
    odd = [odd[0]] + [send_x(odd[step], step) for step in range(1, NX)]
    first, second, four_rows = call(
        last_sum_kernel,
        [piece] * 2 + [shaped((NL * NC * rows, occupied), bf16)],
        (*even, arrived, *odd, two_rows, low_rows),
        "last_sum",
    )
    all_rows = [four_rows] + [send_y(four_rows, step) for step in range(1, NY)]

    got = everywhere(first, first_target)
    more = everywhere(second, second_target)
    block0, block1 = call(
        choose_kernel, [piece] * 2, (second, got, more, *all_rows[1:]), "choose", idle=3
    )
    pair0 = call(stack_kernel, two, (block0, swap_low(block0)), "stack_low")
    block1s = [block1] + [send_y(block1, step) for step in range(1, NY)]
    quad1, mine = call(stack_y_kernel, [quad, shaped((6 * half, orbitals), bf16)], (*block1s, pair0), "stack_y")
    mine = swap_core(mine)
    arrived = [send_y(pair0, step) for step in range(1, NY)] + [swap_low(quad1)]
    arrived = pl.pallas_call(
        pass_kernel,
        out_shape=[two] * 3 + [quad],
        in_specs=[FAR] * 5,
        out_specs=[FAR] * 4,
        input_output_aliases={at: at for at in range(4)},
        compiler_params=pltpu.CompilerParams(vmem_limit_bytes=4 * 2**20),
        name="gathered",
    )(*arrived, mine)
    pieces = [pair0, *arrived[:3], quad1, arrived[3], mine] + [swap_core(a) for a in arrived]
    updated = call(
        taylor_kernel,
        shaped((rows, occupied), bf16),
        (*pieces, *all_rows),
        "taylor",
        scratch=[
            pltpu.VMEM((NH * NY * NL, half, orbitals), bf16),
            pltpu.VMEM((orbitals, orbitals), bf16),
            pltpu.VMEM((2, orbitals, occupied), bf16),
            pltpu.VMEM((NY, NL, NC, rows, occupied), bf16),
        ],
        limit=28,
    )
    return (exchange(updated)[None], fields)


def solution(mesh):
    placed = (
        P("vec", "pair", None),
        P("vec", "pair", None),
        P("vec", None, None),
        P(),
        P(None, "vec"),
    )
    return jax.shard_map(
        on_device,
        mesh=mesh,
        in_specs=placed,
        out_specs=(P("vec", "pair", None), P(None, "vec")),
        check_vma=False,
    )
```

```python
import jax
import jax.numpy as jnp
from jax import lax
from jax.experimental import pallas as pl
from jax.experimental.pallas import tpu as pltpu
from jax.sharding import PartitionSpec as P

TAYLOR = 6
NX, NL, NC = 4, 2, 2
NH, NY = 4, 4
PITCH = 56
GROUP = 16

root_step = 0.5
shift_cap = 1.0

VMEM = pl.BlockSpec(memory_space=pltpu.VMEM)
FAR = pl.BlockSpec(memory_space=pl.ANY)
NT = (((1,), (1,)), ((), ()))


def vec_of(x, low, core):
    return ((x % NX) * NL + low) * NC + core


def places():
    return [(x, low, core) for x in range(NX) for low in range(NL) for core in range(NC)]


def send_x(array, step):
    return lax.ppermute(array, "vec", [(vec_of(*p), vec_of(p[0] + step, p[1], p[2])) for p in places()])


def swap_low(array):
    return lax.ppermute(array, "vec", [(vec_of(*p), vec_of(p[0], 1 - p[1], p[2])) for p in places()])


def swap_core(array):
    return lax.ppermute(array, "vec", [(vec_of(*p), vec_of(p[0], p[1], 1 - p[2])) for p in places()])


def send_y(array, step):
    return lax.ppermute(array, "pair", [(h * NY + y, h * NY + (y + step) % NY) for h in range(NH) for y in range(NY)])


def flip_y(array, bit):
    return lax.ppermute(array, "pair", [(h * NY + y, h * NY + (y ^ bit)) for h in range(NH) for y in range(NY)])


def send_h(array, step):
    return lax.ppermute(array, "pair", [(h * NY + y, ((h + step) % NH) * NY + y) for h in range(NH) for y in range(NY)])


def everywhere(array, target):
    pairs = []
    for x, low, core in places():
        for high in range(NH):
            for y in range(NY):
                to = target(x, low, core, high, y)
                if to is not None:
                    pairs.append(
                        (vec_of(x, low, core) * NH * NY + high * NY + y, vec_of(*to[:3]) * NH * NY + to[3] * NY + to[4])
                    )
    return lax.ppermute(array, ("vec", "pair"), pairs)


def exchange(array):
    return everywhere(array, lambda x, low, core, high, y: (x, high // NC, high % NC, low * NC + core, y))


def first_target(x, low, core, high, y):
    turn = (high - core) % NH
    return (x, low, core if turn % 2 == 0 else 1 - core, core + 2 if turn in (0, 3) else core, y)


def second_target(x, low, core, high, y):
    turn = (high - core) % NH
    return None if turn % 2 == 0 else (x, low, 1 - core, core + 2 if turn == 1 else core, y)


def position():
    me, pair = lax.axis_index("vec"), lax.axis_index("pair")
    return (me // NC) % NL, me // (NL * NC), me % NC, pair // NY, pair % NY


def diagonal_mask(rows, columns):
    row = lax.broadcasted_iota(jnp.int32, (rows, columns), 0)
    column = lax.broadcasted_iota(jnp.int32, (rows, columns), 1)
    return (row % GROUP) == (column // GROUP)


def groups_of(rows):
    return [(start, min(GROUP, rows - start)) for start in range(0, rows, GROUP)]


def rotate_kernel(walkers, inverse, out_ref, walkers_out):
    rows = walkers.shape[1]
    mine = walkers[...].astype(jnp.float32).T
    walkers_out[...] = mine.astype(jnp.bfloat16)
    out_ref[...] = jnp.zeros_like(out_ref)
    out_ref[:rows, :] = jnp.dot(
        mine, inverse[...], precision=lax.Precision.HIGHEST, preferred_element_type=jnp.float32
    ).astype(jnp.bfloat16)


def order_kernel(rotated, partner, trial, out_ref, trial_out):
    at = position()
    trial_out[...] = trial[...]
    out_ref[at[0]] = rotated[...]
    out_ref[1 - at[0]] = partner[...]


def sum_kernel(b0, b1, b2, b3, out_ref):
    out_ref[...] = (b0[...] + b2[...]) + (b1[...] + b3[...])


def write_fields(at, shifted, swapped, out_ref):
    vectors = out_ref.shape[1]
    for step in range(NX):
        for low in range(NL):
            chip = ((at[1] + step) % NX) * NL + low
            row = step * NL + low
            out_ref[pl.ds(chip * NC + at[2], 1), :] = shifted[row : row + 1, :vectors]
            out_ref[pl.ds(chip * NC + 1 - at[2], 1), :] = swapped[row : row + 1, :]


def factor_kernel(trial, block, a1, a2, a3, a4, out_ref):
    count, vectors, depth = block.shape
    product = lax.dot_general(
        block[...].reshape(count * vectors, depth), trial[...], NT, preferred_element_type=jnp.float32
    ).astype(jnp.bfloat16)
    out_ref[...] = product.reshape(count, vectors, trial.shape[0])


def bias_kernel(r0, r1, r2, r3, own, other, aux, walkers, passed, out_ref, aux_out, walkers_out, passed_out):
    aux_out[...] = aux[...]
    walkers_out[...] = walkers[...]
    rows, vectors, depth = own.shape
    parts = []
    for factor in (own, other):
        total = jnp.zeros((8 * GROUP, GROUP * vectors), jnp.float32)
        tail = None
        for start, count in groups_of(rows):
            left = jnp.concatenate(
                [r[low, start : start + GROUP, :] for r in (r0, r1, r2, r3) for low in range(NL)], axis=0
            )
            right = factor[start : start + count].reshape(count * vectors, depth)
            product = lax.dot_general(left, right, NT, preferred_element_type=jnp.float32)
            if count == GROUP:
                total = total + product
            else:
                tail = product
        pieces = [total] if tail is None else [total, tail]
        summed = jnp.zeros((8, vectors), jnp.float32)
        for piece in pieces:
            width = piece.shape[1]
            kept = jnp.where(diagonal_mask(8 * GROUP, width), piece, 0.0)
            kept = jnp.sum(kept.reshape(8, GROUP, width), axis=1)
            pick = lax.broadcasted_iota(jnp.int32, (width, vectors), 0) % vectors == lax.broadcasted_iota(
                jnp.int32, (width, vectors), 1
            )
            summed = summed + jnp.dot(
                kept, pick.astype(jnp.float32), precision=lax.Precision.HIGHEST, preferred_element_type=jnp.float32
            )
        parts.append(summed)
    out_ref[...] = jnp.concatenate(parts, axis=1)


def fields_of(bias_refs, at, aux, aux_other, gathered):
    b0, b1, b2, b3 = bias_refs
    bias = (b0[...] + b2[...]) + (b1[...] + b3[...])
    vectors = aux.shape[1]
    for step in range(NX):
        for low in range(NL):
            walker = (((at[1] + step) % NX) * NL + low) * NC + at[2]
            row = step * NL + low
            gathered[row : row + 1, :vectors] = aux[pl.ds(walker, 1), :]
            gathered[row : row + 1, vectors:] = aux_other[pl.ds(walker, 1), :]
    return gathered[...] - jnp.clip(-root_step * bias, -shift_cap, shift_cap)


def block_diagonals(coefficients, vectors):
    tall, wide = 8 * GROUP, GROUP * vectors
    spread = (
        lax.broadcasted_iota(jnp.int32, (tall, 8), 0) // GROUP == lax.broadcasted_iota(jnp.int32, (tall, 8), 1)
    ).astype(jnp.bfloat16)
    repeat = (
        lax.broadcasted_iota(jnp.int32, (vectors, wide), 1) % vectors
        == lax.broadcasted_iota(jnp.int32, (vectors, wide), 0)
    ).astype(jnp.bfloat16)
    mask = diagonal_mask(tall, wide)
    blocks = []
    for at in range(2):
        piece = coefficients[:, at * vectors : (at + 1) * vectors]
        piece = jnp.dot(spread, piece, preferred_element_type=jnp.float32).astype(jnp.bfloat16)
        piece = jnp.dot(piece, repeat, preferred_element_type=jnp.float32)
        blocks.append(jnp.where(mask, piece, 0.0).astype(jnp.bfloat16))
    return blocks


def walker_sums(blocks, own, other, base, half, store):
    vectors, columns = own.shape[1:]
    for start, count in groups_of(half):
        depth = count * vectors
        for left in range(0, columns, 512):
            right = min(columns, left + 512)
            total = jnp.dot(
                blocks[0][:, :depth],
                own[pl.ds(base + start, count), :, left:right].reshape(depth, right - left),
                preferred_element_type=jnp.float32,
            ) + jnp.dot(
                blocks[1][:, :depth],
                other[pl.ds(base + start, count), :, left:right].reshape(depth, right - left),
                preferred_element_type=jnp.float32,
            )
            total = total.astype(jnp.bfloat16)
            for walker in ALL:
                store(walker, start, count, left, right, total[walker * GROUP : walker * GROUP + count, :])


ALL = list(range(NX * NL))


def operator_kernel(
    b0, b1, b2, b3, aux, aux_other, walkers, neighbours, own, other,
    fields_ref, swap_ref, e0, e1, e2, e3, away_ref, o0, o1, o2, o3, two_rows, gathered,
):
    at = position()
    stack(two_rows, walkers, neighbours)
    half = o0.shape[0]
    fields = fields_of((b0, b1, b2, b3), at, aux, aux_other, gathered)
    fields_ref[...] = fields
    swap_ref[...] = fields[:, own.shape[1] :]
    blocks = block_diagonals((root_step * fields).astype(jnp.bfloat16), own.shape[1])
    evens, odds = (e0, e1, e2, e3), (o0, o1, o2, o3)

    def store_away(walker, start, count, left, right, value):
        if walker % NL:
            row = walker // NL * PITCH + start
            away_ref[row : row + count, left:right] = value
        else:
            evens[walker // NL][half + start : half + start + count, left:right] = value

    def store_keep(walker, start, count, left, right, value):
        out = odds if walker % NL else evens
        out[walker // NL][start : start + count, left:right] = value

    walker_sums(blocks, own, other, (1 - at[0]) * half, half, store_away)
    walker_sums(blocks, own, other, at[0] * half, half, store_keep)


def wide(value):
    return value.astype(jnp.float32)


def pair_sum_kernel(k0, k1, k2, k3, arrived, shifted, swapped, walkers, partners, o0, o1, o2, o3, fields_ref, stacked):
    stack(stacked, walkers, partners)
    write_fields(position(), shifted, swapped, fields_ref)
    half = o0.shape[0]
    for step, (keep, out) in enumerate(((k0, o0), (k1, o1), (k2, o2), (k3, o3))):
        out[...] = (wide(keep[...]) + wide(arrived[step * PITCH : step * PITCH + half, :])).astype(out.dtype)


def stack(out, low, high):
    rows = low.shape[0]
    out[:rows, :] = low[...]
    out[rows:, :] = high[...]


def x_sum_kernel(p0, p1, p2, p3, out):
    half = out.shape[0]
    out[...] = (
        (wide(p0[half:, :]) + wide(p1[half:, :])) + (wide(p2[half:, :]) + wide(p3[half:, :]))
    ).astype(out.dtype)


def last_sum_kernel(p0, p1, p2, p3, arrived, q0, q1, q2, q3, walkers, partners, first, second, stacked):
    stack(stacked, walkers, partners)
    half = first.shape[0]
    even = (
        (wide(p0[:half, :]) + wide(p1[:half, :])) + (wide(p2[:half, :]) + wide(p3[:half, :]))
    ) + wide(arrived[...])
    odd = (wide(q0[...]) + wide(q1[...])) + (wide(q2[...]) + wide(q3[...]))
    at = position()
    turn = (at[3] - at[2] + NH) % NH
    pick = jnp.logical_or(turn == 1, turn == 2)
    first[...] = jnp.where(pick, even, odd).astype(first.dtype)
    second[...] = jnp.where(pick, odd, even).astype(second.dtype)


def choose_kernel(second, got, more, block0, block1):
    at = position()
    active = (at[2] + at[3]) % 2 == 0

    @pl.when(active)
    def _():
        block0[...] = second[...]
        block1[...] = got[...]

    @pl.when(jnp.logical_not(active))
    def _():
        block0[...] = got[...]
        block1[...] = more[...]


def stack_kernel(low, high, out):
    stack(out, low, high)


def stack_y_kernel(b0, b1, b2, b3, pair, after, quad, both):
    half = b0.shape[0]
    both[: 2 * half, :] = pair[...]
    for step, ref in enumerate((b0, b1, b2, b3)):
        quad[step * half : (step + 1) * half, :] = ref[...]
        both[(step + 2) * half : (step + 3) * half, :] = ref[...]


def pass_kernel(*refs):
    pass


def place_rows(pieces, base, held, out):
    low, _, _, _, y = position()
    half = held.shape[1]

    def take(source, index):
        ref, skip = pieces[source]
        return ref[(skip + index) * half : (skip + index + 1) * half, :]

    for step in range(NY):
        row = (((base % NH) // 2) * NY + (y - step + NY) % NY) * NL
        held[row + low] = take(step, 0)
        held[row + 1 - low] = take(step, 1)
        row = ((((base + 2) % NH) // 2) * NY + (y - step + NY) % NY) * NL
        held[row + low] = take(4, step)
        held[row + 1 - low] = take(5, step)
    for block in range(held.shape[0]):
        out[block * half : (block + 1) * half, :] = held[block]


def assemble_kernel(p0, p1, p2, p3, p4, p5, near, far, own_rows, last_rows, start, held, total):
    low, _, core, high, y = position()
    place_rows([(ref, 0) for ref in (p0, p1, p2, p3, p4, p5)], high + ((high + core) & 1), held, own_rows)
    half = held.shape[1]
    rows = 2 * half
    for part in range(NL):
        last_rows[part * half : (part + 1) * half, :] = held[(low * NY + y) * NL + part]
    for step, ref in enumerate((near, far)):
        for index in range(2 * NL * NC):
            total[step, index // (NL * NC), index % (NL * NC)] = ref[index * rows : (index + 1) * rows, :]
    for block in range(NH * NY):
        turn = y ^ (block % NY)
        index = ((block // NY // NC) ^ low) * NC + ((block // NY % NC) ^ core)
        start[block * rows : (block + 1) * rows, :] = total[turn // 2, turn % 2, index]


def taylor_kernel(own_rows, last_rows, start, mine, y1, y2, y3, quad, walkers, out_ref, held, other_rows, terms, total):
    low, _, core, high, y = position()
    base = high + ((high + core + 1) & 1)
    place_rows([(mine, 0), (y1, 0), (y2, 0), (y3, 0), (mine, 2), (quad, 0)], base, held, other_rows)
    rows = last_rows.shape[0]
    stretch = NY * rows
    block_here = (low * NC + core) * NY + y
    terms[0] = start[...]
    total[...] = wide(walkers[:rows, :])

    @pl.loop(1, TAYLOR)
    def _(degree):
        source = (degree - 1) % 2
        for side, ref in enumerate((own_rows, other_rows)):
            product = jnp.dot(ref[...], terms[source], preferred_element_type=jnp.float32)
            term = (product / degree.astype(jnp.float32)).astype(jnp.bfloat16)
            for pair in range(NH // 2):
                to = pl.multiple_of((2 * pair + (core ^ side)) * stretch, 16)
                terms[1 - source, pl.ds(to, stretch), :] = term[pair * stretch : (pair + 1) * stretch, :]
        for block in range(NH * NY):

            @pl.when(block_here == block)
            def _():
                total[...] += wide(terms[1 - source, block * rows : (block + 1) * rows, :])

    product = jnp.dot(last_rows[...], terms[(TAYLOR - 1) % 2], preferred_element_type=jnp.float32)
    out_ref[...] = (total[...] + wide((product / TAYLOR).astype(jnp.bfloat16))).astype(out_ref.dtype)


def call(kernel, outs, args, name, scratch=(), idle=0, limit=16):
    specs = [VMEM] * (len(args) - idle) + [FAR] * idle
    return pl.pallas_call(
        kernel,
        out_shape=outs,
        in_specs=specs,
        out_specs=[VMEM] * len(outs) if isinstance(outs, (list, tuple)) else VMEM,
        scratch_shapes=list(scratch),
        compiler_params=pltpu.CompilerParams(vmem_limit_bytes=limit * 2**20),
        name=name,
    )(*args)


def on_device(cholesky, walkers, inv_correlation, trial_orbitals, aux_fields):
    vectors, rows, orbitals = cholesky.shape
    occupied = walkers.shape[2]
    half = rows // NL
    bf16, f32 = jnp.bfloat16, jnp.float32
    shaped = jax.ShapeDtypeStruct
    own = jnp.transpose(cholesky, (1, 0, 2))
    other = swap_core(own)
    rotated, walker = call(
        rotate_kernel,
        [shaped((rows + -rows % GROUP, occupied), bf16), shaped((rows, occupied), bf16)],
        (walkers[0].T, inv_correlation[0]),
        "rotate",
    )
    partner = swap_low(rotated)
    both, trial = call(
        order_kernel,
        [shaped((NL,) + rotated.shape, bf16), shaped((occupied, orbitals), bf16)],
        (rotated, partner, trial_orbitals.T),
        "order",
    )
    rows_here = exchange(walker)
    met = [both] + [send_x(both, -step) for step in range(1, NX)]
    factor = call(
        factor_kernel,
        shaped((rows, vectors, occupied), bf16),
        (trial, other, *met[1:], rows_here),
        "vector_factor",
        idle=4,
    )
    bias, aux_here, rows_here, other = pl.pallas_call(
        bias_kernel,
        out_shape=[
            shaped((8, 2 * vectors), f32),
            shaped(aux_fields.shape, f32),
            shaped((rows, occupied), bf16),
            shaped(other.shape, bf16),
        ],
        in_specs=[VMEM] * 8 + [FAR],
        out_specs=[VMEM] * 3 + [FAR],
        input_output_aliases={8: 3},
        compiler_params=pltpu.CompilerParams(vmem_limit_bytes=16 * 2**20),
        name="force_bias",
    )(*met, swap_core(factor), factor, aux_fields, rows_here, other)
    near = swap_core(other)
    aux_other = swap_core(aux_here)
    from_y = [bias] + [send_y(bias, step) for step in range(1, NY)]
    bias = call(sum_kernel, shaped(bias.shape, f32), tuple(from_y), "sum_y")
    from_h = [bias] + [send_h(bias, step) for step in range(1, NH)]

    piece, two, quad = [shaped((n * half, orbitals), bf16) for n in (1, 2, 4)]
    shifted, shifted_other, *parts, two_rows = call(
        operator_kernel,
        [shaped((8, 2 * vectors), f32), shaped((8, vectors), f32)]
        + [two] * NX
        + [shaped((NX * PITCH, orbitals), bf16)]
        + [piece] * NX
        + [shaped((NC * rows, occupied), bf16)],
        (*from_h, aux_fields, aux_other, rows_here, swap_core(rows_here), near, other),
        "field_operator",
        scratch=[pltpu.VMEM((8, 2 * vectors), f32)],
    )
    even, away, odd = parts[:NX], parts[NX], parts[NX + 1 :]
    shifted_other = swap_core(shifted_other)
    away = swap_low(away)
    even = [even[0]] + [send_x(even[step], step) for step in range(1, NX)]
    low_rows = swap_low(two_rows)
    arrived = swap_low(call(x_sum_kernel, piece, tuple(even), "x_sum"))
    *odd, fields, four_rows = call(
        pair_sum_kernel,
        [piece] * NX + [shaped(aux_fields.shape, f32), shaped((NL * NC * rows, occupied), bf16)],
        (*odd, away, shifted, shifted_other, two_rows, low_rows),
        "pair_sum",
    )
    odd = [odd[0]] + [send_x(odd[step], step) for step in range(1, NX)]
    first, second, eight_rows = call(
        last_sum_kernel,
        [piece] * 2 + [shaped((2 * NL * NC * rows, occupied), bf16)],
        (*even, arrived, *odd, four_rows, flip_y(four_rows, 1)),
        "last_sum",
    )
    far_rows = flip_y(eight_rows, 2)

    got = everywhere(first, first_target)
    more = everywhere(second, second_target)
    block0, block1 = call(choose_kernel, [piece] * 2, (second, got, more), "choose")
    pair0 = call(stack_kernel, two, (block0, swap_low(block0)), "stack_low")
    block1s = [block1] + [send_y(block1, step) for step in range(1, NY)]
    quad1, mine = call(
        stack_y_kernel, [quad, shaped((6 * half, orbitals), bf16)], (*block1s, pair0, far_rows), "stack_y", idle=1
    )
    mine = swap_core(mine)
    arrived = [send_y(pair0, step) for step in range(1, NY)] + [swap_low(quad1)]
    arrived = pl.pallas_call(
        pass_kernel,
        out_shape=[two] * 3 + [quad],
        in_specs=[FAR] * 5,
        out_specs=[FAR] * 4,
        input_output_aliases={at: at for at in range(4)},
        compiler_params=pltpu.CompilerParams(vmem_limit_bytes=4 * 2**20),
        name="gathered",
    )(*arrived, mine)
    held = pltpu.VMEM((NH * NY, half, orbitals), bf16)
    own_rows, last_rows, start = call(
        assemble_kernel,
        [shaped((orbitals // 2, orbitals), bf16), two, shaped((orbitals, occupied), bf16)],
        (pair0, *arrived[:3], quad1, arrived[3], eight_rows, far_rows),
        "assemble",
        scratch=[held, pltpu.VMEM((2, 2, NL * NC, rows, occupied), bf16)],
    )
    updated = call(
        taylor_kernel,
        shaped((rows, occupied), bf16),
        (own_rows, last_rows, start, mine, *[swap_core(a) for a in arrived], eight_rows),
        "taylor",
        scratch=[
            held,
            pltpu.VMEM((orbitals // 2, orbitals), bf16),
            pltpu.VMEM((2, orbitals, occupied), bf16),
            pltpu.VMEM((rows, occupied), f32),
        ],
        limit=24,
    )
    return (exchange(updated)[None], fields)


def solution(mesh):
    placed = (
        P("vec", "pair", None),
        P("vec", "pair", None),
        P("vec", None, None),
        P(),
        P(None, "vec"),
    )
    return jax.shard_map(
        on_device,
        mesh=mesh,
        in_specs=placed,
        out_specs=(P("vec", "pair", None), P(None, "vec")),
        check_vma=False,
    )
```

```python
import jax
import jax.numpy as jnp
from jax import lax
from jax.experimental import pallas as pl
from jax.experimental.pallas import tpu as pltpu
from jax.sharding import PartitionSpec as P

TAYLOR = 6
NX, NL, NC = 4, 2, 2
NH, NY = 4, 4
PITCH = 56
GROUP = 16

root_step = 0.5
shift_cap = 1.0

VMEM = pl.BlockSpec(memory_space=pltpu.VMEM)
FAR = pl.BlockSpec(memory_space=pl.ANY)
NT = (((1,), (1,)), ((), ()))


def vec_of(x, low, core):
    return ((x % NX) * NL + low) * NC + core


def places():
    return [(x, low, core) for x in range(NX) for low in range(NL) for core in range(NC)]


def send_x(array, step):
    return lax.ppermute(array, "vec", [(vec_of(*p), vec_of(p[0] + step, p[1], p[2])) for p in places()])


def swap_low(array):
    return lax.ppermute(array, "vec", [(vec_of(*p), vec_of(p[0], 1 - p[1], p[2])) for p in places()])


def swap_core(array):
    return lax.ppermute(array, "vec", [(vec_of(*p), vec_of(p[0], p[1], 1 - p[2])) for p in places()])


def send_y(array, step):
    return lax.ppermute(array, "pair", [(h * NY + y, h * NY + (y + step) % NY) for h in range(NH) for y in range(NY)])


def flip_y(array, bit):
    return lax.ppermute(array, "pair", [(h * NY + y, h * NY + (y ^ bit)) for h in range(NH) for y in range(NY)])


def send_h(array, step):
    return lax.ppermute(array, "pair", [(h * NY + y, ((h + step) % NH) * NY + y) for h in range(NH) for y in range(NY)])


def everywhere(array, target):
    pairs = []
    for x, low, core in places():
        for high in range(NH):
            for y in range(NY):
                to = target(x, low, core, high, y)
                if to is not None:
                    pairs.append(
                        (vec_of(x, low, core) * NH * NY + high * NY + y, vec_of(*to[:3]) * NH * NY + to[3] * NY + to[4])
                    )
    return lax.ppermute(array, ("vec", "pair"), pairs)


def exchange(array):
    return everywhere(array, lambda x, low, core, high, y: (x, high // NC, high % NC, low * NC + core, y))


def first_target(x, low, core, high, y):
    turn = (high - core) % NH
    return (x, low, core if turn % 2 == 0 else 1 - core, core + 2 if turn in (0, 3) else core, y)


def second_target(x, low, core, high, y):
    turn = (high - core) % NH
    return None if turn % 2 == 0 else (x, low, 1 - core, core + 2 if turn == 1 else core, y)


def position():
    me, pair = lax.axis_index("vec"), lax.axis_index("pair")
    return (me // NC) % NL, me // (NL * NC), me % NC, pair // NY, pair % NY


def diagonal_mask(rows, columns):
    row = lax.broadcasted_iota(jnp.int32, (rows, columns), 0)
    column = lax.broadcasted_iota(jnp.int32, (rows, columns), 1)
    return (row % GROUP) == (column // GROUP)


def groups_of(rows):
    return [(start, min(GROUP, rows - start)) for start in range(0, rows, GROUP)]


def rotate_kernel(walkers, inverse, out_ref):
    rows = walkers.shape[1]
    mine = walkers[...].astype(jnp.float32).T
    out_ref[...] = jnp.zeros_like(out_ref)
    out_ref[:rows, :] = jnp.dot(
        mine, inverse[...], precision=lax.Precision.HIGHEST, preferred_element_type=jnp.float32
    ).astype(jnp.bfloat16)


def order_kernel(rotated, partner, trial, after, out_ref, trial_out):
    at = position()
    trial_out[...] = trial[...]
    out_ref[at[0]] = rotated[...]
    out_ref[1 - at[0]] = partner[...]


def sum_kernel(b0, b1, b2, b3, out_ref):
    out_ref[...] = (b0[...] + b2[...]) + (b1[...] + b3[...])


def write_fields(at, shifted, swapped, out_ref):
    vectors = out_ref.shape[1]
    for step in range(NX):
        for low in range(NL):
            chip = ((at[1] + step) % NX) * NL + low
            row = step * NL + low
            out_ref[pl.ds(chip * NC + at[2], 1), :] = shifted[row : row + 1, :vectors]
            out_ref[pl.ds(chip * NC + 1 - at[2], 1), :] = swapped[row : row + 1, :]


def factor_kernel(trial, block, a1, a2, a3, out_ref):
    count, vectors, depth = block.shape
    product = lax.dot_general(
        block[...].reshape(count * vectors, depth), trial[...], NT, preferred_element_type=jnp.float32
    ).astype(jnp.bfloat16)
    out_ref[...] = product.reshape(count, vectors, trial.shape[0])


def bias_kernel(r0, r1, r2, r3, own, other, aux, walkers, passed, out_ref, aux_out, walkers_out, passed_out):
    aux_out[...] = aux[...]
    walkers_out[...] = walkers[...].astype(jnp.float32).T.astype(walkers_out.dtype)
    rows, vectors, depth = own.shape
    parts = []
    for factor in (own, other):
        total = jnp.zeros((8 * GROUP, GROUP * vectors), jnp.float32)
        tail = None
        for start, count in groups_of(rows):
            left = jnp.concatenate(
                [r[low, start : start + GROUP, :] for r in (r0, r1, r2, r3) for low in range(NL)], axis=0
            )
            right = factor[start : start + count].reshape(count * vectors, depth)
            product = lax.dot_general(left, right, NT, preferred_element_type=jnp.float32)
            if count == GROUP:
                total = total + product
            else:
                tail = product
        pieces = [total] if tail is None else [total, tail]
        summed = jnp.zeros((8, vectors), jnp.float32)
        for piece in pieces:
            width = piece.shape[1]
            kept = jnp.where(diagonal_mask(8 * GROUP, width), piece, 0.0)
            kept = jnp.sum(kept.reshape(8, GROUP, width), axis=1)
            pick = lax.broadcasted_iota(jnp.int32, (width, vectors), 0) % vectors == lax.broadcasted_iota(
                jnp.int32, (width, vectors), 1
            )
            summed = summed + jnp.dot(
                kept, pick.astype(jnp.float32), precision=lax.Precision.HIGHEST, preferred_element_type=jnp.float32
            )
        parts.append(summed)
    out_ref[...] = jnp.concatenate(parts, axis=1)


def fields_of(bias_refs, at, aux, aux_other, gathered):
    b0, b1, b2, b3 = bias_refs
    bias = (b0[...] + b2[...]) + (b1[...] + b3[...])
    vectors = aux.shape[1]
    for step in range(NX):
        for low in range(NL):
            walker = (((at[1] + step) % NX) * NL + low) * NC + at[2]
            row = step * NL + low
            gathered[row : row + 1, :vectors] = aux[pl.ds(walker, 1), :]
            gathered[row : row + 1, vectors:] = aux_other[pl.ds(walker, 1), :]
    return gathered[...] - jnp.clip(-root_step * bias, -shift_cap, shift_cap)


def block_diagonals(coefficients, vectors):
    tall, wide = 8 * GROUP, GROUP * vectors
    spread = (
        lax.broadcasted_iota(jnp.int32, (tall, 8), 0) // GROUP == lax.broadcasted_iota(jnp.int32, (tall, 8), 1)
    ).astype(jnp.bfloat16)
    repeat = (
        lax.broadcasted_iota(jnp.int32, (vectors, wide), 1) % vectors
        == lax.broadcasted_iota(jnp.int32, (vectors, wide), 0)
    ).astype(jnp.bfloat16)
    mask = diagonal_mask(tall, wide)
    blocks = []
    for at in range(2):
        piece = coefficients[:, at * vectors : (at + 1) * vectors]
        piece = jnp.dot(spread, piece, preferred_element_type=jnp.float32).astype(jnp.bfloat16)
        piece = jnp.dot(piece, repeat, preferred_element_type=jnp.float32)
        blocks.append(jnp.where(mask, piece, 0.0).astype(jnp.bfloat16))
    return blocks


def walker_sums(blocks, own, other, base, half, store):
    vectors, columns = own.shape[1:]
    for start, count in groups_of(half):
        depth = count * vectors
        for left in range(0, columns, 512):
            right = min(columns, left + 512)
            total = jnp.dot(
                blocks[0][:, :depth],
                own[pl.ds(base + start, count), :, left:right].reshape(depth, right - left),
                preferred_element_type=jnp.float32,
            ) + jnp.dot(
                blocks[1][:, :depth],
                other[pl.ds(base + start, count), :, left:right].reshape(depth, right - left),
                preferred_element_type=jnp.float32,
            )
            total = total.astype(jnp.bfloat16)
            for walker in ALL:
                store(walker, start, count, left, right, total[walker * GROUP : walker * GROUP + count, :])


ALL = list(range(NX * NL))


def operator_kernel(
    b0, b1, b2, b3, aux, aux_other, walkers, neighbours, own, other,
    fields_ref, swap_ref, e0, e1, e2, e3, away_ref, o0, o1, o2, o3, two_rows, gathered,
):
    at = position()
    stack(two_rows, walkers, neighbours)
    half = o0.shape[0]
    fields = fields_of((b0, b1, b2, b3), at, aux, aux_other, gathered)
    fields_ref[...] = fields
    swap_ref[...] = fields[:, own.shape[1] :]
    blocks = block_diagonals((root_step * fields).astype(jnp.bfloat16), own.shape[1])
    evens, odds = (e0, e1, e2, e3), (o0, o1, o2, o3)

    def store_away(walker, start, count, left, right, value):
        if walker % NL:
            row = walker // NL * PITCH + start
            away_ref[row : row + count, left:right] = value
        else:
            evens[walker // NL][half + start : half + start + count, left:right] = value

    def store_keep(walker, start, count, left, right, value):
        out = odds if walker % NL else evens
        out[walker // NL][start : start + count, left:right] = value

    walker_sums(blocks, own, other, (1 - at[0]) * half, half, store_away)
    walker_sums(blocks, own, other, at[0] * half, half, store_keep)


def wide(value):
    return value.astype(jnp.float32)


def pair_sum_kernel(k0, k1, k2, k3, arrived, shifted, swapped, walkers, partners, o0, o1, o2, o3, fields_ref, stacked):
    stack(stacked, walkers, partners)
    write_fields(position(), shifted, swapped, fields_ref)
    half = o0.shape[0]
    for step, (keep, out) in enumerate(((k0, o0), (k1, o1), (k2, o2), (k3, o3))):
        out[...] = (wide(keep[...]) + wide(arrived[step * PITCH : step * PITCH + half, :])).astype(out.dtype)


def stack(out, low, high):
    rows = low.shape[0]
    out[:rows, :] = low[...]
    out[rows:, :] = high[...]


def x_sum_kernel(p0, p1, p2, p3, out):
    half = out.shape[0]
    out[...] = (
        (wide(p0[half:, :]) + wide(p1[half:, :])) + (wide(p2[half:, :]) + wide(p3[half:, :]))
    ).astype(out.dtype)


def last_sum_kernel(p0, p1, p2, p3, arrived, q0, q1, q2, q3, walkers, partners, first, second, stacked):
    stack(stacked, walkers, partners)
    half = first.shape[0]
    even = (
        (wide(p0[:half, :]) + wide(p1[:half, :])) + (wide(p2[:half, :]) + wide(p3[:half, :]))
    ) + wide(arrived[...])
    odd = (wide(q0[...]) + wide(q1[...])) + (wide(q2[...]) + wide(q3[...]))
    at = position()
    turn = (at[3] - at[2] + NH) % NH
    pick = jnp.logical_or(turn == 1, turn == 2)
    first[...] = jnp.where(pick, even, odd).astype(first.dtype)
    second[...] = jnp.where(pick, odd, even).astype(second.dtype)


def choose_kernel(second, got, more, block0, block1):
    at = position()
    active = (at[2] + at[3]) % 2 == 0

    @pl.when(active)
    def _():
        block0[...] = second[...]
        block1[...] = got[...]

    @pl.when(jnp.logical_not(active))
    def _():
        block0[...] = got[...]
        block1[...] = more[...]


def stack_kernel(low, high, out):
    stack(out, low, high)


def stack_y_kernel(b0, b1, b2, b3, after, quad):
    half = b0.shape[0]
    for step, ref in enumerate((b0, b1, b2, b3)):
        quad[step * half : (step + 1) * half, :] = ref[...]


def own_base():
    _, _, core, high, _ = position()
    return (high + ((high + core) & 1)) % NH


def compact(held, out, last):
    half = held.shape[1]
    y = position()[4]
    for block in range(held.shape[0]):
        out[block * half : (block + 1) * half, :] = held[block]
    for part in range(NL):
        last[part * half : (part + 1) * half, :] = held[y * NL + part]


def first_rows_kernel(p0, p1, p2, p3, near, far, out, last, start, held, total):
    low, _, core, _, y = position()
    half = held.shape[1]
    for step, ref in enumerate((p0, p1, p2, p3)):
        row = ((y - step + NY) % NY) * NL
        held[row + low] = ref[:half, :]
        held[row + 1 - low] = ref[half:, :]
    compact(held, out, last)
    rows = 2 * half
    for step, ref in enumerate((near, far)):
        for index in range(2 * NL * NC):
            total[step, index // (NL * NC), index % (NL * NC)] = ref[index * rows : (index + 1) * rows, :]
    for block in range(NH * NY):
        turn = y ^ (block % NY)
        index = ((block // NY // NC) ^ low) * NC + ((block // NY % NC) ^ core)
        start[block * rows : (block + 1) * rows, :] = total[turn // 2, turn % 2, index]


def second_rows_kernel(mine, partner, after, out, last, held):
    low, _, _, _, y = position()
    half = held.shape[1]
    for step in range(NY):
        row = ((y - step + NY) % NY) * NL
        held[row + low] = mine[step * half : (step + 1) * half, :]
        held[row + 1 - low] = partner[step * half : (step + 1) * half, :]
    compact(held, out, last)


def taylor_kernel(rows0, rows1, other0, other1, last0, last1, start, walkers, out_ref, operator, terms, total):
    low, _, core, high, y = position()
    base = own_base()
    other = (high + ((high + core + 1) & 1)) % NH
    stretch, rows = rows0.shape[0], last0.shape[0]
    for place, ref in ((base, rows0), ((base + 2) % NH, rows1), (other, other0), ((other + 2) % NH, other1)):
        operator[pl.ds(pl.multiple_of(place * stretch, 16), stretch), :] = ref[...]
    block_here = (low * NC + core) * NY + y
    terms[0] = start[...]
    total[...] = wide(walkers[:rows, :])

    @pl.loop(1, TAYLOR)
    def _(degree):
        source = (degree - 1) % 2
        product = jnp.dot(operator[...], terms[source], preferred_element_type=jnp.float32)
        terms[1 - source] = (product / degree.astype(jnp.float32)).astype(jnp.bfloat16)
        for block in range(NH * NY):

            @pl.when(block_here == block)
            def _():
                total[...] += wide(terms[1 - source, block * rows : (block + 1) * rows, :])

    last = jnp.where(base == low * NC + core, last0[...], last1[...])
    product = jnp.dot(last, terms[(TAYLOR - 1) % 2], preferred_element_type=jnp.float32)
    out_ref[...] = (total[...] + wide((product / TAYLOR).astype(jnp.bfloat16))).T.astype(out_ref.dtype)


def call(kernel, outs, args, name, scratch=(), idle=0, limit=16, flops=None):
    specs = [VMEM] * (len(args) - idle) + [FAR] * idle
    return pl.pallas_call(
        kernel,
        out_shape=outs,
        in_specs=specs,
        out_specs=[VMEM] * len(outs) if isinstance(outs, (list, tuple)) else VMEM,
        scratch_shapes=list(scratch),
        compiler_params=pltpu.CompilerParams(vmem_limit_bytes=limit * 2**20),
        cost_estimate=None if flops is None else pl.CostEstimate(flops=flops, bytes_accessed=0, transcendentals=0),
        name=name,
    )(*args)


def on_device(cholesky, walkers, inv_correlation, trial_orbitals, aux_fields):
    vectors, rows, orbitals = cholesky.shape
    occupied = walkers.shape[2]
    half = rows // NL
    bf16, f32 = jnp.bfloat16, jnp.float32
    shaped = jax.ShapeDtypeStruct
    own = jnp.transpose(cholesky, (1, 0, 2))
    other = swap_core(own)
    rows_here = exchange(walkers[0].T)
    rotated = call(
        rotate_kernel,
        shaped((rows + -rows % GROUP, occupied), bf16),
        (walkers[0].T, inv_correlation[0]),
        "rotate",
    )
    partner = swap_low(rotated)
    both, trial = call(
        order_kernel,
        [shaped((NL,) + rotated.shape, bf16), shaped((occupied, orbitals), bf16)],
        (rotated, partner, trial_orbitals.T, rows_here),
        "order",
        idle=1,
    )
    met = [both] + [send_x(both, -step) for step in range(1, NX)]
    factor = call(
        factor_kernel,
        shaped((rows, vectors, occupied), bf16),
        (trial, other, *met[1:]),
        "vector_factor",
        idle=3,
    )
    bias, aux_here, rows_here, other = pl.pallas_call(
        bias_kernel,
        out_shape=[
            shaped((8, 2 * vectors), f32),
            shaped(aux_fields.shape, f32),
            shaped((rows, occupied), bf16),
            shaped(other.shape, bf16),
        ],
        in_specs=[VMEM] * 8 + [FAR],
        out_specs=[VMEM] * 3 + [FAR],
        input_output_aliases={8: 3},
        compiler_params=pltpu.CompilerParams(vmem_limit_bytes=16 * 2**20),
        name="force_bias",
    )(*met, swap_core(factor), factor, aux_fields, rows_here, other)
    near = swap_core(other)
    aux_other = swap_core(aux_here)
    from_y = [bias] + [send_y(bias, step) for step in range(1, NY)]
    bias = call(sum_kernel, shaped(bias.shape, f32), tuple(from_y), "sum_y")
    from_h = [bias] + [send_h(bias, step) for step in range(1, NH)]

    piece, two, quad = [shaped((n * half, orbitals), bf16) for n in (1, 2, 4)]
    shifted, shifted_other, *parts, two_rows = call(
        operator_kernel,
        [shaped((8, 2 * vectors), f32), shaped((8, vectors), f32)]
        + [two] * NX
        + [shaped((NX * PITCH, orbitals), bf16)]
        + [piece] * NX
        + [shaped((NC * rows, occupied), bf16)],
        (*from_h, aux_fields, aux_other, rows_here, swap_core(rows_here), near, other),
        "field_operator",
        scratch=[pltpu.VMEM((8, 2 * vectors), f32)],
    )
    even, away, odd = parts[:NX], parts[NX], parts[NX + 1 :]
    shifted_other = swap_core(shifted_other)
    away = swap_low(away)
    even = [even[0]] + [send_x(even[step], step) for step in range(1, NX)]
    low_rows = swap_low(two_rows)
    arrived = swap_low(call(x_sum_kernel, piece, tuple(even), "x_sum"))
    *odd, fields, four_rows = call(
        pair_sum_kernel,
        [piece] * NX + [shaped(aux_fields.shape, f32), shaped((NL * NC * rows, occupied), bf16)],
        (*odd, away, shifted, shifted_other, two_rows, low_rows),
        "pair_sum",
    )
    odd = [odd[0]] + [send_x(odd[step], step) for step in range(1, NX)]
    first, second, eight_rows = call(
        last_sum_kernel,
        [piece] * 2 + [shaped((2 * NL * NC * rows, occupied), bf16)],
        (*even, arrived, *odd, four_rows, flip_y(four_rows, 1)),
        "last_sum",
    )
    far_rows = flip_y(eight_rows, 2)

    got = everywhere(first, first_target)
    more = everywhere(second, second_target)
    block0, block1 = call(choose_kernel, [piece] * 2, (second, got, more), "choose")
    pair0 = call(stack_kernel, two, (block0, swap_low(block0)), "stack_low")
    block1s = [block1] + [send_y(block1, step) for step in range(1, NY)]
    quad1 = call(stack_y_kernel, quad, (*block1s, far_rows), "stack_y", idle=1)
    stretch = shaped((NY * rows, orbitals), bf16)
    held = pltpu.VMEM((NY * NL, half, orbitals), bf16)
    rows0, last0, start = call(
        first_rows_kernel,
        [stretch, two, shaped((orbitals, occupied), bf16)],
        (pair0, *[send_y(pair0, step) for step in range(1, NY)], eight_rows, far_rows),
        "first_rows",
        scratch=[held, pltpu.VMEM((2, 2, NL * NC, rows, occupied), bf16)],
        flops=4 * 10**9,
    )
    rows1, last1 = call(
        second_rows_kernel,
        [stretch, two],
        (quad1, swap_low(quad1), rows0),
        "second_rows",
        scratch=[held],
        idle=1,
    )
    updated = call(
        taylor_kernel,
        shaped((occupied, rows), bf16),
        (rows0, rows1, swap_core(rows0), swap_core(rows1), last0, last1, start, eight_rows),
        "taylor",
        scratch=[
            pltpu.VMEM((orbitals, orbitals), bf16),
            pltpu.VMEM((2, orbitals, occupied), bf16),
            pltpu.VMEM((rows, occupied), f32),
        ],
        limit=24,
    )
    return (exchange(updated).T[None], fields)


def solution(mesh):
    placed = (
        P("vec", "pair", None),
        P("vec", "pair", None),
        P("vec", None, None),
        P(),
        P(None, "vec"),
    )
    return jax.shard_map(
        on_device,
        mesh=mesh,
        in_specs=placed,
        out_specs=(P("vec", "pair", None), P(None, "vec")),
        check_vma=False,
    )
```

```python
import jax
import jax.numpy as jnp
from jax import lax
from jax.experimental import pallas as pl
from jax.experimental.pallas import tpu as pltpu
from jax.sharding import PartitionSpec as P

TAYLOR = 6
NX, NL, NC = 4, 2, 2
NH, NY = 4, 4
PITCH = 56
GROUP = 16

root_step = 0.5
shift_cap = 1.0

VMEM = pl.BlockSpec(memory_space=pltpu.VMEM)
FAR = pl.BlockSpec(memory_space=pl.ANY)
NT = (((1,), (1,)), ((), ()))


def vec_of(x, low, core):
    return ((x % NX) * NL + low) * NC + core


def places():
    return [(x, low, core) for x in range(NX) for low in range(NL) for core in range(NC)]


def send_x(array, step):
    return lax.ppermute(array, "vec", [(vec_of(*p), vec_of(p[0] + step, p[1], p[2])) for p in places()])


def swap_low(array):
    return lax.ppermute(array, "vec", [(vec_of(*p), vec_of(p[0], 1 - p[1], p[2])) for p in places()])


def swap_core(array):
    return lax.ppermute(array, "vec", [(vec_of(*p), vec_of(p[0], p[1], 1 - p[2])) for p in places()])


def send_y(array, step):
    return lax.ppermute(array, "pair", [(h * NY + y, h * NY + (y + step) % NY) for h in range(NH) for y in range(NY)])


def flip_y(array, bit):
    return lax.ppermute(array, "pair", [(h * NY + y, h * NY + (y ^ bit)) for h in range(NH) for y in range(NY)])


def send_h(array, step):
    return lax.ppermute(array, "pair", [(h * NY + y, ((h + step) % NH) * NY + y) for h in range(NH) for y in range(NY)])


def everywhere(array, target):
    pairs = []
    for x, low, core in places():
        for high in range(NH):
            for y in range(NY):
                to = target(x, low, core, high, y)
                if to is not None:
                    pairs.append(
                        (vec_of(x, low, core) * NH * NY + high * NY + y, vec_of(*to[:3]) * NH * NY + to[3] * NY + to[4])
                    )
    return lax.ppermute(array, ("vec", "pair"), pairs)


def exchange(array):
    return everywhere(array, lambda x, low, core, high, y: (x, high // NC, high % NC, low * NC + core, y))


def first_target(x, low, core, high, y):
    turn = (high - core) % NH
    return (x, low, core if turn % 2 == 0 else 1 - core, core + 2 if turn in (0, 3) else core, y)


def second_target(x, low, core, high, y):
    turn = (high - core) % NH
    return None if turn % 2 == 0 else (x, low, 1 - core, core + 2 if turn == 1 else core, y)


def position():
    me, pair = lax.axis_index("vec"), lax.axis_index("pair")
    return (me // NC) % NL, me // (NL * NC), me % NC, pair // NY, pair % NY


def diagonal_mask(rows, columns):
    row = lax.broadcasted_iota(jnp.int32, (rows, columns), 0)
    column = lax.broadcasted_iota(jnp.int32, (rows, columns), 1)
    return (row % GROUP) == (column // GROUP)


def groups_of(rows):
    return [(start, min(GROUP, rows - start)) for start in range(0, rows, GROUP)]


def rotate_kernel(walkers, inverse, out_ref):
    rows = walkers.shape[1]
    mine = walkers[...].astype(jnp.float32).T
    out_ref[...] = jnp.zeros_like(out_ref)
    out_ref[:rows, :] = jnp.dot(
        mine, inverse[...], precision=lax.Precision.HIGHEST, preferred_element_type=jnp.float32
    ).astype(jnp.bfloat16)


def order_kernel(rotated, partner, trial, out_ref, trial_out):
    at = position()
    trial_out[...] = trial[...]
    out_ref[at[0]] = rotated[...]
    out_ref[1 - at[0]] = partner[...]


def sum_kernel(b0, b1, b2, b3, out_ref):
    out_ref[...] = (b0[...] + b2[...]) + (b1[...] + b3[...])


def write_fields(at, shifted, swapped, out_ref):
    vectors = out_ref.shape[1]
    for step in range(NX):
        for low in range(NL):
            chip = ((at[1] + step) % NX) * NL + low
            row = step * NL + low
            out_ref[pl.ds(chip * NC + at[2], 1), :] = shifted[row : row + 1, :vectors]
            out_ref[pl.ds(chip * NC + 1 - at[2], 1), :] = swapped[row : row + 1, :]


def factor_kernel(trial, block, a1, a2, a3, out_ref):
    count, vectors, depth = block.shape
    product = lax.dot_general(
        block[...].reshape(count * vectors, depth), trial[...], NT, preferred_element_type=jnp.float32
    ).astype(jnp.bfloat16)
    out_ref[...] = product.reshape(count, vectors, trial.shape[0])


def bias_kernel(r0, r1, r2, r3, own, other, aux, passed, out_ref, aux_out, passed_out):
    aux_out[...] = aux[...]
    rows, vectors, depth = own.shape
    parts = []
    for factor in (own, other):
        total = jnp.zeros((8 * GROUP, GROUP * vectors), jnp.float32)
        tail = None
        for start, count in groups_of(rows):
            left = jnp.concatenate(
                [r[low, start : start + GROUP, :] for r in (r0, r1, r2, r3) for low in range(NL)], axis=0
            )
            right = factor[start : start + count].reshape(count * vectors, depth)
            product = lax.dot_general(left, right, NT, preferred_element_type=jnp.float32)
            if count == GROUP:
                total = total + product
            else:
                tail = product
        pieces = [total] if tail is None else [total, tail]
        summed = jnp.zeros((8, vectors), jnp.float32)
        for piece in pieces:
            width = piece.shape[1]
            kept = jnp.where(diagonal_mask(8 * GROUP, width), piece, 0.0)
            kept = jnp.sum(kept.reshape(8, GROUP, width), axis=1)
            pick = lax.broadcasted_iota(jnp.int32, (width, vectors), 0) % vectors == lax.broadcasted_iota(
                jnp.int32, (width, vectors), 1
            )
            summed = summed + jnp.dot(
                kept, pick.astype(jnp.float32), precision=lax.Precision.HIGHEST, preferred_element_type=jnp.float32
            )
        parts.append(summed)
    out_ref[...] = jnp.concatenate(parts, axis=1)


def fields_of(bias_refs, at, aux, aux_other, gathered):
    b0, b1, b2, b3 = bias_refs
    bias = (b0[...] + b2[...]) + (b1[...] + b3[...])
    vectors = aux.shape[1]
    for step in range(NX):
        for low in range(NL):
            walker = (((at[1] + step) % NX) * NL + low) * NC + at[2]
            row = step * NL + low
            gathered[row : row + 1, :vectors] = aux[pl.ds(walker, 1), :]
            gathered[row : row + 1, vectors:] = aux_other[pl.ds(walker, 1), :]
    return gathered[...] - jnp.clip(-root_step * bias, -shift_cap, shift_cap)


def block_diagonals(coefficients, vectors):
    tall, wide = 8 * GROUP, GROUP * vectors
    spread = (
        lax.broadcasted_iota(jnp.int32, (tall, 8), 0) // GROUP == lax.broadcasted_iota(jnp.int32, (tall, 8), 1)
    ).astype(jnp.bfloat16)
    repeat = (
        lax.broadcasted_iota(jnp.int32, (vectors, wide), 1) % vectors
        == lax.broadcasted_iota(jnp.int32, (vectors, wide), 0)
    ).astype(jnp.bfloat16)
    mask = diagonal_mask(tall, wide)
    blocks = []
    for at in range(2):
        piece = coefficients[:, at * vectors : (at + 1) * vectors]
        piece = jnp.dot(spread, piece, preferred_element_type=jnp.float32).astype(jnp.bfloat16)
        piece = jnp.dot(piece, repeat, preferred_element_type=jnp.float32)
        blocks.append(jnp.where(mask, piece, 0.0).astype(jnp.bfloat16))
    return blocks


def walker_sums(blocks, own, other, base, half, store):
    vectors, columns = own.shape[1:]
    for start, count in groups_of(half):
        depth = count * vectors
        for left in range(0, columns, 512):
            right = min(columns, left + 512)
            total = jnp.dot(
                blocks[0][:, :depth],
                own[pl.ds(base + start, count), :, left:right].reshape(depth, right - left),
                preferred_element_type=jnp.float32,
            ) + jnp.dot(
                blocks[1][:, :depth],
                other[pl.ds(base + start, count), :, left:right].reshape(depth, right - left),
                preferred_element_type=jnp.float32,
            )
            total = total.astype(jnp.bfloat16)
            for walker in ALL:
                store(walker, start, count, left, right, total[walker * GROUP : walker * GROUP + count, :])


ALL = list(range(NX * NL))


def operator_kernel(
    b0, b1, b2, b3, aux, aux_other, walkers, own, other,
    fields_ref, swap_ref, e0, e1, e2, e3, away_ref, o0, o1, o2, o3, walkers_out, gathered,
):
    at = position()
    walkers_out[...] = walkers[...].astype(jnp.float32).T.astype(walkers_out.dtype)
    half = o0.shape[0]
    fields = fields_of((b0, b1, b2, b3), at, aux, aux_other, gathered)
    fields_ref[...] = fields
    swap_ref[...] = fields[:, own.shape[1] :]
    blocks = block_diagonals((root_step * fields).astype(jnp.bfloat16), own.shape[1])
    evens, odds = (e0, e1, e2, e3), (o0, o1, o2, o3)

    def store_away(walker, start, count, left, right, value):
        if walker % NL:
            row = walker // NL * PITCH + start
            away_ref[row : row + count, left:right] = value
        else:
            evens[walker // NL][half + start : half + start + count, left:right] = value

    def store_keep(walker, start, count, left, right, value):
        out = odds if walker % NL else evens
        out[walker // NL][start : start + count, left:right] = value

    walker_sums(blocks, own, other, (1 - at[0]) * half, half, store_away)
    walker_sums(blocks, own, other, at[0] * half, half, store_keep)


def wide(value):
    return value.astype(jnp.float32)


def pair_sum_kernel(k0, k1, k2, k3, arrived, shifted, swapped, walkers, partners, o0, o1, o2, o3, fields_ref, stacked):
    stack(stacked, walkers, partners)
    write_fields(position(), shifted, swapped, fields_ref)
    half = o0.shape[0]
    for step, (keep, out) in enumerate(((k0, o0), (k1, o1), (k2, o2), (k3, o3))):
        out[...] = (wide(keep[...]) + wide(arrived[step * PITCH : step * PITCH + half, :])).astype(out.dtype)


def stack(out, low, high):
    rows = low.shape[0]
    out[:rows, :] = low[...]
    out[rows:, :] = high[...]


def x_sum_kernel(p0, p1, p2, p3, out):
    half = out.shape[0]
    out[...] = (
        (wide(p0[half:, :]) + wide(p1[half:, :])) + (wide(p2[half:, :]) + wide(p3[half:, :]))
    ).astype(out.dtype)


def last_sum_kernel(p0, p1, p2, p3, arrived, q0, q1, q2, q3, walkers, partners, first, second, stacked):
    stack(stacked, walkers, partners)
    half = first.shape[0]
    even = (
        (wide(p0[:half, :]) + wide(p1[:half, :])) + (wide(p2[:half, :]) + wide(p3[:half, :]))
    ) + wide(arrived[...])
    odd = (wide(q0[...]) + wide(q1[...])) + (wide(q2[...]) + wide(q3[...]))
    at = position()
    turn = (at[3] - at[2] + NH) % NH
    pick = jnp.logical_or(turn == 1, turn == 2)
    first[...] = jnp.where(pick, even, odd).astype(first.dtype)
    second[...] = jnp.where(pick, odd, even).astype(second.dtype)


def choose_kernel(second, got, more, after, block0, block1):
    at = position()
    active = (at[2] + at[3]) % 2 == 0

    @pl.when(active)
    def _():
        block0[...] = second[...]
        block1[...] = got[...]

    @pl.when(jnp.logical_not(active))
    def _():
        block0[...] = got[...]
        block1[...] = more[...]


def stack_kernel(low, high, out):
    stack(out, low, high)


def stack_y_kernel(b0, b1, b2, b3, near, far, quad, stacked):
    stack(stacked, near, far)
    half = b0.shape[0]
    for step, ref in enumerate((b0, b1, b2, b3)):
        quad[step * half : (step + 1) * half, :] = ref[...]


def own_base():
    _, _, core, high, _ = position()
    return (high + ((high + core) & 1)) % NH


def compact(held, out, last):
    half = held.shape[1]
    y = position()[4]
    for block in range(held.shape[0]):
        out[block * half : (block + 1) * half, :] = held[block]
    for part in range(NL):
        last[part * half : (part + 1) * half, :] = held[y * NL + part]


def first_rows_kernel(p0, p1, p2, p3, walkers, swapped, out, last, start, held, total):
    low, _, core, _, y = position()
    half = held.shape[1]
    for step, ref in enumerate((p0, p1, p2, p3)):
        row = ((y - step + NY) % NY) * NL
        held[row + low] = ref[:half, :]
        held[row + 1 - low] = ref[half:, :]
    compact(held, out, last)
    rows = 2 * half
    for step, ref in enumerate((walkers, swapped)):
        for index in range(NY * NL):
            total[step, index] = ref[index * rows : (index + 1) * rows, :]
    for block in range(NH * NY):
        row, column = block // NY, block % NY
        piece = total[(row % NC) ^ core, (y ^ column) * NL + ((row // NC) ^ low)]
        start[block * rows : (block + 1) * rows, :] = piece


def second_rows_kernel(mine, partner, after, out, last, held):
    low, _, _, _, y = position()
    half = held.shape[1]
    for step in range(NY):
        row = ((y - step + NY) % NY) * NL
        held[row + low] = mine[step * half : (step + 1) * half, :]
        held[row + 1 - low] = partner[step * half : (step + 1) * half, :]
    compact(held, out, last)


def taylor_kernel(rows0, rows1, other0, other1, last0, last1, start, walkers, out_ref, operator, terms, total):
    low, _, core, high, y = position()
    base = own_base()
    other = (high + ((high + core + 1) & 1)) % NH
    stretch, rows = rows0.shape[0], last0.shape[0]
    for place, ref in ((base, rows0), ((base + 2) % NH, rows1), (other, other0), ((other + 2) % NH, other1)):
        operator[pl.ds(pl.multiple_of(place * stretch, 16), stretch), :] = ref[...]
    block_here = (low * NC + core) * NY + y
    terms[0] = start[...]
    total[...] = wide(walkers[:rows, :])

    @pl.loop(1, TAYLOR)
    def _(degree):
        source = (degree - 1) % 2
        product = jnp.dot(operator[...], terms[source], preferred_element_type=jnp.float32)
        terms[1 - source] = (product / degree.astype(jnp.float32)).astype(jnp.bfloat16)
        for block in range(NH * NY):

            @pl.when(block_here == block)
            def _():
                total[...] += wide(terms[1 - source, block * rows : (block + 1) * rows, :])

    last = jnp.where(base == low * NC + core, last0[...], last1[...])
    product = jnp.dot(last, terms[(TAYLOR - 1) % 2], preferred_element_type=jnp.float32)
    out_ref[...] = (total[...] + wide((product / TAYLOR).astype(jnp.bfloat16))).T.astype(out_ref.dtype)


def call(kernel, outs, args, name, scratch=(), idle=0, limit=16, flops=None):
    specs = [VMEM] * (len(args) - idle) + [FAR] * idle
    return pl.pallas_call(
        kernel,
        out_shape=outs,
        in_specs=specs,
        out_specs=[VMEM] * len(outs) if isinstance(outs, (list, tuple)) else VMEM,
        scratch_shapes=list(scratch),
        compiler_params=pltpu.CompilerParams(vmem_limit_bytes=limit * 2**20),
        cost_estimate=None if flops is None else pl.CostEstimate(flops=flops, bytes_accessed=0, transcendentals=0),
        name=name,
    )(*args)


def on_device(cholesky, walkers, inv_correlation, trial_orbitals, aux_fields):
    vectors, rows, orbitals = cholesky.shape
    occupied = walkers.shape[2]
    half = rows // NL
    bf16, f32 = jnp.bfloat16, jnp.float32
    shaped = jax.ShapeDtypeStruct
    own = jnp.transpose(cholesky, (1, 0, 2))
    other = swap_core(own)
    rows_here = exchange(walkers[0].T)
    rotated = call(
        rotate_kernel,
        shaped((rows + -rows % GROUP, occupied), bf16),
        (walkers[0].T, inv_correlation[0]),
        "rotate",
    )
    partner = swap_low(rotated)
    both, trial = call(
        order_kernel,
        [shaped((NL,) + rotated.shape, bf16), shaped((occupied, orbitals), bf16)],
        (rotated, partner, trial_orbitals.T),
        "order",
    )
    met = [both] + [send_x(both, -step) for step in range(1, NX)]
    factor = call(
        factor_kernel,
        shaped((rows, vectors, occupied), bf16),
        (trial, other, *met[1:]),
        "vector_factor",
        idle=3,
    )
    bias, aux_here, other = pl.pallas_call(
        bias_kernel,
        out_shape=[shaped((8, 2 * vectors), f32), shaped(aux_fields.shape, f32), shaped(other.shape, bf16)],
        in_specs=[VMEM] * 7 + [FAR],
        out_specs=[VMEM] * 2 + [FAR],
        input_output_aliases={7: 2},
        compiler_params=pltpu.CompilerParams(vmem_limit_bytes=16 * 2**20),
        name="force_bias",
    )(*met, swap_core(factor), factor, aux_fields, other)
    near = swap_core(other)
    aux_other = swap_core(aux_here)
    from_y = [bias] + [send_y(bias, step) for step in range(1, NY)]
    bias = call(sum_kernel, shaped(bias.shape, f32), tuple(from_y), "sum_y")
    from_h = [bias] + [send_h(bias, step) for step in range(1, NH)]

    piece, two, quad = [shaped((n * half, orbitals), bf16) for n in (1, 2, 4)]
    shifted, shifted_other, *parts, rows_here = call(
        operator_kernel,
        [shaped((8, 2 * vectors), f32), shaped((8, vectors), f32)]
        + [two] * NX
        + [shaped((NX * PITCH, orbitals), bf16)]
        + [piece] * NX
        + [shaped((rows, occupied), bf16)],
        (*from_h, aux_fields, aux_other, rows_here, near, other),
        "field_operator",
        scratch=[pltpu.VMEM((8, 2 * vectors), f32)],
    )
    even, away, odd = parts[:NX], parts[NX], parts[NX + 1 :]
    shifted_other = swap_core(shifted_other)
    away = swap_low(away)
    even = [even[0]] + [send_x(even[step], step) for step in range(1, NX)]
    low_rows = swap_low(rows_here)
    arrived = swap_low(call(x_sum_kernel, piece, tuple(even), "x_sum"))
    *odd, fields, two_rows = call(
        pair_sum_kernel,
        [piece] * NX + [shaped(aux_fields.shape, f32), shaped((NL * rows, occupied), bf16)],
        (*odd, away, shifted, shifted_other, rows_here, low_rows),
        "pair_sum",
    )
    odd = [odd[0]] + [send_x(odd[step], step) for step in range(1, NX)]
    first, second, four_rows = call(
        last_sum_kernel,
        [piece] * 2 + [shaped((2 * NL * rows, occupied), bf16)],
        (*even, arrived, *odd, two_rows, flip_y(two_rows, 1)),
        "last_sum",
    )
    far_rows = flip_y(four_rows, 2)

    got = everywhere(first, first_target)
    more = everywhere(second, second_target)
    block0, block1 = call(choose_kernel, [piece] * 2, (second, got, more, far_rows), "choose", idle=1)
    pair0 = call(stack_kernel, two, (block0, swap_low(block0)), "stack_low")
    block1s = [block1] + [send_y(block1, step) for step in range(1, NY)]
    quad1, eight_rows = call(
        stack_y_kernel,
        [quad, shaped((4 * NL * rows, occupied), bf16)],
        (*block1s, four_rows, far_rows),
        "stack_y",
    )
    stretch = shaped((NY * rows, orbitals), bf16)
    held = pltpu.VMEM((NY * NL, half, orbitals), bf16)
    rows0, last0, start = call(
        first_rows_kernel,
        [stretch, two, shaped((orbitals, occupied), bf16)],
        (pair0, *[send_y(pair0, step) for step in range(1, NY)], eight_rows, swap_core(eight_rows)),
        "first_rows",
        scratch=[held, pltpu.VMEM((NC, NY * NL, rows, occupied), bf16)],
        flops=4 * 10**9,
    )
    rows1, last1 = call(
        second_rows_kernel,
        [stretch, two],
        (quad1, swap_low(quad1), rows0),
        "second_rows",
        scratch=[held],
        idle=1,
    )
    updated = call(
        taylor_kernel,
        shaped((occupied, rows), bf16),
        (rows0, rows1, swap_core(rows0), swap_core(rows1), last0, last1, start, eight_rows),
        "taylor",
        scratch=[
            pltpu.VMEM((orbitals, orbitals), bf16),
            pltpu.VMEM((2, orbitals, occupied), bf16),
            pltpu.VMEM((rows, occupied), f32),
        ],
        limit=24,
    )
    return (exchange(updated).T[None], fields)


def solution(mesh):
    placed = (
        P("vec", "pair", None),
        P("vec", "pair", None),
        P("vec", None, None),
        P(),
        P(None, "vec"),
    )
    return jax.shard_map(
        on_device,
        mesh=mesh,
        in_specs=placed,
        out_specs=(P("vec", "pair", None), P(None, "vec")),
        check_vma=False,
    )
```

```python
import jax
import jax.numpy as jnp
from jax import lax
from jax.experimental import pallas as pl
from jax.experimental.pallas import tpu as pltpu
from jax.sharding import PartitionSpec as P

TAYLOR = 6
NX, NL, NC = 4, 2, 2
NH, NY = 4, 4
PITCH = 56
GROUP = 16

root_step = 0.5
shift_cap = 1.0

VMEM = pl.BlockSpec(memory_space=pltpu.VMEM)
FAR = pl.BlockSpec(memory_space=pl.ANY)
NT = (((1,), (1,)), ((), ()))


def vec_of(x, low, core):
    return ((x % NX) * NL + low) * NC + core


def places():
    return [(x, low, core) for x in range(NX) for low in range(NL) for core in range(NC)]


def send_x(array, step):
    return lax.ppermute(array, "vec", [(vec_of(*p), vec_of(p[0] + step, p[1], p[2])) for p in places()])


def swap_low(array):
    return lax.ppermute(array, "vec", [(vec_of(*p), vec_of(p[0], 1 - p[1], p[2])) for p in places()])


def swap_core(array):
    return lax.ppermute(array, "vec", [(vec_of(*p), vec_of(p[0], p[1], 1 - p[2])) for p in places()])


def send_y(array, step):
    return lax.ppermute(array, "pair", [(h * NY + y, h * NY + (y + step) % NY) for h in range(NH) for y in range(NY)])


def flip_y(array, bit):
    return lax.ppermute(array, "pair", [(h * NY + y, h * NY + (y ^ bit)) for h in range(NH) for y in range(NY)])


def send_h(array, step):
    return lax.ppermute(array, "pair", [(h * NY + y, ((h + step) % NH) * NY + y) for h in range(NH) for y in range(NY)])


def everywhere(array, target):
    pairs = []
    for x, low, core in places():
        for high in range(NH):
            for y in range(NY):
                to = target(x, low, core, high, y)
                if to is not None:
                    pairs.append(
                        (vec_of(x, low, core) * NH * NY + high * NY + y, vec_of(*to[:3]) * NH * NY + to[3] * NY + to[4])
                    )
    return lax.ppermute(array, ("vec", "pair"), pairs)


def exchange(array):
    return everywhere(array, lambda x, low, core, high, y: (x, high // NC, high % NC, low * NC + core, y))


def first_target(x, low, core, high, y):
    turn = (high - core) % NH
    return (x, low, core if turn % 2 == 0 else 1 - core, core + 2 if turn in (0, 3) else core, y)


def second_target(x, low, core, high, y):
    turn = (high - core) % NH
    return None if turn % 2 == 0 else (x, low, 1 - core, core + 2 if turn == 1 else core, y)


def position():
    me, pair = lax.axis_index("vec"), lax.axis_index("pair")
    return (me // NC) % NL, me // (NL * NC), me % NC, pair // NY, pair % NY


def diagonal_mask(rows, columns):
    row = lax.broadcasted_iota(jnp.int32, (rows, columns), 0)
    column = lax.broadcasted_iota(jnp.int32, (rows, columns), 1)
    return (row % GROUP) == (column // GROUP)


def groups_of(rows):
    return [(start, min(GROUP, rows - start)) for start in range(0, rows, GROUP)]


def rotate_kernel(walkers, inverse, out_ref):
    rows = walkers.shape[1]
    mine = walkers[...].astype(jnp.float32).T
    out_ref[...] = jnp.zeros_like(out_ref)
    out_ref[:rows, :] = jnp.dot(
        mine, inverse[...], precision=lax.Precision.HIGHEST, preferred_element_type=jnp.float32
    ).astype(jnp.bfloat16)


def order_kernel(rotated, partner, trial, out_ref, trial_out):
    at = position()
    trial_out[...] = trial[...]
    out_ref[at[0]] = rotated[...]
    out_ref[1 - at[0]] = partner[...]


def sum_kernel(b0, b1, b2, b3, out_ref):
    out_ref[...] = (b0[...] + b2[...]) + (b1[...] + b3[...])


def write_fields(at, shifted, swapped, out_ref):
    vectors = out_ref.shape[1]
    for step in range(NX):
        for low in range(NL):
            chip = ((at[1] + step) % NX) * NL + low
            row = step * NL + low
            out_ref[pl.ds(chip * NC + at[2], 1), :] = shifted[row : row + 1, :vectors]
            out_ref[pl.ds(chip * NC + 1 - at[2], 1), :] = swapped[row : row + 1, :]


def factor_kernel(trial, block, a1, a2, a3, out_ref):
    count, vectors, depth = block.shape
    product = lax.dot_general(
        block[...].reshape(count * vectors, depth), trial[...], NT, preferred_element_type=jnp.float32
    ).astype(jnp.bfloat16)
    out_ref[...] = product.reshape(count, vectors, trial.shape[0])


def bias_kernel(r0, r1, r2, r3, own, other, aux, passed, out_ref, aux_out, passed_out):
    aux_out[...] = aux[...]
    rows, vectors, depth = own.shape
    parts = []
    for factor in (own, other):
        total = jnp.zeros((8 * GROUP, GROUP * vectors), jnp.float32)
        tail = None
        for start, count in groups_of(rows):
            left = jnp.concatenate(
                [r[low, start : start + GROUP, :] for r in (r0, r1, r2, r3) for low in range(NL)], axis=0
            )
            right = factor[start : start + count].reshape(count * vectors, depth)
            product = lax.dot_general(left, right, NT, preferred_element_type=jnp.float32)
            if count == GROUP:
                total = total + product
            else:
                tail = product
        pieces = [total] if tail is None else [total, tail]
        summed = jnp.zeros((8, vectors), jnp.float32)
        for piece in pieces:
            width = piece.shape[1]
            kept = jnp.where(diagonal_mask(8 * GROUP, width), piece, 0.0)
            kept = jnp.sum(kept.reshape(8, GROUP, width), axis=1)
            pick = lax.broadcasted_iota(jnp.int32, (width, vectors), 0) % vectors == lax.broadcasted_iota(
                jnp.int32, (width, vectors), 1
            )
            summed = summed + jnp.dot(
                kept, pick.astype(jnp.float32), precision=lax.Precision.HIGHEST, preferred_element_type=jnp.float32
            )
        parts.append(summed)
    out_ref[...] = jnp.concatenate(parts, axis=1)


def fields_of(bias_refs, at, aux, aux_other, gathered):
    b0, b1, b2, b3 = bias_refs
    bias = (b0[...] + b2[...]) + (b1[...] + b3[...])
    vectors = aux.shape[1]
    for step in range(NX):
        for low in range(NL):
            walker = (((at[1] + step) % NX) * NL + low) * NC + at[2]
            row = step * NL + low
            gathered[row : row + 1, :vectors] = aux[pl.ds(walker, 1), :]
            gathered[row : row + 1, vectors:] = aux_other[pl.ds(walker, 1), :]
    return gathered[...] - jnp.clip(-root_step * bias, -shift_cap, shift_cap)


def block_diagonals(coefficients, vectors):
    tall, wide = 8 * GROUP, GROUP * vectors
    spread = (
        lax.broadcasted_iota(jnp.int32, (tall, 8), 0) // GROUP == lax.broadcasted_iota(jnp.int32, (tall, 8), 1)
    ).astype(jnp.bfloat16)
    repeat = (
        lax.broadcasted_iota(jnp.int32, (vectors, wide), 1) % vectors
        == lax.broadcasted_iota(jnp.int32, (vectors, wide), 0)
    ).astype(jnp.bfloat16)
    mask = diagonal_mask(tall, wide)
    blocks = []
    for at in range(2):
        piece = coefficients[:, at * vectors : (at + 1) * vectors]
        piece = jnp.dot(spread, piece, preferred_element_type=jnp.float32).astype(jnp.bfloat16)
        piece = jnp.dot(piece, repeat, preferred_element_type=jnp.float32)
        blocks.append(jnp.where(mask, piece, 0.0).astype(jnp.bfloat16))
    return blocks


def walker_sums(blocks, own, other, base, half, store):
    vectors, columns = own.shape[1:]
    for start, count in groups_of(half):
        depth = count * vectors
        for left in range(0, columns, 512):
            right = min(columns, left + 512)
            total = jnp.dot(
                blocks[0][:, :depth],
                own[pl.ds(base + start, count), :, left:right].reshape(depth, right - left),
                preferred_element_type=jnp.float32,
            ) + jnp.dot(
                blocks[1][:, :depth],
                other[pl.ds(base + start, count), :, left:right].reshape(depth, right - left),
                preferred_element_type=jnp.float32,
            )
            total = total.astype(jnp.bfloat16)
            for walker in ALL:
                store(walker, start, count, left, right, total[walker * GROUP : walker * GROUP + count, :])


ALL = list(range(NX * NL))


def operator_kernel(
    b0, b1, b2, b3, aux, aux_other, walkers, own, other,
    fields_ref, swap_ref, e0, e1, e2, e3, away_ref, o0, o1, o2, o3, walkers_out, gathered,
):
    at = position()
    walkers_out[...] = walkers[...].astype(jnp.float32).T.astype(walkers_out.dtype)
    half = o0.shape[0]
    fields = fields_of((b0, b1, b2, b3), at, aux, aux_other, gathered)
    fields_ref[...] = fields
    swap_ref[...] = fields[:, own.shape[1] :]
    blocks = block_diagonals((root_step * fields).astype(jnp.bfloat16), own.shape[1])
    evens, odds = (e0, e1, e2, e3), (o0, o1, o2, o3)

    def store_away(walker, start, count, left, right, value):
        if walker % NL:
            row = walker // NL * PITCH + start
            away_ref[row : row + count, left:right] = value
        else:
            evens[walker // NL][half + start : half + start + count, left:right] = value

    def store_keep(walker, start, count, left, right, value):
        out = odds if walker % NL else evens
        out[walker // NL][start : start + count, left:right] = value

    walker_sums(blocks, own, other, (1 - at[0]) * half, half, store_away)
    walker_sums(blocks, own, other, at[0] * half, half, store_keep)


def wide(value):
    return value.astype(jnp.float32)


def pair_sum_kernel(k0, k1, k2, k3, arrived, shifted, swapped, walkers, partners, o0, o1, o2, o3, fields_ref, stacked):
    stack(stacked, walkers, partners)
    write_fields(position(), shifted, swapped, fields_ref)
    half = o0.shape[0]
    for step, (keep, out) in enumerate(((k0, o0), (k1, o1), (k2, o2), (k3, o3))):
        out[...] = (wide(keep[...]) + wide(arrived[step * PITCH : step * PITCH + half, :])).astype(out.dtype)


def stack(out, low, high):
    rows = low.shape[0]
    out[:rows, :] = low[...]
    out[rows:, :] = high[...]


def x_sum_kernel(p0, p1, p2, p3, out):
    half = out.shape[0]
    out[...] = (
        (wide(p0[half:, :]) + wide(p1[half:, :])) + (wide(p2[half:, :]) + wide(p3[half:, :]))
    ).astype(out.dtype)


def last_sum_kernel(p0, p1, p2, p3, arrived, q0, q1, q2, q3, walkers, partners, first, second, stacked):
    stack(stacked, walkers, partners)
    half = first.shape[0]
    even = (
        (wide(p0[:half, :]) + wide(p1[:half, :])) + (wide(p2[:half, :]) + wide(p3[:half, :]))
    ) + wide(arrived[...])
    odd = (wide(q0[...]) + wide(q1[...])) + (wide(q2[...]) + wide(q3[...]))
    at = position()
    turn = (at[3] - at[2] + NH) % NH
    pick = jnp.logical_or(turn == 1, turn == 2)
    first[...] = jnp.where(pick, even, odd).astype(first.dtype)
    second[...] = jnp.where(pick, odd, even).astype(second.dtype)


def choose_kernel(second, got, more, after, block0, block1, blocks):
    at = position()
    active = (at[2] + at[3]) % 2 == 0

    @pl.when(active)
    def _():
        block0[...] = second[...]
        block1[...] = got[...]
        stack(blocks, second, got)

    @pl.when(jnp.logical_not(active))
    def _():
        block0[...] = got[...]
        block1[...] = more[...]
        stack(blocks, got, more)


def stack_low_kernel(block, partners, out):
    stack(out, block[...], partners[: block.shape[0], :])


def stack_y_kernel(b1, b2, b3, near, far, three, stacked):
    stack(stacked, near, far)
    half = b1.shape[0]
    for step, ref in enumerate((b1, b2, b3)):
        three[step * half : (step + 1) * half, :] = ref[...]


def own_base():
    _, _, core, high, _ = position()
    return (high + ((high + core) & 1)) % NH


def compact(held, out, last):
    half = held.shape[1]
    y = position()[4]
    for block in range(held.shape[0]):
        out[block * half : (block + 1) * half, :] = held[block]
    for part in range(NL):
        last[part * half : (part + 1) * half, :] = held[y * NL + part]


def first_rows_kernel(p0, p1, p2, p3, walkers, out, last, walkers_out, held):
    low, _, _, _, y = position()
    walkers_out[...] = walkers[...]
    half = held.shape[1]
    for step, ref in enumerate((p0, p1, p2, p3)):
        row = ((y - step + NY) % NY) * NL
        held[row + low] = ref[:half, :]
        held[row + 1 - low] = ref[half:, :]
    compact(held, out, last)


def second_rows_kernel(block, three, low_blocks, low_three, walkers, swapped, out, last, start, held, total):
    low, _, core, _, y = position()
    half = held.shape[1]
    for step in range(NY):
        row = ((y - step + NY) % NY) * NL
        if step == 0:
            held[row + low] = block[...]
            held[row + 1 - low] = low_blocks[half:, :]
        else:
            place = slice((step - 1) * half, step * half)
            held[row + low] = three[place, :]
            held[row + 1 - low] = low_three[place, :]
    compact(held, out, last)
    rows = 2 * half
    for step, ref in enumerate((walkers, swapped)):
        for index in range(NY * NL):
            total[step, index] = ref[index * rows : (index + 1) * rows, :]
    for at in range(NH * NY):
        row, column = at // NY, at % NY
        piece = total[(row % NC) ^ core, (y ^ column) * NL + ((row // NC) ^ low)]
        start[at * rows : (at + 1) * rows, :] = piece


def taylor_kernel(rows0, rows1, other0, other1, last0, last1, start, walkers, out_ref, operator, terms, total):
    low, _, core, high, y = position()
    base = own_base()
    other = (high + ((high + core + 1) & 1)) % NH
    stretch, rows = rows0.shape[0], last0.shape[0]
    for place, ref in ((base, rows0), ((base + 2) % NH, rows1), (other, other0), ((other + 2) % NH, other1)):
        operator[pl.ds(pl.multiple_of(place * stretch, 16), stretch), :] = ref[...]
    block_here = (low * NC + core) * NY + y
    terms[0] = start[...]
    total[...] = wide(walkers[:rows, :])

    @pl.loop(1, TAYLOR)
    def _(degree):
        source = (degree - 1) % 2
        product = jnp.dot(operator[...], terms[source], preferred_element_type=jnp.float32)
        terms[1 - source] = (product / degree.astype(jnp.float32)).astype(jnp.bfloat16)
        for block in range(NH * NY):

            @pl.when(block_here == block)
            def _():
                total[...] += wide(terms[1 - source, block * rows : (block + 1) * rows, :])

    last = jnp.where(base == low * NC + core, last0[...], last1[...])
    product = jnp.dot(last, terms[(TAYLOR - 1) % 2], preferred_element_type=jnp.float32)
    out_ref[...] = (total[...] + wide((product / TAYLOR).astype(jnp.bfloat16))).T.astype(out_ref.dtype)


def call(kernel, outs, args, name, scratch=(), idle=0, limit=16, flops=None):
    specs = [VMEM] * (len(args) - idle) + [FAR] * idle
    return pl.pallas_call(
        kernel,
        out_shape=outs,
        in_specs=specs,
        out_specs=[VMEM] * len(outs) if isinstance(outs, (list, tuple)) else VMEM,
        scratch_shapes=list(scratch),
        compiler_params=pltpu.CompilerParams(vmem_limit_bytes=limit * 2**20),
        cost_estimate=None if flops is None else pl.CostEstimate(flops=flops, bytes_accessed=0, transcendentals=0),
        name=name,
    )(*args)


def on_device(cholesky, walkers, inv_correlation, trial_orbitals, aux_fields):
    vectors, rows, orbitals = cholesky.shape
    occupied = walkers.shape[2]
    half = rows // NL
    bf16, f32 = jnp.bfloat16, jnp.float32
    shaped = jax.ShapeDtypeStruct
    own = jnp.transpose(cholesky, (1, 0, 2))
    other = swap_core(own)
    rows_here = exchange(walkers[0].T)
    rotated = call(
        rotate_kernel,
        shaped((rows + -rows % GROUP, occupied), bf16),
        (walkers[0].T, inv_correlation[0]),
        "rotate",
    )
    partner = swap_low(rotated)
    both, trial = call(
        order_kernel,
        [shaped((NL,) + rotated.shape, bf16), shaped((occupied, orbitals), bf16)],
        (rotated, partner, trial_orbitals.T),
        "order",
    )
    met = [both] + [send_x(both, -step) for step in range(1, NX)]
    factor = call(
        factor_kernel,
        shaped((rows, vectors, occupied), bf16),
        (trial, other, *met[1:]),
        "vector_factor",
        idle=3,
    )
    bias, aux_here, other = pl.pallas_call(
        bias_kernel,
        out_shape=[shaped((8, 2 * vectors), f32), shaped(aux_fields.shape, f32), shaped(other.shape, bf16)],
        in_specs=[VMEM] * 7 + [FAR],
        out_specs=[VMEM] * 2 + [FAR],
        input_output_aliases={7: 2},
        compiler_params=pltpu.CompilerParams(vmem_limit_bytes=16 * 2**20),
        name="force_bias",
    )(*met, swap_core(factor), factor, aux_fields, other)
    near = swap_core(other)
    aux_other = swap_core(aux_here)
    from_y = [bias] + [send_y(bias, step) for step in range(1, NY)]
    bias = call(sum_kernel, shaped(bias.shape, f32), tuple(from_y), "sum_y")
    from_h = [bias] + [send_h(bias, step) for step in range(1, NH)]

    piece, two, quad = [shaped((n * half, orbitals), bf16) for n in (1, 2, 4)]
    shifted, shifted_other, *parts, rows_here = call(
        operator_kernel,
        [shaped((8, 2 * vectors), f32), shaped((8, vectors), f32)]
        + [two] * NX
        + [shaped((NX * PITCH, orbitals), bf16)]
        + [piece] * NX
        + [shaped((rows, occupied), bf16)],
        (*from_h, aux_fields, aux_other, rows_here, near, other),
        "field_operator",
        scratch=[pltpu.VMEM((8, 2 * vectors), f32)],
    )
    even, away, odd = parts[:NX], parts[NX], parts[NX + 1 :]
    shifted_other = swap_core(shifted_other)
    away = swap_low(away)
    even = [even[0]] + [send_x(even[step], step) for step in range(1, NX)]
    low_rows = swap_low(rows_here)
    arrived = swap_low(call(x_sum_kernel, piece, tuple(even), "x_sum"))
    *odd, fields, two_rows = call(
        pair_sum_kernel,
        [piece] * NX + [shaped(aux_fields.shape, f32), shaped((NL * rows, occupied), bf16)],
        (*odd, away, shifted, shifted_other, rows_here, low_rows),
        "pair_sum",
    )
    odd = [odd[0]] + [send_x(odd[step], step) for step in range(1, NX)]
    first, second, four_rows = call(
        last_sum_kernel,
        [piece] * 2 + [shaped((2 * NL * rows, occupied), bf16)],
        (*even, arrived, *odd, two_rows, flip_y(two_rows, 1)),
        "last_sum",
    )
    far_rows = flip_y(four_rows, 2)

    got = everywhere(first, first_target)
    more = everywhere(second, second_target)
    block0, block1, blocks = call(
        choose_kernel, [piece] * 2 + [two], (second, got, more, far_rows), "choose", idle=1
    )
    low_blocks = swap_low(blocks)
    pair0 = call(stack_low_kernel, two, (block0, low_blocks), "stack_low")
    three, eight_rows = call(
        stack_y_kernel,
        [shaped((3 * half, orbitals), bf16), shaped((4 * NL * rows, occupied), bf16)],
        (*[send_y(block1, step) for step in range(1, NY)], four_rows, far_rows),
        "stack_y",
    )
    stretch = shaped((NY * rows, orbitals), bf16)
    held = pltpu.VMEM((NY * NL, half, orbitals), bf16)
    rows0, last0, eight_rows = call(
        first_rows_kernel,
        [stretch, two, shaped(eight_rows.shape, bf16)],
        (pair0, *[send_y(pair0, step) for step in range(1, NY)], eight_rows),
        "first_rows",
        scratch=[held],
        flops=None,
    )
    rows1, last1, start = call(
        second_rows_kernel,
        [stretch, two, shaped((orbitals, occupied), bf16)],
        (block1, three, low_blocks, swap_low(three), eight_rows, swap_core(eight_rows)),
        "second_rows",
        scratch=[held, pltpu.VMEM((NC, NY * NL, rows, occupied), bf16)],
    )
    updated = call(
        taylor_kernel,
        shaped((occupied, rows), bf16),
        (rows0, rows1, swap_core(rows0), swap_core(rows1), last0, last1, start, eight_rows),
        "taylor",
        scratch=[
            pltpu.VMEM((orbitals, orbitals), bf16),
            pltpu.VMEM((2, orbitals, occupied), bf16),
            pltpu.VMEM((rows, occupied), f32),
        ],
        limit=24,
    )
    return (exchange(updated).T[None], fields)


def solution(mesh):
    placed = (
        P("vec", "pair", None),
        P("vec", "pair", None),
        P("vec", None, None),
        P(),
        P(None, "vec"),
    )
    return jax.shard_map(
        on_device,
        mesh=mesh,
        in_specs=placed,
        out_specs=(P("vec", "pair", None), P(None, "vec")),
        check_vma=False,
    )
```

```python
import jax
import jax.numpy as jnp
from jax import lax
from jax.experimental import pallas as pl
from jax.experimental.pallas import tpu as pltpu
from jax.sharding import PartitionSpec as P

TAYLOR = 6
NX, NL, NC = 4, 2, 2
NH, NY = 4, 4
PITCH = 56
GROUP = 16

root_step = 0.5
shift_cap = 1.0

VMEM = pl.BlockSpec(memory_space=pltpu.VMEM)
FAR = pl.BlockSpec(memory_space=pl.ANY)
NT = (((1,), (1,)), ((), ()))


def vec_of(x, low, core):
    return ((x % NX) * NL + low) * NC + core


def places():
    return [(x, low, core) for x in range(NX) for low in range(NL) for core in range(NC)]


def send_x(array, step):
    return lax.ppermute(array, "vec", [(vec_of(*p), vec_of(p[0] + step, p[1], p[2])) for p in places()])


def swap_low(array):
    return lax.ppermute(array, "vec", [(vec_of(*p), vec_of(p[0], 1 - p[1], p[2])) for p in places()])


def swap_core(array):
    return lax.ppermute(array, "vec", [(vec_of(*p), vec_of(p[0], p[1], 1 - p[2])) for p in places()])


def send_y(array, step):
    return lax.ppermute(array, "pair", [(h * NY + y, h * NY + (y + step) % NY) for h in range(NH) for y in range(NY)])


def flip_y(array, bit):
    return lax.ppermute(array, "pair", [(h * NY + y, h * NY + (y ^ bit)) for h in range(NH) for y in range(NY)])


def send_h(array, step):
    return lax.ppermute(array, "pair", [(h * NY + y, ((h + step) % NH) * NY + y) for h in range(NH) for y in range(NY)])


def everywhere(array, target):
    pairs = []
    for x, low, core in places():
        for high in range(NH):
            for y in range(NY):
                to = target(x, low, core, high, y)
                if to is not None:
                    pairs.append(
                        (vec_of(x, low, core) * NH * NY + high * NY + y, vec_of(*to[:3]) * NH * NY + to[3] * NY + to[4])
                    )
    return lax.ppermute(array, ("vec", "pair"), pairs)


def exchange(array):
    return everywhere(array, lambda x, low, core, high, y: (x, high // NC, high % NC, low * NC + core, y))


def first_target(x, low, core, high, y):
    turn = (high - core) % NH
    return (x, low, core if turn % 2 == 0 else 1 - core, core + 2 if turn in (0, 3) else core, y)


def second_target(x, low, core, high, y):
    turn = (high - core) % NH
    return None if turn % 2 == 0 else (x, low, 1 - core, core + 2 if turn == 1 else core, y)


def position():
    me, pair = lax.axis_index("vec"), lax.axis_index("pair")
    return (me // NC) % NL, me // (NL * NC), me % NC, pair // NY, pair % NY


def diagonal_mask(rows, columns):
    row = lax.broadcasted_iota(jnp.int32, (rows, columns), 0)
    column = lax.broadcasted_iota(jnp.int32, (rows, columns), 1)
    return (row % GROUP) == (column // GROUP)


def groups_of(rows):
    return [(start, min(GROUP, rows - start)) for start in range(0, rows, GROUP)]


def rotate_kernel(walkers, inverse, out_ref):
    rows = walkers.shape[1]
    mine = walkers[...].astype(jnp.float32).T
    out_ref[...] = jnp.zeros_like(out_ref)
    out_ref[:rows, :] = jnp.dot(
        mine, inverse[...], precision=lax.Precision.HIGHEST, preferred_element_type=jnp.float32
    ).astype(jnp.bfloat16)


def order_kernel(rotated, partner, trial, out_ref, trial_out):
    at = position()
    trial_out[...] = trial[...]
    out_ref[at[0]] = rotated[...]
    out_ref[1 - at[0]] = partner[...]


def sum_kernel(mine, arrived, out_ref):
    out_ref[...] = mine[...] + arrived[...]


def write_fields(at, shifted, swapped, out_ref):
    vectors = out_ref.shape[1]
    for step in range(NX):
        for low in range(NL):
            chip = ((at[1] + step) % NX) * NL + low
            row = step * NL + low
            out_ref[pl.ds(chip * NC + at[2], 1), :] = shifted[row : row + 1, :vectors]
            out_ref[pl.ds(chip * NC + 1 - at[2], 1), :] = swapped[row : row + 1, :]


def factor_kernel(trial, block, a1, a2, a3, out_ref):
    count, vectors, depth = block.shape
    product = lax.dot_general(
        block[...].reshape(count * vectors, depth), trial[...], NT, preferred_element_type=jnp.float32
    ).astype(jnp.bfloat16)
    out_ref[...] = product.reshape(count, vectors, trial.shape[0])


def bias_kernel(r0, r1, r2, r3, own, other, aux, passed, out_ref, aux_out, passed_out):
    aux_out[...] = aux[...]
    rows, vectors, depth = own.shape
    parts = []
    for factor in (own, other):
        total = jnp.zeros((8 * GROUP, GROUP * vectors), jnp.float32)
        tail = None
        for start, count in groups_of(rows):
            left = jnp.concatenate(
                [r[low, start : start + GROUP, :] for r in (r0, r1, r2, r3) for low in range(NL)], axis=0
            )
            right = factor[start : start + count].reshape(count * vectors, depth)
            product = lax.dot_general(left, right, NT, preferred_element_type=jnp.float32)
            if count == GROUP:
                total = total + product
            else:
                tail = product
        pieces = [total] if tail is None else [total, tail]
        summed = jnp.zeros((8, vectors), jnp.float32)
        for piece in pieces:
            width = piece.shape[1]
            kept = jnp.where(diagonal_mask(8 * GROUP, width), piece, 0.0)
            kept = jnp.sum(kept.reshape(8, GROUP, width), axis=1)
            pick = lax.broadcasted_iota(jnp.int32, (width, vectors), 0) % vectors == lax.broadcasted_iota(
                jnp.int32, (width, vectors), 1
            )
            summed = summed + jnp.dot(
                kept, pick.astype(jnp.float32), precision=lax.Precision.HIGHEST, preferred_element_type=jnp.float32
            )
        parts.append(summed)
    out_ref[...] = jnp.concatenate(parts, axis=1)


def fields_of(bias_refs, at, aux, aux_other, gathered):
    b0, b1, b2, b3 = bias_refs
    bias = (b0[...] + b2[...]) + (b1[...] + b3[...])
    vectors = aux.shape[1]
    for step in range(NX):
        for low in range(NL):
            walker = (((at[1] + step) % NX) * NL + low) * NC + at[2]
            row = step * NL + low
            gathered[row : row + 1, :vectors] = aux[pl.ds(walker, 1), :]
            gathered[row : row + 1, vectors:] = aux_other[pl.ds(walker, 1), :]
    return gathered[...] - jnp.clip(-root_step * bias, -shift_cap, shift_cap)


def block_diagonals(coefficients, vectors):
    tall, wide = 8 * GROUP, GROUP * vectors
    spread = (
        lax.broadcasted_iota(jnp.int32, (tall, 8), 0) // GROUP == lax.broadcasted_iota(jnp.int32, (tall, 8), 1)
    ).astype(jnp.bfloat16)
    repeat = (
        lax.broadcasted_iota(jnp.int32, (vectors, wide), 1) % vectors
        == lax.broadcasted_iota(jnp.int32, (vectors, wide), 0)
    ).astype(jnp.bfloat16)
    mask = diagonal_mask(tall, wide)
    blocks = []
    for at in range(2):
        piece = coefficients[:, at * vectors : (at + 1) * vectors]
        piece = jnp.dot(spread, piece, preferred_element_type=jnp.float32).astype(jnp.bfloat16)
        piece = jnp.dot(piece, repeat, preferred_element_type=jnp.float32)
        blocks.append(jnp.where(mask, piece, 0.0).astype(jnp.bfloat16))
    return blocks


def walker_sums(blocks, own, other, base, half, store):
    vectors, columns = own.shape[1:]
    for start, count in groups_of(half):
        depth = count * vectors
        for left in range(0, columns, 512):
            right = min(columns, left + 512)
            total = jnp.dot(
                blocks[0][:, :depth],
                own[pl.ds(base + start, count), :, left:right].reshape(depth, right - left),
                preferred_element_type=jnp.float32,
            ) + jnp.dot(
                blocks[1][:, :depth],
                other[pl.ds(base + start, count), :, left:right].reshape(depth, right - left),
                preferred_element_type=jnp.float32,
            )
            total = total.astype(jnp.bfloat16)
            for walker in ALL:
                store(walker, start, count, left, right, total[walker * GROUP : walker * GROUP + count, :])


ALL = list(range(NX * NL))


def operator_kernel(
    b0, b1, b2, b3, aux, aux_other, walkers, own, other,
    fields_ref, swap_ref, e0, e1, e2, e3, away_ref, o0, o1, o2, o3, walkers_out, gathered,
):
    at = position()
    walkers_out[...] = walkers[...].astype(jnp.float32).T.astype(walkers_out.dtype)
    half = o0.shape[0]
    fields = fields_of((b0, b1, b2, b3), at, aux, aux_other, gathered)
    fields_ref[...] = fields
    swap_ref[...] = fields[:, own.shape[1] :]
    blocks = block_diagonals((root_step * fields).astype(jnp.bfloat16), own.shape[1])
    evens, odds = (e0, e1, e2, e3), (o0, o1, o2, o3)

    def store_away(walker, start, count, left, right, value):
        if walker % NL:
            row = walker // NL * PITCH + start
            away_ref[row : row + count, left:right] = value
        else:
            evens[walker // NL][half + start : half + start + count, left:right] = value

    def store_keep(walker, start, count, left, right, value):
        out = odds if walker % NL else evens
        out[walker // NL][start : start + count, left:right] = value

    walker_sums(blocks, own, other, (1 - at[0]) * half, half, store_away)
    walker_sums(blocks, own, other, at[0] * half, half, store_keep)


def wide(value):
    return value.astype(jnp.float32)


def pair_sum_kernel(k0, k1, k2, k3, arrived, shifted, swapped, walkers, partners, o0, o1, o2, o3, fields_ref, stacked):
    stack(stacked, walkers, partners)
    write_fields(position(), shifted, swapped, fields_ref)
    half = o0.shape[0]
    for step, (keep, out) in enumerate(((k0, o0), (k1, o1), (k2, o2), (k3, o3))):
        out[...] = (wide(keep[...]) + wide(arrived[step * PITCH : step * PITCH + half, :])).astype(out.dtype)


def stack(out, low, high):
    rows = low.shape[0]
    out[:rows, :] = low[...]
    out[rows:, :] = high[...]


def x_sum_kernel(p0, p1, p2, p3, out):
    half = out.shape[0]
    out[...] = (
        (wide(p0[half:, :]) + wide(p1[half:, :])) + (wide(p2[half:, :]) + wide(p3[half:, :]))
    ).astype(out.dtype)


def last_sum_kernel(p0, p1, p2, p3, arrived, q0, q1, q2, q3, walkers, partners, first, second, stacked):
    stack(stacked, walkers, partners)
    half = first.shape[0]
    even = (
        (wide(p0[:half, :]) + wide(p1[:half, :])) + (wide(p2[:half, :]) + wide(p3[:half, :]))
    ) + wide(arrived[...])
    odd = (wide(q0[...]) + wide(q1[...])) + (wide(q2[...]) + wide(q3[...]))
    at = position()
    turn = (at[3] - at[2] + NH) % NH
    pick = jnp.logical_or(turn == 1, turn == 2)
    first[...] = jnp.where(pick, even, odd).astype(first.dtype)
    second[...] = jnp.where(pick, odd, even).astype(second.dtype)


def choose_kernel(second, got, more, after, block0, block1, blocks):
    at = position()
    active = (at[2] + at[3]) % 2 == 0

    @pl.when(active)
    def _():
        block0[...] = second[...]
        block1[...] = got[...]
        stack(blocks, second, got)

    @pl.when(jnp.logical_not(active))
    def _():
        block0[...] = got[...]
        block1[...] = more[...]
        stack(blocks, got, more)


def stack_low_kernel(block, partners, out):
    stack(out, block[...], partners[: block.shape[0], :])


def stack_y_kernel(b1, b2, b3, near, far, three, stacked):
    stack(stacked, near, far)
    half = b1.shape[0]
    for step, ref in enumerate((b1, b2, b3)):
        three[step * half : (step + 1) * half, :] = ref[...]


def own_base():
    _, _, core, high, _ = position()
    return (high + ((high + core) & 1)) % NH


def compact(held, out, last):
    half = held.shape[1]
    y = position()[4]
    for block in range(held.shape[0]):
        out[block * half : (block + 1) * half, :] = held[block]
    for part in range(NL):
        last[part * half : (part + 1) * half, :] = held[y * NL + part]


def first_rows_kernel(p0, p1, p2, p3, walkers, out, last, walkers_out, held):
    low, _, _, _, y = position()
    walkers_out[...] = walkers[...]
    half = held.shape[1]
    for step, ref in enumerate((p0, p1, p2, p3)):
        row = ((y - step + NY) % NY) * NL
        held[row + low] = ref[:half, :]
        held[row + 1 - low] = ref[half:, :]
    compact(held, out, last)


def second_rows_kernel(block, three, low_blocks, low_three, walkers, swapped, out, last, start, held, total):
    low, _, core, _, y = position()
    half = held.shape[1]
    for step in range(NY):
        row = ((y - step + NY) % NY) * NL
        if step == 0:
            held[row + low] = block[...]
            held[row + 1 - low] = low_blocks[half:, :]
        else:
            place = slice((step - 1) * half, step * half)
            held[row + low] = three[place, :]
            held[row + 1 - low] = low_three[place, :]
    compact(held, out, last)
    rows = 2 * half
    for step, ref in enumerate((walkers, swapped)):
        for index in range(NY * NL):
            total[step, index] = ref[index * rows : (index + 1) * rows, :]
    for at in range(NH * NY):
        row, column = at // NY, at % NY
        piece = total[(row % NC) ^ core, (y ^ column) * NL + ((row // NC) ^ low)]
        start[at * rows : (at + 1) * rows, :] = piece


def taylor_kernel(rows0, rows1, other0, other1, last0, last1, start, walkers, out_ref, operator, terms, total):
    low, _, core, high, y = position()
    base = own_base()
    other = (high + ((high + core + 1) & 1)) % NH
    stretch, rows = rows0.shape[0], last0.shape[0]
    for place, ref in ((base, rows0), ((base + 2) % NH, rows1), (other, other0), ((other + 2) % NH, other1)):
        operator[pl.ds(pl.multiple_of(place * stretch, 16), stretch), :] = ref[...]
    block_here = (low * NC + core) * NY + y
    terms[0] = start[...]
    total[...] = wide(walkers[:rows, :])

    @pl.loop(1, TAYLOR)
    def _(degree):
        source = (degree - 1) % 2
        product = jnp.dot(operator[...], terms[source], preferred_element_type=jnp.float32)
        terms[1 - source] = (product / degree.astype(jnp.float32)).astype(jnp.bfloat16)
        for block in range(NH * NY):

            @pl.when(block_here == block)
            def _():
                total[...] += wide(terms[1 - source, block * rows : (block + 1) * rows, :])

    last = jnp.where(base == low * NC + core, last0[...], last1[...])
    product = jnp.dot(last, terms[(TAYLOR - 1) % 2], preferred_element_type=jnp.float32)
    out_ref[...] = (total[...] + wide((product / TAYLOR).astype(jnp.bfloat16))).T.astype(out_ref.dtype)


def call(kernel, outs, args, name, scratch=(), idle=0, limit=16, flops=None):
    specs = [VMEM] * (len(args) - idle) + [FAR] * idle
    return pl.pallas_call(
        kernel,
        out_shape=outs,
        in_specs=specs,
        out_specs=[VMEM] * len(outs) if isinstance(outs, (list, tuple)) else VMEM,
        scratch_shapes=list(scratch),
        compiler_params=pltpu.CompilerParams(vmem_limit_bytes=limit * 2**20),
        cost_estimate=None if flops is None else pl.CostEstimate(flops=flops, bytes_accessed=0, transcendentals=0),
        name=name,
    )(*args)


def on_device(cholesky, walkers, inv_correlation, trial_orbitals, aux_fields):
    vectors, rows, orbitals = cholesky.shape
    occupied = walkers.shape[2]
    half = rows // NL
    bf16, f32 = jnp.bfloat16, jnp.float32
    shaped = jax.ShapeDtypeStruct
    own = jnp.transpose(cholesky, (1, 0, 2))
    other = swap_core(own)
    rows_here = exchange(walkers[0].T)
    rotated = call(
        rotate_kernel,
        shaped((rows + -rows % GROUP, occupied), bf16),
        (walkers[0].T, inv_correlation[0]),
        "rotate",
    )
    partner = swap_low(rotated)
    both, trial = call(
        order_kernel,
        [shaped((NL,) + rotated.shape, bf16), shaped((occupied, orbitals), bf16)],
        (rotated, partner, trial_orbitals.T),
        "order",
    )
    met = [both] + [send_x(both, -step) for step in range(1, NX)]
    factor = call(
        factor_kernel,
        shaped((rows, vectors, occupied), bf16),
        (trial, other, *met[1:]),
        "vector_factor",
        idle=3,
    )
    bias, aux_here, other = pl.pallas_call(
        bias_kernel,
        out_shape=[shaped((8, 2 * vectors), f32), shaped(aux_fields.shape, f32), shaped(other.shape, bf16)],
        in_specs=[VMEM] * 7 + [FAR],
        out_specs=[VMEM] * 2 + [FAR],
        input_output_aliases={7: 2},
        compiler_params=pltpu.CompilerParams(vmem_limit_bytes=16 * 2**20),
        name="force_bias",
    )(*met, swap_core(factor), factor, aux_fields, other)
    near = swap_core(other)
    aux_other = swap_core(aux_here)
    for bit in (1, 2):
        bias = call(sum_kernel, shaped(bias.shape, f32), (bias, flip_y(bias, bit)), "sum_y")
    from_h = [bias] + [send_h(bias, step) for step in range(1, NH)]

    piece, two, quad = [shaped((n * half, orbitals), bf16) for n in (1, 2, 4)]
    shifted, shifted_other, *parts, rows_here = call(
        operator_kernel,
        [shaped((8, 2 * vectors), f32), shaped((8, vectors), f32)]
        + [two] * NX
        + [shaped((NX * PITCH, orbitals), bf16)]
        + [piece] * NX
        + [shaped((rows, occupied), bf16)],
        (*from_h, aux_fields, aux_other, rows_here, near, other),
        "field_operator",
        scratch=[pltpu.VMEM((8, 2 * vectors), f32)],
    )
    even, away, odd = parts[:NX], parts[NX], parts[NX + 1 :]
    shifted_other = swap_core(shifted_other)
    away = swap_low(away)
    even = [even[0]] + [send_x(even[step], step) for step in range(1, NX)]
    low_rows = swap_low(rows_here)
    arrived = swap_low(call(x_sum_kernel, piece, tuple(even), "x_sum"))
    *odd, fields, two_rows = call(
        pair_sum_kernel,
        [piece] * NX + [shaped(aux_fields.shape, f32), shaped((NL * rows, occupied), bf16)],
        (*odd, away, shifted, shifted_other, rows_here, low_rows),
        "pair_sum",
    )
    odd = [odd[0]] + [send_x(odd[step], step) for step in range(1, NX)]
    first, second, four_rows = call(
        last_sum_kernel,
        [piece] * 2 + [shaped((2 * NL * rows, occupied), bf16)],
        (*even, arrived, *odd, two_rows, flip_y(two_rows, 1)),
        "last_sum",
    )
    far_rows = flip_y(four_rows, 2)

    got = everywhere(first, first_target)
    more = everywhere(second, second_target)
    block0, block1, blocks = call(
        choose_kernel, [piece] * 2 + [two], (second, got, more, far_rows), "choose", idle=1
    )
    low_blocks = swap_low(blocks)
    pair0 = call(stack_low_kernel, two, (block0, low_blocks), "stack_low")
    three, eight_rows = call(
        stack_y_kernel,
        [shaped((3 * half, orbitals), bf16), shaped((4 * NL * rows, occupied), bf16)],
        (*[send_y(block1, step) for step in range(1, NY)], four_rows, far_rows),
        "stack_y",
    )
    stretch = shaped((NY * rows, orbitals), bf16)
    held = pltpu.VMEM((NY * NL, half, orbitals), bf16)
    rows0, last0, eight_rows = call(
        first_rows_kernel,
        [stretch, two, shaped(eight_rows.shape, bf16)],
        (pair0, *[send_y(pair0, step) for step in range(1, NY)], eight_rows),
        "first_rows",
        scratch=[held],
        flops=None,
    )
    rows1, last1, start = call(
        second_rows_kernel,
        [stretch, two, shaped((orbitals, occupied), bf16)],
        (block1, three, low_blocks, swap_low(three), eight_rows, swap_core(eight_rows)),
        "second_rows",
        scratch=[held, pltpu.VMEM((NC, NY * NL, rows, occupied), bf16)],
    )
    updated = call(
        taylor_kernel,
        shaped((occupied, rows), bf16),
        (rows0, rows1, swap_core(rows0), swap_core(rows1), last0, last1, start, eight_rows),
        "taylor",
        scratch=[
            pltpu.VMEM((orbitals, orbitals), bf16),
            pltpu.VMEM((2, orbitals, occupied), bf16),
            pltpu.VMEM((rows, occupied), f32),
        ],
        limit=24,
    )
    return (exchange(updated).T[None], fields)


def solution(mesh):
    placed = (
        P("vec", "pair", None),
        P("vec", "pair", None),
        P("vec", None, None),
        P(),
        P(None, "vec"),
    )
    return jax.shard_map(
        on_device,
        mesh=mesh,
        in_specs=placed,
        out_specs=(P("vec", "pair", None), P(None, "vec")),
        check_vma=False,
    )
```
